256 devices in a mesh: clip: 4 (over y), frame: 8 (over x, core), tensor: 8 (over z).
Axes of the slice: x: 4, y: 4, z: 8, core: 2. Of those that a mesh axis runs over, the one named last changes fastest.
Arguments:
- spatial_qkv: bfloat16 [4, 16, 128, 3, 3072], P('clip', 'frame', None, None, 'tensor'), may hold values from -16 to 16
- w_qkv: bfloat16 [3072, 24, 3, 128], P(('clip', 'frame'), 'tensor'), may hold values from -0.109375 to 0.109375
- w_out: bfloat16 [24, 128, 3072], P('tensor', None, ('clip', 'frame')), may hold values from -0.109375 to 0.109375
- out_grad: bfloat16 [4, 16, 128, 3072], P('clip', 'frame', None, 'tensor'), may hold values from -6 to 6
- frame_clip: int32 [4, 16], P('clip'), may hold values from 0 to 7, never falling along the last dimension, each value on 1 to 4 neighbouring positions
- clip_patches: int32 [4, 8], P('clip'), may hold values from 32 to 128, as said below
Outputs:
- block_out: bfloat16 [4, 16, 128, 3072], P('clip', 'frame', None, 'tensor')
- qkv_grad: bfloat16 [4, 16, 128, 3, 3072], P('clip', 'frame', None, None, 'tensor')
- w_qkv_grad: float32 [3072, 24, 3, 128], P(('clip', 'frame'), 'tensor')
- w_out_grad: float32 [24, 128, 3072], P('tensor', None, ('clip', 'frame'))
The draws below stay inside these ranges and needn't reach their ends.
Inputs may be any that keep to these rules, and one draw needn't show every extreme that they name: `frame_clip`: within a group, the frames of one clip stand together, clip numbers never fall, every one of the 8 clips has 1 to 4 frames and one has exactly 4. `clip_patches`: at least 32; 128 for one clip of every group.
All inputs are finite; a program needn't handle non-finite values.
Results may differ from the reference program's by a relative error of at most 0.022.
Values may be sent and summed in bfloat16 or wider, within the bound.
No kernel may reach another device: no remote copies, remote signals or barrier semaphores. Data moves between devices by JAX's collectives and lax.ppermute only.
A program may use at most 128 MiB of HBM per device.

```python
import math
import jax
import jax.numpy as jnp
import numpy as np
from jax import lax

H = 24
HD = 128
D = 3072
P_SIZE = 128
F_TOT = 16
CLIPS = 8
GROUPS = 4
MOST_FRAMES = 4
N_FRAME = 8


def draw_spatial_qkv(key, part):
    key = jax.random.fold_in(key, 11)
    shape = (GROUPS, F_TOT, P_SIZE, 3, H * HD)
    third = jax.random.fold_in(key, 2)
    whole = jax.random.truncated_normal(third, -6.0, 6.0, shape, jnp.float32)
    return whole.astype(jnp.bfloat16)


def draw_clip_patches(key, part):
    key = jax.random.fold_in(key, 23)
    first, second = jax.random.split(key)
    counts = jax.random.randint(first, (GROUPS, CLIPS), P_SIZE // 4, P_SIZE + 1)
    chosen = jax.random.randint(second, (GROUPS, 1), 0, CLIPS)
    full = jnp.arange(CLIPS, dtype=jnp.int32)[None, :] == chosen
    return jnp.where(full, P_SIZE, counts).astype(jnp.int32)


def level_of(own_key, dims, cuts, low, high):
    def one(dim, blocks):
        draws = jax.random.uniform(jax.random.fold_in(jax.random.fold_in(own_key, 6), dim), (blocks,), jnp.float32, low / len(cuts), high / len(cuts))
        return jnp.repeat(jnp.exp(draws), dims[dim] // blocks).reshape((-1,) + (1,) * (len(dims) - dim - 1))

    factor_of = one(*cuts[0])
    for cut in cuts[1:]:
        factor_of = factor_of * one(*cut)
    return factor_of


def length_profile(count, total, most, lean):
    weights = [(1 << 20) // math.isqrt(rank ** lean) + 1 for rank in range(2, count + 1)]
    spare, given = total - most - (count - 1), [1] * (count - 1)
    while spare > 0:
        movable = [i for i in range(count - 1) if given[i] < most]
        whole, remaining = sum([weights[i] for i in movable]), spare
        for i in movable:
            addition = min(most - given[i], max(1, remaining * weights[i] // whole), spare)
            given[i] = given[i] + addition
            spare = spare - addition
    return np.array([most] + given)


def uneven_parts(own_key, count, total, bound, skew):
    if count == 2:
        one = jax.random.randint(own_key, (), max(1, total - bound), min(bound, total - 1) + 1)
        return jnp.stack([one, total - one])
    tallies = jnp.asarray(length_profile(count, total, bound, skew), jnp.int32)
    couples = (count - 1) // 2
    donor, sink = tallies[1:1 + 2 * couples:2], tallies[2:2 + 2 * couples:2]
    margin = jnp.minimum(donor - 1, bound - sink)
    passed = jax.random.randint(jax.random.fold_in(own_key, 1), (couples,), 0, 1 << 20) % (margin + 1)
    tallies = tallies.at[1:1 + 2 * couples:2].set(donor - passed).at[2:2 + 2 * couples:2].set(sink + passed)
    return tallies[jax.random.permutation(jax.random.fold_in(own_key, 2), count)]


def gaussian(stream_key, shape, deviation, most, pieces=(), kind=jnp.bfloat16):
    result = deviation * jax.random.normal(stream_key, shape, jnp.float32)
    if pieces:
        result = result * level_of(stream_key, shape, pieces, -0.22, 0.18)
    return jnp.clip(result, -most, most).astype(kind)


def setup_inputs(seed: int = 0) -> dict:
    arg_keys = jax.random.split(jax.random.key(seed), 7)
    return {
        "spatial_qkv": draw_spatial_qkv(jax.random.fold_in(arg_keys[6], 71), 0),
        "w_qkv": gaussian(arg_keys[1], (D, H, 3, HD), D ** -0.5, 0.109375, ((0, 32), (1, 8))),
        "w_out": gaussian(arg_keys[2], (H, HD, D), D ** -0.5, 0.109375, ((0, 8), (2, 32))),
        "out_grad": gaussian(arg_keys[3], (GROUPS, F_TOT, P_SIZE, D), 1.0, 6.0, ((0, 4), (1, 8), (3, 8))),
        "frame_clip": jax.vmap(lambda own: jnp.searchsorted(jnp.cumsum(uneven_parts(own, CLIPS, F_TOT, MOST_FRAMES, 1)), jnp.arange(F_TOT), side="right"))(jax.random.split(arg_keys[4], GROUPS)).reshape((GROUPS, F_TOT)).astype(jnp.int32),
        "clip_patches": draw_clip_patches(jax.random.fold_in(arg_keys[6], 71), 0),
    }


def settle(values):
    return lax.optimization_barrier(values.astype(jnp.bfloat16)).astype(jnp.float32)

def spatial_core(query, keys, values, valid):
    scale = 1.0 / math.sqrt(query.shape[-1])
    scores = jnp.einsum('fphd,fqhd->fhpq', query, keys) * scale
    scores = jnp.where(valid[:, None, None, :], scores, -1e+30)
    top = lax.optimization_barrier(jnp.max(scores, axis=-1, keepdims=True))
    expo = jnp.exp(scores - top)
    probs = (expo / lax.optimization_barrier(jnp.sum(expo, axis=-1, keepdims=True))).astype(jnp.bfloat16)
    mixed = jnp.einsum('fhpq,fqhd->fphd', probs, values.astype(jnp.bfloat16), preferred_element_type=jnp.float32)
    return mixed * valid[:, :, None, None].astype(jnp.float32)

def temporal_core(query, keys, values, same):
    scale = 1.0 / math.sqrt(query.shape[-1])
    scores = jnp.einsum('fphd,gphd->phfg', query, keys) * scale
    scores = jnp.where(same[None, None, :, :], scores, -1e+30)
    top = lax.optimization_barrier(jnp.max(scores, axis=-1, keepdims=True))
    expo = jnp.exp(scores - top)
    probs = (expo / lax.optimization_barrier(jnp.sum(expo, axis=-1, keepdims=True))).astype(jnp.bfloat16)
    return jnp.einsum('phfg,gphd->fphd', probs, values.astype(jnp.bfloat16), preferred_element_type=jnp.float32)

def reference(spatial_qkv, w_qkv, w_out, out_grad, frame_clip, clip_patches):
    patch_block = P_SIZE // N_FRAME
    qkv_flat = w_qkv.reshape(D, H * 3 * HD)
    out_flat = w_out.reshape(D, D)
    contract_last = (((1,), (1,)), ((), ()))
    contract_first = (((0,), (0,)), ((), ()))
    qkv_total = jnp.zeros((D, H * 3 * HD), jnp.float32)
    out_total = jnp.zeros((D, D), jnp.float32)
    outputs = []
    grads = []
    for group in range(GROUPS):
        clip_row = frame_clip[group]
        counts = clip_patches[group]
        frame_count = jnp.take(counts, clip_row)
        valid = jnp.arange(P_SIZE, dtype=jnp.int32)[None, :] < frame_count[:, None]
        same = clip_row[:, None] == clip_row[None, :]
        inputs = spatial_qkv[group].astype(jnp.float32)
        shape_s = (F_TOT, P_SIZE, H, HD)
        mixed, spatial_back = jax.vjp(lambda a, b, c: spatial_core(a, b, c, valid), inputs[:, :, 0].reshape(shape_s), inputs[:, :, 1].reshape(shape_s), inputs[:, :, 2].reshape(shape_s))
        spatial = mixed.reshape(F_TOT, P_SIZE, D).astype(jnp.bfloat16)
        qkv_t = jnp.dot(spatial.reshape(-1, D), qkv_flat, preferred_element_type=jnp.float32)
        qkv_t = settle(qkv_t).reshape(F_TOT, P_SIZE, H, 3, HD)
        mixed_t, temporal_back = jax.vjp(lambda a, b, c: temporal_core(a, b, c, same), qkv_t[:, :, :, 0], qkv_t[:, :, :, 1], qkv_t[:, :, :, 2])
        temporal = mixed_t.reshape(F_TOT, P_SIZE, D).astype(jnp.bfloat16)
        projected = jnp.dot(temporal.reshape(-1, D), out_flat, preferred_element_type=jnp.float32).reshape(F_TOT, P_SIZE, D)
        mask = valid[:, :, None]
        outputs.append(((spatial.astype(jnp.float32) + projected) * mask.astype(jnp.float32)).astype(jnp.bfloat16))
        gated = jnp.where(mask, out_grad[group], jnp.zeros((), jnp.bfloat16))
        d_temporal = lax.dot_general(gated.reshape(-1, D), out_flat, contract_last, preferred_element_type=jnp.float32)
        d_temporal = settle(d_temporal).reshape(F_TOT, P_SIZE, H, HD)
        grads_t = temporal_back(d_temporal)
        d_qkv = jnp.stack(grads_t, axis=3).astype(jnp.bfloat16)
        back = lax.dot_general(d_qkv.reshape(-1, H * 3 * HD), qkv_flat, contract_last, preferred_element_type=jnp.float32)
        back = settle(back).reshape(F_TOT, P_SIZE, D)
        d_spatial = gated.astype(jnp.float32) + back
        grads_s = spatial_back(d_spatial.reshape(shape_s))
        grads.append(jnp.stack(grads_s, axis=2).reshape(F_TOT, P_SIZE, 3, D).astype(jnp.bfloat16))
        for block in range(N_FRAME):
            low = block * patch_block
            high = low + patch_block
            spatial_rows = spatial[:, low:high].reshape(-1, D)
            gated_rows = gated[:, low:high].reshape(-1, D)
            temporal_rows = temporal[:, low:high].reshape(-1, D)
            d_rows = d_qkv[:, low:high].reshape(-1, H * 3 * HD)
            qkv_total = qkv_total + settle(lax.dot_general(spatial_rows, d_rows, contract_first, preferred_element_type=jnp.float32))
            out_total = out_total + settle(lax.dot_general(temporal_rows, gated_rows, contract_first, preferred_element_type=jnp.float32))
    return (jnp.stack(outputs), jnp.stack(grads), qkv_total.reshape(D, H, 3, HD), out_total.reshape(H, HD, D))
```

```python
import math

import jax
import jax.numpy as jnp
from jax import lax
from jax.experimental import pallas as pl
from jax.experimental.pallas import tpu as pltpu
from jax.sharding import PartitionSpec as P

HD = 128
SCALE = 1.0 / math.sqrt(HD)
BF = jnp.bfloat16
F32 = jnp.float32
NT = (((1,), (1,)), ((), ()))
TN = (((0,), (0,)), ((), ()))


def dot(a, b, dims=(((1,), (0,)), ((), ()))):
    return lax.dot_general(a, b, dims, preferred_element_type=F32)


def softmax(query, keys, mask):
    scores = jnp.where(mask, dot(query, keys, NT) * SCALE, -1e30)
    expo = jnp.exp(scores - jnp.max(scores, axis=-1, keepdims=True))
    return expo / jnp.sum(expo, axis=-1, keepdims=True)


def attention_grads(query, keys, values, probs, cotangent):
    d_values = dot(probs.astype(BF), cotangent, TN).astype(BF)
    d_probs = dot(cotangent, values, NT).astype(BF).astype(F32)
    inner = jnp.sum(probs * d_probs, axis=-1, keepdims=True)
    d_scores = (probs * (d_probs - inner) * SCALE).astype(BF)
    return dot(d_scores, keys).astype(BF), dot(d_scores, query, TN).astype(BF), d_values


def spatial_forward(count_ref, qkv_ref, cot_ref, out_ref):
    frames, _, patches, width = qkv_ref.shape
    owners = out_ref.shape[0]
    block = patches // owners
    for f in range(frames):
        count = count_ref[f]
        keys_live = lax.broadcasted_iota(jnp.int32, (patches, patches), 1) < count
        rows_live = lax.broadcasted_iota(jnp.int32, (patches, 1), 0) < count
        pieces = []
        for h in range(width // HD):
            cols = slice(h * HD, (h + 1) * HD)
            probs = softmax(qkv_ref[f, 0, :, cols], qkv_ref[f, 1, :, cols], keys_live)
            mixed = dot(probs.astype(BF), qkv_ref[f, 2, :, cols])
            pieces.append(jnp.where(rows_live, mixed, 0.0).astype(BF))
        whole = jnp.concatenate(pieces, axis=1)
        gated = jnp.where(rows_live, cot_ref[f].astype(F32), 0.0).astype(BF)
        for s in range(owners):
            out_ref[s, 0, f] = whole[s * block : (s + 1) * block]
            out_ref[s, 1, f] = gated[s * block : (s + 1) * block]


def spatial_backward(count_ref, qkv_ref, cot_ref, sums_ref, out_ref, grad_ref):
    frames, _, patches, width = qkv_ref.shape
    owners = sums_ref.shape[0]
    for f in range(frames):
        count = count_ref[f]
        keys_live = lax.broadcasted_iota(jnp.int32, (patches, patches), 1) < count
        rows_live = lax.broadcasted_iota(jnp.int32, (patches, 1), 0) < count
        projected = jnp.concatenate([sums_ref[s, 0, f] for s in range(owners)], axis=0)
        back = jnp.concatenate([sums_ref[s, 1, f] for s in range(owners)], axis=0)
        d_spatial = cot_ref[f].astype(F32) + back.astype(F32)
        d_mixed = jnp.where(rows_live, d_spatial, 0.0).astype(BF)
        for h in range(width // HD):
            cols = slice(h * HD, (h + 1) * HD)
            query, keys, values = (qkv_ref[f, i, :, cols] for i in range(3))
            probs = softmax(query, keys, keys_live)
            mixed = dot(probs.astype(BF), values).astype(BF).astype(F32)
            total = mixed + projected[:, cols].astype(F32)
            out_ref[f, :, cols] = jnp.where(rows_live, total, 0.0).astype(BF)
            grads = attention_grads(query, keys, values, probs, d_mixed[:, cols])
            for i in range(3):
                grad_ref[f, i, :, cols] = grads[i]


def temporal_kernel(heads, ranks, place_ref, row_key_ref, col_key_ref, *refs):
    blocks, refs = refs[: 2 * ranks], refs[2 * ranks :]
    w_hbm, sums_ref, d_qkv_ref, mixed_ref, feat_ref, gated_ref, w_ref, w_sem, in_sem = refs
    width = heads * HD
    me = place_ref[0]
    slots = w_ref.shape[0]
    loads = [pltpu.make_async_copy(w_hbm.at[i], w_ref.at[i], w_sem.at[i]) for i in range(slots)]
    arrivals = []
    for a, whole in enumerate((feat_ref, gated_ref)):
        for d in range(ranks):
            start = pl.multiple_of(lax.rem(me + d, ranks) * width, HD)
            i = a * ranks + d
            arrivals.append(
                pltpu.make_async_copy(blocks[i], whole.at[:, pl.ds(start, width)], in_sem.at[i])
            )
    for copy in arrivals:
        copy.start()
    for h in range(heads):
        for i in (3 * h, 3 * h + 1, 3 * h + 2, 3 * heads + h):
            loads[i].start()
    for copy in arrivals:
        copy.wait()
    mask = row_key_ref[...] == col_key_ref[...]
    for h in range(heads):
        for i in (3 * h, 3 * h + 1, 3 * h + 2, 3 * heads + h):
            loads[i].wait()
        w_head = jnp.concatenate([w_ref[3 * h + i] for i in range(3)], axis=1)
        qkv = dot(feat_ref[...], w_head).astype(BF)
        cotangent = dot(gated_ref[...], w_ref[3 * heads + h]).astype(BF)
        query, keys, values = (qkv[:, i * HD : (i + 1) * HD] for i in range(3))
        probs = softmax(query, keys, mask)
        mixed_ref[:, h * HD : (h + 1) * HD] = dot(probs.astype(BF), values).astype(BF)
        grads = attention_grads(query, keys, values, probs, cotangent)
        for i in range(3):
            start = (3 * h + i) * HD
            d_qkv_ref[:, start : start + HD] = grads[i]
    owners = sums_ref.shape[1]
    rows = sums_ref.shape[3]
    for z in range(ranks):
        part = slice(z * width, (z + 1) * width)
        w_back = jnp.concatenate([w_ref[i, part] for i in range(3 * heads)], axis=1)
        w_proj = jnp.concatenate([w_ref[3 * heads + i, part] for i in range(heads)], axis=1)
        projected = dot(mixed_ref[...], w_proj, NT).astype(BF)
        back = dot(d_qkv_ref[...], w_back, NT).astype(BF)
        for s in range(owners):
            sums_ref[z, s, 0] = projected[s * rows : (s + 1) * rows]
            sums_ref[z, s, 1] = back[s * rows : (s + 1) * rows]


def weight_grad_kernel(place_ref, *refs):
    pairs, (mine_ref, other_ref) = refs[:-2], refs[-2:]
    lead_x = place_ref[3] == 1
    at_x, core = place_ref[1], place_ref[2]
    n_x = 4
    rows = mine_ref.shape[3]
    total = jnp.concatenate(
        [dot(pairs[i][...], pairs[i + 1][...], TN) for i in range(0, len(pairs), 2)], axis=1
    ).astype(BF)
    slots = mine_ref.shape[2]
    del lead_x
    for k in range(2):
        for x in range(n_x):
            at = lax.rem(x + n_x - at_x, n_x)
            start = (2 * x + k) * rows
            block = total[start : start + rows]

            def write(ref, at=at, block=block):
                for s in range(slots):
                    part = block[:, s * HD : (s + 1) * HD]
                    if mine_ref.shape[0] == 1:
                        ref[0, at, s] = part
                    else:
                        ref[at, 0, s] = part

            pl.when(core == k)(lambda write=write: write(mine_ref))
            pl.when(core != k)(lambda write=write: write(other_ref))


def weight_grads(place, pairs, slots, x_first):
    n_c, n_x = 4, 4
    model = pairs[0][0].shape[1]
    per = model // n_c
    rows = per // (2 * n_x)
    specs, args = [], []
    for left, right in pairs:
        specs.append(pl.BlockSpec((left.shape[0], per), lambda i, p: (0, lax.rem(i + p[0], n_c))))
        specs.append(pl.BlockSpec(right.shape, lambda i, p: (0, 0)))
        args += [left, right]
    if x_first:
        shape, spec = (n_x, n_c, slots, rows, HD), pl.BlockSpec(
            (n_x, 1, slots, rows, HD), lambda i, p: (0, i, 0, 0, 0)
        )
    else:
        shape, spec = (n_c, n_x, slots, rows, HD), pl.BlockSpec(
            (1, n_x, slots, rows, HD), lambda i, p: (i, 0, 0, 0, 0)
        )
    return pl.pallas_call(
        weight_grad_kernel,
        grid_spec=pltpu.PrefetchScalarGridSpec(
            num_scalar_prefetch=1, grid=(n_c,), in_specs=specs, out_specs=[spec, spec]
        ),
        out_shape=[jax.ShapeDtypeStruct(shape, BF)] * 2,
        compiler_params=pltpu.CompilerParams(vmem_limit_bytes=48 * 2**20),
    )(place, *args)


def shift(value, axis, step, size, stride=1):
    count = size * stride
    return lax.ppermute(value, axis, [(i, (i + step * stride) % count) for i in range(count)])


def ring_gather(value, axis, size, last_forward):
    found = {0: value}
    up = down = value
    for step in range(1, size // 2):
        up = shift(up, axis, 1, size)
        down = shift(down, axis, -1, size)
        found[size - step], found[step] = up, down
    found[size // 2] = shift(up, axis, 1, size) if last_forward else shift(down, axis, -1, size)
    return [found[d] for d in range(size)]


def add(*values):
    return sum(v.astype(F32) for v in values).astype(BF)


def ring_scatter(parts, move):
    own, right, far, left = parts
    half = far.shape[0] // 2
    from_left = move(far[:half], 1)
    from_right = move(far[half:], -1)
    right = jnp.concatenate([add(right[:half], from_left), right[half:]], axis=0)
    left = jnp.concatenate([left[:half], add(left[half:], from_right)], axis=0)
    return own, move(right, 1), move(left, -1)


def scatter_grads(mine, other, x_first):
    moves = [
        lambda v, s: shift(v, "frame", s, 4, 2),
        lambda v, s: shift(v, "clip", s, 4),
    ]
    if not x_first:
        moves = moves[::-1]
    received = lax.ppermute(other, "frame", [(i, i ^ 1) for i in range(8)])
    sums = ring_scatter([add(mine[i], received[i]) for i in range(4)], moves[0])
    sums = ring_scatter([add(*(s[i] for s in sums)) for i in range(4)], moves[1])
    return sum(s.astype(F32) for s in sums)


def body(spatial_qkv, w_qkv, w_out, out_grad, frame_clip, clip_patches):
    ranks = lax.axis_size("frame")
    width_ranks = lax.axis_size("tensor")
    at_frame = lax.axis_index("frame").astype(jnp.int32)
    at_clip = lax.axis_index("clip").astype(jnp.int32)
    at_width = lax.axis_index("tensor").astype(jnp.int32)
    clip_row = frame_clip[0]
    counts = clip_patches[0]
    total_frames = clip_row.shape[0]
    _, frames, patches, _, width = spatial_qkv.shape
    heads = width // HD
    block = patches // ranks
    rows_t = total_frames * block
    model = width * width_ranks
    slots = 4 * heads

    w_rows = w_qkv.shape[0]
    w_own = jnp.concatenate(
        [w_qkv.transpose(1, 2, 0, 3).reshape(3 * heads, w_rows, HD), w_out.transpose(0, 2, 1)],
        axis=0,
    )
    w_all = lax.all_gather(w_own, ("clip", "frame"), axis=1, tiled=True)

    own_clips = lax.dynamic_slice_in_dim(clip_row, at_frame * frames, frames, 0)
    member = own_clips[:, None] == jnp.arange(counts.shape[0], dtype=jnp.int32)[None, :]
    live = jnp.sum(jnp.where(member, counts[None, :], 0), axis=1).astype(jnp.int32)
    keys = (clip_row[:, None] * block + jnp.arange(block, dtype=jnp.int32)[None, :]).reshape(rows_t)

    qkv = spatial_qkv[0].transpose(0, 2, 1, 3)
    cot = out_grad[0]
    smem = pl.BlockSpec(memory_space=pltpu.SMEM)
    vmem = pl.BlockSpec(memory_space=pltpu.VMEM)
    anywhere = pl.BlockSpec(memory_space=pl.ANY)
    sent = pl.pallas_call(
        spatial_forward,
        out_shape=jax.ShapeDtypeStruct((ranks, 2, frames, block, width), BF),
        in_specs=[smem, vmem, vmem],
        out_specs=vmem,
        compiler_params=pltpu.CompilerParams(vmem_limit_bytes=24 * 2**20),
    )(live, qkv, cot)
    cols = lax.all_to_all(sent, "frame", split_axis=0, concat_axis=0, tiled=True)
    blocks = []
    for a in range(2):
        rows = cols[:, a].reshape(rows_t, width)
        blocks += ring_gather(rows, "tensor", width_ranks, a == 0)

    wide = jax.ShapeDtypeStruct((rows_t, model), BF)
    sums, d_qkv, mixed, feats, gated = pl.pallas_call(
        lambda *refs: temporal_kernel(heads, width_ranks, *refs),
        out_shape=[
            jax.ShapeDtypeStruct((width_ranks, ranks, 2, frames * block, width), BF),
            jax.ShapeDtypeStruct((rows_t, 3 * width), BF),
            jax.ShapeDtypeStruct((rows_t, width), BF),
            wide,
            wide,
        ],
        in_specs=[smem, vmem, vmem] + [anywhere] * (2 * width_ranks + 1),
        out_specs=[vmem] * 5,
        scratch_shapes=[
            pltpu.VMEM((slots, model, HD), BF),
            pltpu.SemaphoreType.DMA((slots,)),
            pltpu.SemaphoreType.DMA((2 * width_ranks,)),
        ],
        compiler_params=pltpu.CompilerParams(vmem_limit_bytes=48 * 2**20),
    )(at_width[None], keys[:, None], keys[None, :], *blocks, w_all)

    own_sums = lax.psum_scatter(sums, "tensor", scatter_dimension=0, tiled=True)[0]
    place = jnp.stack([at_clip, at_frame // 2, at_frame % 2, at_frame * 0])
    split = slots // 2 * HD
    first = weight_grads(place, [(feats, d_qkv[:, :split])], slots // 2, True)
    second = weight_grads(place, [(feats, d_qkv[:, split:]), (gated, mixed)], slots // 2, False)

    row_sums = lax.all_to_all(own_sums, "frame", split_axis=0, concat_axis=0, tiled=True)
    row_sums = row_sums.reshape(ranks, 2, frames, block, width)
    block_out, qkv_grad = pl.pallas_call(
        spatial_backward,
        out_shape=[
            jax.ShapeDtypeStruct((frames, patches, width), BF),
            jax.ShapeDtypeStruct((frames, 3, patches, width), BF),
        ],
        in_specs=[smem, vmem, vmem, vmem],
        out_specs=[vmem, vmem],
        compiler_params=pltpu.CompilerParams(vmem_limit_bytes=24 * 2**20),
    )(live, qkv, cot, row_sums)

    grads = jnp.concatenate(
        [scatter_grads(*first, True), scatter_grads(*second, False)], axis=0
    )
    w_qkv_grad = grads[: 3 * heads].reshape(heads, 3, w_rows, HD).transpose(2, 0, 1, 3)
    w_out_grad = grads[3 * heads :].transpose(0, 2, 1)
    return (block_out[None], qkv_grad.transpose(0, 2, 1, 3)[None], w_qkv_grad, w_out_grad)


def solution(mesh):
    in_specs = (
        P("clip", "frame", None, None, "tensor"),
        P(("clip", "frame"), "tensor", None, None),
        P("tensor", None, ("clip", "frame")),
        P("clip", "frame", None, "tensor"),
        P("clip", None),
        P("clip", None),
    )
    out_specs = (
        P("clip", "frame", None, "tensor"),
        P("clip", "frame", None, None, "tensor"),
        P(("clip", "frame"), "tensor", None, None),
        P("tensor", None, ("clip", "frame")),
    )
    return jax.shard_map(body, mesh=mesh, in_specs=in_specs, out_specs=out_specs, check_vma=False)
```

```python
import math

import jax
import jax.numpy as jnp
from jax import lax
from jax.experimental import pallas as pl
from jax.experimental.pallas import tpu as pltpu
from jax.sharding import PartitionSpec as P

HD = 128
SCALE = 1.0 / math.sqrt(HD)
BF = jnp.bfloat16
F32 = jnp.float32
NT = (((1,), (1,)), ((), ()))
TN = (((0,), (0,)), ((), ()))


def dot(a, b, dims=(((1,), (0,)), ((), ()))):
    return lax.dot_general(a, b, dims, preferred_element_type=F32)


def softmax(query, keys, mask):
    scores = jnp.where(mask, dot(query, keys, NT) * SCALE, -1e30)
    expo = jnp.exp(scores - jnp.max(scores, axis=-1, keepdims=True))
    return expo / jnp.sum(expo, axis=-1, keepdims=True)


def attention_grads(query, keys, values, probs, cotangent):
    d_values = dot(probs.astype(BF), cotangent, TN).astype(BF)
    d_probs = dot(cotangent, values, NT).astype(BF).astype(F32)
    inner = jnp.sum(probs * d_probs, axis=-1, keepdims=True)
    d_scores = (probs * (d_probs - inner) * SCALE).astype(BF)
    return dot(d_scores, keys).astype(BF), dot(d_scores, query, TN).astype(BF), d_values


def spatial_forward(count_ref, qkv_ref, cot_ref, out_ref):
    frames, _, patches, width = qkv_ref.shape
    owners = out_ref.shape[0]
    block = patches // owners
    for f in range(frames):
        count = count_ref[f]
        keys_live = lax.broadcasted_iota(jnp.int32, (patches, patches), 1) < count
        rows_live = lax.broadcasted_iota(jnp.int32, (patches, 1), 0) < count
        pieces = []
        for h in range(width // HD):
            cols = slice(h * HD, (h + 1) * HD)
            probs = softmax(qkv_ref[f, 0, :, cols], qkv_ref[f, 1, :, cols], keys_live)
            mixed = dot(probs.astype(BF), qkv_ref[f, 2, :, cols])
            pieces.append(jnp.where(rows_live, mixed, 0.0).astype(BF))
        whole = jnp.concatenate(pieces, axis=1)
        gated = jnp.where(rows_live, cot_ref[f].astype(F32), 0.0).astype(BF)
        for s in range(owners):
            out_ref[s, 0, f] = whole[s * block : (s + 1) * block]
            out_ref[s, 1, f] = gated[s * block : (s + 1) * block]


def spatial_backward(count_ref, qkv_ref, cot_ref, sums_ref, out_ref, grad_ref):
    frames, _, patches, width = qkv_ref.shape
    owners = sums_ref.shape[0]
    for f in range(frames):
        count = count_ref[f]
        keys_live = lax.broadcasted_iota(jnp.int32, (patches, patches), 1) < count
        rows_live = lax.broadcasted_iota(jnp.int32, (patches, 1), 0) < count
        projected = jnp.concatenate([sums_ref[s, 0, f] for s in range(owners)], axis=0)
        back = jnp.concatenate([sums_ref[s, 1, f] for s in range(owners)], axis=0)
        d_spatial = cot_ref[f].astype(F32) + back.astype(F32)
        d_mixed = jnp.where(rows_live, d_spatial, 0.0).astype(BF)
        for h in range(width // HD):
            cols = slice(h * HD, (h + 1) * HD)
            query, keys, values = (qkv_ref[f, i, :, cols] for i in range(3))
            probs = softmax(query, keys, keys_live)
            mixed = dot(probs.astype(BF), values).astype(BF).astype(F32)
            total = mixed + projected[:, cols].astype(F32)
            out_ref[f, :, cols] = jnp.where(rows_live, total, 0.0).astype(BF)
            grads = attention_grads(query, keys, values, probs, d_mixed[:, cols])
            for i in range(3):
                grad_ref[f, i, :, cols] = grads[i]


def assemble_kernel(ranks, place_ref, *refs):
    blocks, refs = refs[: 2 * ranks], refs[2 * ranks :]
    feat_ref, gated_ref, own_ref, other_ref, flip_ref, sem = refs
    me, core = place_ref[3], place_ref[2]
    width = feat_ref.shape[1] // ranks
    copies = []
    for a, whole in enumerate((feat_ref, gated_ref)):
        for d in range(ranks):
            start = pl.multiple_of(lax.rem(me + d, ranks) * width, HD)
            i = a * ranks + d
            copies.append(
                pltpu.make_async_copy(blocks[i], whole.at[:, pl.ds(start, width)], sem.at[i])
            )
    for copy in copies:
        copy.start()
    for copy in copies:
        copy.wait()
    pieces = 32
    rows = feat_ref.shape[1] // pieces
    for a, whole in enumerate((feat_ref, gated_ref)):
        for z in range(ranks):
            part = slice(z * width, (z + 1) * width)
            flip_ref[part, :] = whole[:, part].T
        for i in range(pieces // 2):
            to = slice(i * rows, (i + 1) * rows)
            own_ref[a, to] = flip_ref[pl.ds(pl.multiple_of((2 * i + core) * rows, 16), rows), :]
            other_ref[a, to] = flip_ref[pl.ds(pl.multiple_of((2 * i + 1 - core) * rows, 16), rows), :]


def temporal_kernel(heads, row_key_ref, col_key_ref, feat_ref, gated_ref, _, *refs):
    w_hbm, sums_hbm, both_ref, w_ref, sums_ref, w_sem, out_sem = refs
    width = heads * HD
    slots = 4 * heads
    ranks, owners, _, rows, _ = sums_ref.shape
    loads = [
        pltpu.make_async_copy(w_hbm.at[i], w_ref.at[:, i * HD : (i + 1) * HD], w_sem.at[i])
        for i in range(slots)
    ]
    for copy in loads:
        copy.start()
    mask = row_key_ref[...] == col_key_ref[...]
    query, keys, values = [], [], []
    for h in range(heads):
        for i in range(3):
            loads[3 * h + i].wait()
        qkv = dot(feat_ref[...], w_ref[:, 3 * h * HD : 3 * (h + 1) * HD]).astype(BF)
        for i, parts in enumerate((query, keys, values)):
            parts.append(qkv[:, i * HD : (i + 1) * HD])
    for h in range(heads):
        loads[3 * heads + h].wait()
    cotangent = dot(gated_ref[...], w_ref[:, 3 * width :]).astype(BF)
    cotangent = [cotangent[:, h * HD : (h + 1) * HD] for h in range(heads)]
    each = range(heads)
    probs = [softmax(query[h], keys[h], mask) for h in each]
    for h in each:
        grads = attention_grads(query[h], keys[h], values[h], probs[h], cotangent[h])
        for i in range(3):
            start = (3 * h + i) * HD
            both_ref[:, start : start + HD] = grads[i]
        start = 3 * width + h * HD
        both_ref[:, start : start + HD] = dot(probs[h].astype(BF), values[h]).astype(BF)
    stores = []
    for z in range(ranks):
        part = slice(z * width, (z + 1) * width)
        projected = dot(both_ref[:, 3 * width :], w_ref[part, 3 * width :], NT).astype(BF)
        back = dot(both_ref[:, : 3 * width], w_ref[part, : 3 * width], NT).astype(BF)
        for s in range(owners):
            sums_ref[z, s, 0] = projected[s * rows : (s + 1) * rows]
            sums_ref[z, s, 1] = back[s * rows : (s + 1) * rows]
        stores.append(pltpu.make_async_copy(sums_ref.at[z], sums_hbm.at[z], out_sem.at[z]))
        stores[-1].start()
    for copy in stores:
        copy.wait()


def weight_grad_kernel(step, place_ref, own_ref, pair_ref, both_ref, pair_both_ref, out_ref):
    at_clip, at_x, core = place_ref[0], place_ref[1], place_ref[2]
    n, slots, rows, _ = out_ref.shape
    wide = both_ref.shape[1] * 3 // 4
    starts = []
    for r in range(n):
        clip = lax.rem(at_clip + jnp.where(core == 0, r, step), n)
        x = lax.rem(at_x + jnp.where(core == 0, step, r), n)
        starts.append(pl.multiple_of((clip * n + x) * rows, 16))
    for a, cols in ((0, slice(0, wide)), (1, slice(wide, 4 * wide // 3))):
        left = jnp.concatenate(
            [
                jnp.concatenate([ref[a, pl.ds(start, rows), :] for start in starts], axis=0)
                for ref in (own_ref, pair_ref)
            ],
            axis=1,
        )
        right = jnp.concatenate([both_ref[:, cols], pair_both_ref[:, cols]], axis=0)
        total = dot(left, right).astype(BF)
        for r in range(n):
            for s in range(total.shape[1] // HD):
                part = total[r * rows : (r + 1) * rows, s * HD : (s + 1) * HD]
                out_ref[r, a * (slots * 3 // 4) + s] = part


def shift(value, axis, step, size):
    return lax.ppermute(value, axis, [(i, (i + step) % size) for i in range(size)])


def pair_swap(value):
    return lax.ppermute(value, "frame", [(i, i ^ 1) for i in range(8)])


def spread(value, step, second):
    pairs = []
    for clip in range(4):
        for x in range(4):
            for core in range(2):
                to_clip, to_x = clip, x
                if (core == 0) != second:
                    to_x = (x + step) % 4
                else:
                    to_clip = (clip + step) % 4
                pairs.append((clip * 8 + x * 2 + core, to_clip * 8 + to_x * 2 + core))
    return lax.ppermute(value, ("clip", "frame"), pairs)


def ring_gather(value, axis, size, last_forward):
    found = {0: value}
    up = down = value
    for step in range(1, size // 2):
        up = shift(up, axis, 1, size)
        down = shift(down, axis, -1, size)
        found[size - step], found[step] = up, down
    found[size // 2] = shift(up, axis, 1, size) if last_forward else shift(down, axis, -1, size)
    return [found[d] for d in range(size)]


def add(*values):
    return sum(v.astype(F32) for v in values)


def body(spatial_qkv, w_qkv, w_out, out_grad, frame_clip, clip_patches):
    ranks = lax.axis_size("frame")
    width_ranks = lax.axis_size("tensor")
    at_frame = lax.axis_index("frame").astype(jnp.int32)
    at_clip = lax.axis_index("clip").astype(jnp.int32)
    at_width = lax.axis_index("tensor").astype(jnp.int32)
    clip_row = frame_clip[0]
    counts = clip_patches[0]
    total_frames = clip_row.shape[0]
    _, frames, patches, _, width = spatial_qkv.shape
    heads = width // HD
    block = patches // ranks
    rows_t = total_frames * block
    model = width * width_ranks
    slots = 4 * heads

    w_rows = w_qkv.shape[0]
    w_own = jnp.concatenate(
        [w_qkv.transpose(1, 2, 0, 3).reshape(3 * heads, w_rows, HD), w_out.transpose(0, 2, 1)],
        axis=0,
    )
    w_all = lax.all_gather(w_own, ("clip", "frame"), axis=1, tiled=True)

    own_clips = lax.dynamic_slice_in_dim(clip_row, at_frame * frames, frames, 0)
    member = own_clips[:, None] == jnp.arange(counts.shape[0], dtype=jnp.int32)[None, :]
    live = jnp.sum(jnp.where(member, counts[None, :], 0), axis=1).astype(jnp.int32)
    keys = (clip_row[:, None] * block + jnp.arange(block, dtype=jnp.int32)[None, :]).reshape(rows_t)

    qkv = spatial_qkv[0].transpose(0, 2, 1, 3)
    cot = out_grad[0]
    smem = pl.BlockSpec(memory_space=pltpu.SMEM)
    vmem = pl.BlockSpec(memory_space=pltpu.VMEM)
    hbm = pl.BlockSpec(memory_space=pltpu.HBM)
    sent = pl.pallas_call(
        spatial_forward,
        out_shape=jax.ShapeDtypeStruct((ranks, 2, frames, block, width), BF),
        in_specs=[smem, vmem, vmem],
        out_specs=vmem,
        compiler_params=pltpu.CompilerParams(vmem_limit_bytes=24 * 2**20),
    )(live, qkv, cot)
    cols = lax.all_to_all(sent, "frame", split_axis=0, concat_axis=0, tiled=True)
    blocks = []
    for a in range(2):
        rows = cols[:, a].reshape(rows_t, width)
        blocks += ring_gather(rows, "tensor", width_ranks, a == 0)

    place = jnp.stack([at_clip, at_frame // 2, at_frame % 2, at_width])
    halves = jax.ShapeDtypeStruct((2, model // 2, rows_t), BF)
    wide = jax.ShapeDtypeStruct((rows_t, model), BF)
    feats, gated, own_flip, other_flip = pl.pallas_call(
        lambda *refs: assemble_kernel(width_ranks, *refs),
        out_shape=[wide, wide, halves, halves],
        in_specs=[smem] + [hbm] * (2 * width_ranks),
        out_specs=[vmem] * 4,
        scratch_shapes=[
            pltpu.VMEM((model, rows_t), BF),
            pltpu.SemaphoreType.DMA((2 * width_ranks,)),
        ],
        compiler_params=pltpu.CompilerParams(vmem_limit_bytes=58 * 2**20),
    )(place, *blocks)
    pair_flip = pair_swap(other_flip)

    sums_shape = (width_ranks, ranks, 2, frames * block, width)
    sums, both = pl.pallas_call(
        lambda *refs: temporal_kernel(heads, *refs),
        out_shape=[
            jax.ShapeDtypeStruct(sums_shape, BF),
            jax.ShapeDtypeStruct((rows_t, 4 * width), BF),
        ],
        in_specs=[vmem] * 4 + [hbm] * 2,
        out_specs=[hbm, vmem],
        scratch_shapes=[
            pltpu.VMEM((model, 4 * width), BF),
            pltpu.VMEM(sums_shape, BF),
            pltpu.SemaphoreType.DMA((slots,)),
            pltpu.SemaphoreType.DMA((width_ranks,)),
        ],
        compiler_params=pltpu.CompilerParams(vmem_limit_bytes=56 * 2**20),
    )(keys[:, None], keys[None, :], feats, gated, pair_flip, w_all)

    own_sums = lax.psum_scatter(sums, "tensor", scatter_dimension=0, tiled=True)[0]
    pair_both = pair_swap(both)
    parts = {}
    for step in (2, 1, 3, 0):
        parts[step] = pl.pallas_call(
            lambda *refs, step=step: weight_grad_kernel(step, *refs),
            out_shape=jax.ShapeDtypeStruct((4, slots, w_rows, HD), BF),
            in_specs=[smem] + [vmem] * 4,
            out_specs=vmem,
            compiler_params=pltpu.CompilerParams(vmem_limit_bytes=24 * 2**20),
        )(place, own_flip, pair_flip, both, pair_both)
    arrived = [parts[0]] + [spread(parts[step], step, False) for step in (2, 1, 3)]
    partial = [add(*(part[i] for part in arrived)).astype(BF) for i in range(4)]
    grads = add(partial[0], *(spread(partial[step], step, True) for step in (2, 1, 3)))

    row_sums = lax.all_to_all(own_sums, "frame", split_axis=0, concat_axis=0, tiled=True)
    row_sums = row_sums.reshape(ranks, 2, frames, block, width)
    block_out, qkv_grad = pl.pallas_call(
        spatial_backward,
        out_shape=[
            jax.ShapeDtypeStruct((frames, patches, width), BF),
            jax.ShapeDtypeStruct((frames, 3, patches, width), BF),
        ],
        in_specs=[smem, vmem, vmem, vmem],
        out_specs=[vmem, vmem],
        compiler_params=pltpu.CompilerParams(vmem_limit_bytes=24 * 2**20),
    )(live, qkv, cot, row_sums)

    w_qkv_grad = grads[: 3 * heads].reshape(heads, 3, w_rows, HD).transpose(2, 0, 1, 3)
    w_out_grad = grads[3 * heads :].transpose(0, 2, 1)
    return (block_out[None], qkv_grad.transpose(0, 2, 1, 3)[None], w_qkv_grad, w_out_grad)


def solution(mesh):
    in_specs = (
        P("clip", "frame", None, None, "tensor"),
        P(("clip", "frame"), "tensor", None, None),
        P("tensor", None, ("clip", "frame")),
        P("clip", "frame", None, "tensor"),
        P("clip", None),
        P("clip", None),
    )
    out_specs = (
        P("clip", "frame", None, "tensor"),
        P("clip", "frame", None, None, "tensor"),
        P(("clip", "frame"), "tensor", None, None),
        P("tensor", None, ("clip", "frame")),
    )
    return jax.shard_map(body, mesh=mesh, in_specs=in_specs, out_specs=out_specs, check_vma=False)
```

```python
import math

import jax
import jax.numpy as jnp
from jax import lax
from jax.experimental import pallas as pl
from jax.experimental.pallas import tpu as pltpu
from jax.sharding import PartitionSpec as P

HD = 128
SCALE = 1.0 / math.sqrt(HD)
BF = jnp.bfloat16
F32 = jnp.float32
NT = (((1,), (1,)), ((), ()))
TN = (((0,), (0,)), ((), ()))


def dot(a, b, dims=(((1,), (0,)), ((), ()))):
    return lax.dot_general(a, b, dims, preferred_element_type=F32)


def softmax(query, keys, mask):
    scores = jnp.where(mask, dot(query, keys, NT) * SCALE, -1e30)
    expo = jnp.exp(scores - jnp.max(scores, axis=-1, keepdims=True))
    return expo / jnp.sum(expo, axis=-1, keepdims=True)


def attention_grads(query, keys, values, probs, cotangent):
    d_values = dot(probs.astype(BF), cotangent, TN).astype(BF)
    d_probs = dot(cotangent, values, NT).astype(BF).astype(F32)
    inner = jnp.sum(probs * d_probs, axis=-1, keepdims=True)
    d_scores = (probs * (d_probs - inner) * SCALE).astype(BF)
    return dot(d_scores, keys).astype(BF), dot(d_scores, query, TN).astype(BF), d_values


def spatial_forward(count_ref, qkv_ref, cot_ref, out_ref):
    frames, _, patches, width = qkv_ref.shape
    owners = out_ref.shape[0]
    block = patches // owners
    for f in range(frames):
        count = count_ref[f]
        keys_live = lax.broadcasted_iota(jnp.int32, (patches, patches), 1) < count
        rows_live = lax.broadcasted_iota(jnp.int32, (patches, 1), 0) < count
        pieces = []
        for h in range(width // HD):
            cols = slice(h * HD, (h + 1) * HD)
            probs = softmax(qkv_ref[f, 0, :, cols], qkv_ref[f, 1, :, cols], keys_live)
            mixed = dot(probs.astype(BF), qkv_ref[f, 2, :, cols])
            pieces.append(jnp.where(rows_live, mixed, 0.0).astype(BF))
        whole = jnp.concatenate(pieces, axis=1)
        gated = jnp.where(rows_live, cot_ref[f].astype(F32), 0.0).astype(BF)
        for s in range(owners):
            out_ref[s, 0, f] = whole[s * block : (s + 1) * block]
            out_ref[s, 1, f] = gated[s * block : (s + 1) * block]


def spatial_backward(count_ref, qkv_ref, cot_ref, sums_ref, out_ref, grad_ref):
    frames, _, patches, width = qkv_ref.shape
    owners = sums_ref.shape[0]
    for f in range(frames):
        count = count_ref[f]
        keys_live = lax.broadcasted_iota(jnp.int32, (patches, patches), 1) < count
        rows_live = lax.broadcasted_iota(jnp.int32, (patches, 1), 0) < count
        projected = jnp.concatenate([sums_ref[s, 0, f] for s in range(owners)], axis=0)
        back = jnp.concatenate([sums_ref[s, 1, f] for s in range(owners)], axis=0)
        d_spatial = cot_ref[f].astype(F32) + back.astype(F32)
        d_mixed = jnp.where(rows_live, d_spatial, 0.0).astype(BF)
        for h in range(width // HD):
            cols = slice(h * HD, (h + 1) * HD)
            query, keys, values = (qkv_ref[f, i, :, cols] for i in range(3))
            probs = softmax(query, keys, keys_live)
            mixed = dot(probs.astype(BF), values).astype(BF).astype(F32)
            total = mixed + projected[:, cols].astype(F32)
            out_ref[f, :, cols] = jnp.where(rows_live, total, 0.0).astype(BF)
            grads = attention_grads(query, keys, values, probs, d_mixed[:, cols])
            for i in range(3):
                grad_ref[f, i, :, cols] = grads[i]


def pack_kernel(qkv_ref, out_ref, packed_ref):
    for ref, first in ((qkv_ref, 0), (out_ref, qkv_ref.shape[0])):
        for s in range(ref.shape[0]):
            packed_ref[:, (first + s) * HD : (first + s + 1) * HD] = ref[s]


def flip_kernel(place_ref, whole_ref, own_ref, other_ref):
    core = place_ref[2]
    pieces = 32
    owners, _, tokens, model = whole_ref.shape
    rows = model // pieces
    step = 4 * rows
    for a in range(2):
        for z in range(model // step):
            part = whole_ref[:, a, :, z * step : (z + 1) * step]
            flipped = part.reshape(owners * tokens, step).T
            for i in range(2):
                even = flipped[2 * i * rows : (2 * i + 1) * rows]
                odd = flipped[(2 * i + 1) * rows : (2 * i + 2) * rows]
                to = slice((2 * z + i) * rows, (2 * z + i + 1) * rows)
                own_ref[a, to] = jnp.where(core == 0, even, odd)
                other_ref[a, to] = jnp.where(core == 0, odd, even)


def temporal_kernel(heads, place_ref, row_key_ref, col_key_ref, whole_hbm, *refs):
    planes, refs = refs[:-8], refs[-8:]
    sums_hbm, both_ref, w_ref, token_ref, sums_ref, w_sem, in_sem, out_sem = refs
    at_clip, at_x, core = place_ref[0], place_ref[1], place_ref[2]
    width = heads * HD
    ranks, owners, _, rows, _ = sums_ref.shape
    n, w_rows, _ = planes[0].shape
    tokens = [
        pltpu.make_async_copy(whole_hbm.at[:, a], token_ref.at[a], in_sem.at[a]) for a in range(2)
    ]
    loads = [[] for _ in range(heads + 1)]
    for half, owner in ((0, core), (1, 1 - core)):
        for second in range(n):
            for first in range(n):
                clip = lax.rem(at_clip + n - jnp.where(owner == 0, second, first), n)
                x = lax.rem(at_x + n - jnp.where(owner == 0, first, second), n)
                start = pl.multiple_of((clip * 2 * n + x * 2 + owner) * w_rows, 16)
                for g in range(heads + 1):
                    cols = pl.ds(g * width, width)
                    loads[g].append(
                        pltpu.make_async_copy(
                            planes[half * n + second].at[first, :, cols],
                            w_ref.at[pl.ds(start, w_rows), cols],
                            w_sem.at[g, len(loads[g])],
                        )
                    )

    def start(g):
        for copy in loads[g]:
            copy.start()

    def finish(g):
        for copy in loads[g]:
            copy.wait()

    tokens[0].start()
    start(0)
    start(1)
    mask = row_key_ref[...] == col_key_ref[...]
    tokens[0].wait()
    feats = token_ref[0].reshape(owners * rows, -1)
    query, keys, values = [], [], []
    for h in range(heads):
        finish(h)
        if h == 0:
            tokens[1].start()
        if h + 2 <= heads:
            start(h + 2)
        qkv = dot(feats, w_ref[:, h * width : (h + 1) * width]).astype(BF)
        for i, parts in enumerate((query, keys, values)):
            parts.append(qkv[:, i * HD : (i + 1) * HD])
    each = range(heads)
    probs = [softmax(query[h], keys[h], mask) for h in each]
    mixed = [dot(probs[h].astype(BF), values[h]).astype(BF) for h in each]
    tokens[1].wait()
    finish(heads)
    gated = token_ref[1].reshape(owners * rows, -1)
    cotangent = dot(gated, w_ref[:, 3 * width :]).astype(BF)
    for h in each:
        cols = slice(h * HD, (h + 1) * HD)
        grads = attention_grads(query[h], keys[h], values[h], probs[h], cotangent[:, cols])
        for i in range(3):
            both_ref[:, (3 * h + i) * HD : (3 * h + i + 1) * HD] = grads[i]
        both_ref[:, 3 * width + h * HD : 3 * width + (h + 1) * HD] = mixed[h]
    stores = []
    pair = 2
    for first in range(0, ranks, pair):
        part = slice(first * width, (first + pair) * width)
        projected = dot(both_ref[:, 3 * width :], w_ref[part, 3 * width :], NT).astype(BF)
        back = dot(both_ref[:, : 3 * width], w_ref[part, : 3 * width], NT).astype(BF)
        for i in range(pair):
            z, cols = first + i, slice(i * width, (i + 1) * width)
            for s in range(owners):
                sums_ref[z, s, 0] = projected[s * rows : (s + 1) * rows, cols]
                sums_ref[z, s, 1] = back[s * rows : (s + 1) * rows, cols]
            stores.append(pltpu.make_async_copy(sums_ref.at[z], sums_hbm.at[z], out_sem.at[z]))
            stores[-1].start()
    for copy in stores:
        copy.wait()


def weight_grad_kernel(step, place_ref, own_ref, pair_ref, both_ref, pair_both_ref, out_ref):
    at_clip, at_x, core = place_ref[0], place_ref[1], place_ref[2]
    n, slots, rows, _ = out_ref.shape
    wide = both_ref.shape[1] * 3 // 4
    starts = []
    for r in range(n):
        clip = lax.rem(at_clip + jnp.where(core == 0, r, step), n)
        x = lax.rem(at_x + jnp.where(core == 0, step, r), n)
        starts.append(pl.multiple_of((clip * n + x) * rows, 16))
    for a, cols in ((0, slice(0, wide)), (1, slice(wide, 4 * wide // 3))):
        left = jnp.concatenate(
            [
                jnp.concatenate([ref[a, pl.ds(start, rows), :] for start in starts], axis=0)
                for ref in (own_ref, pair_ref)
            ],
            axis=1,
        )
        right = jnp.concatenate([both_ref[:, cols], pair_both_ref[:, cols]], axis=0)
        total = dot(left, right).astype(BF)
        for r in range(n):
            for s in range(total.shape[1] // HD):
                part = total[r * rows : (r + 1) * rows, s * HD : (s + 1) * HD]
                out_ref[r, a * (slots * 3 // 4) + s] = part


def pair_swap(value):
    return lax.ppermute(value, "frame", [(i, i ^ 1) for i in range(8)])


def spread(value, step, second):
    pairs = []
    for clip in range(4):
        for x in range(4):
            for core in range(2):
                to_clip, to_x = clip, x
                if (core == 0) != second:
                    to_x = (x + step) % 4
                else:
                    to_clip = (clip + step) % 4
                pairs.append((clip * 8 + x * 2 + core, to_clip * 8 + to_x * 2 + core))
    return lax.ppermute(value, ("clip", "frame"), pairs)


def add(*values):
    return sum(v.astype(F32) for v in values)


def body(spatial_qkv, w_qkv, w_out, out_grad, frame_clip, clip_patches):
    ranks = lax.axis_size("frame")
    width_ranks = lax.axis_size("tensor")
    at_frame = lax.axis_index("frame").astype(jnp.int32)
    at_clip = lax.axis_index("clip").astype(jnp.int32)
    at_width = lax.axis_index("tensor").astype(jnp.int32)
    clip_row = frame_clip[0]
    counts = clip_patches[0]
    total_frames = clip_row.shape[0]
    _, frames, patches, _, width = spatial_qkv.shape
    heads = width // HD
    block = patches // ranks
    rows_t = total_frames * block
    model = width * width_ranks
    slots = 4 * heads

    w_rows = w_qkv.shape[0]
    place = jnp.stack([at_clip, at_frame // 2, at_frame % 2, at_width])
    smem = pl.BlockSpec(memory_space=pltpu.SMEM)
    vmem = pl.BlockSpec(memory_space=pltpu.VMEM)
    hbm = pl.BlockSpec(memory_space=pltpu.HBM)
    packed = pl.pallas_call(
        pack_kernel,
        out_shape=jax.ShapeDtypeStruct((w_rows, slots * HD), BF),
        in_specs=[vmem, vmem],
        out_specs=vmem,
    )(w_qkv.transpose(1, 2, 0, 3).reshape(3 * heads, w_rows, HD), w_out.transpose(0, 2, 1))
    line = jnp.stack([packed] + [spread(packed, step, False) for step in (1, 2, 3)])
    plane = [line] + [spread(line, step, True) for step in (1, 2, 3)]
    plane += [pair_swap(rows) for rows in plane]

    own_clips = lax.dynamic_slice_in_dim(clip_row, at_frame * frames, frames, 0)
    member = own_clips[:, None] == jnp.arange(counts.shape[0], dtype=jnp.int32)[None, :]
    live = jnp.sum(jnp.where(member, counts[None, :], 0), axis=1).astype(jnp.int32)
    keys = (clip_row[:, None] * block + jnp.arange(block, dtype=jnp.int32)[None, :]).reshape(rows_t)

    qkv = spatial_qkv[0].transpose(0, 2, 1, 3)
    cot = out_grad[0]
    sent = pl.pallas_call(
        spatial_forward,
        out_shape=jax.ShapeDtypeStruct((ranks, 2, frames, block, width), BF),
        in_specs=[smem, vmem, vmem],
        out_specs=vmem,
        compiler_params=pltpu.CompilerParams(vmem_limit_bytes=24 * 2**20),
    )(live, qkv, cot)
    cols = lax.all_to_all(sent, "frame", split_axis=0, concat_axis=0, tiled=True)
    cols = cols.reshape(ranks, 2, frames * block, width)
    whole = lax.all_gather(cols, "tensor", axis=3, tiled=True)

    sums_shape = (width_ranks, ranks, 2, frames * block, width)
    sums, both = pl.pallas_call(
        lambda *refs: temporal_kernel(heads, *refs),
        out_shape=[
            jax.ShapeDtypeStruct(sums_shape, BF),
            jax.ShapeDtypeStruct((rows_t, 4 * width), BF),
        ],
        in_specs=[smem, vmem, vmem] + [hbm] * (1 + len(plane)),
        out_specs=[hbm, vmem],
        scratch_shapes=[
            pltpu.VMEM((model, 4 * width), BF),
            pltpu.VMEM((2, ranks, frames * block, model), BF),
            pltpu.VMEM(sums_shape, BF),
            pltpu.SemaphoreType.DMA((heads + 1, 4 * len(plane))),
            pltpu.SemaphoreType.DMA((2,)),
            pltpu.SemaphoreType.DMA((width_ranks,)),
        ],
        compiler_params=pltpu.CompilerParams(vmem_limit_bytes=58 * 2**20),
    )(place, keys[:, None], keys[None, :], whole, *plane)

    halves = jax.ShapeDtypeStruct((2, model // 2, rows_t), BF)
    own_flip, other_flip = pl.pallas_call(
        flip_kernel,
        out_shape=[halves, halves],
        in_specs=[smem, vmem],
        out_specs=[vmem] * 2,
        compiler_params=pltpu.CompilerParams(vmem_limit_bytes=16 * 2**20),
    )(place, whole)
    pair_flip = pair_swap(other_flip)
    own_sums = lax.psum_scatter(sums, "tensor", scatter_dimension=0, tiled=True)[0]
    pair_both = pair_swap(both)
    parts = {}
    for step in (2, 1, 3, 0):
        parts[step] = pl.pallas_call(
            lambda *refs, step=step: weight_grad_kernel(step, *refs),
            out_shape=jax.ShapeDtypeStruct((4, slots, w_rows, HD), BF),
            in_specs=[smem] + [vmem] * 4,
            out_specs=vmem,
            compiler_params=pltpu.CompilerParams(vmem_limit_bytes=24 * 2**20),
        )(place, own_flip, pair_flip, both, pair_both)
    arrived = [parts[0]] + [spread(parts[step], step, False) for step in (2, 1, 3)]
    partial = [add(*(part[i] for part in arrived)).astype(BF) for i in range(4)]
    grads = add(partial[0], *(spread(partial[step], step, True) for step in (2, 1, 3)))

    row_sums = lax.all_to_all(own_sums, "frame", split_axis=0, concat_axis=0, tiled=True)
    row_sums = row_sums.reshape(ranks, 2, frames, block, width)
    block_out, qkv_grad = pl.pallas_call(
        spatial_backward,
        out_shape=[
            jax.ShapeDtypeStruct((frames, patches, width), BF),
            jax.ShapeDtypeStruct((frames, 3, patches, width), BF),
        ],
        in_specs=[smem, vmem, vmem, vmem],
        out_specs=[vmem, vmem],
        compiler_params=pltpu.CompilerParams(vmem_limit_bytes=24 * 2**20),
    )(live, qkv, cot, row_sums)

    w_qkv_grad = grads[: 3 * heads].reshape(heads, 3, w_rows, HD).transpose(2, 0, 1, 3)
    w_out_grad = grads[3 * heads :].transpose(0, 2, 1)
    return (block_out[None], qkv_grad.transpose(0, 2, 1, 3)[None], w_qkv_grad, w_out_grad)


def solution(mesh):
    in_specs = (
        P("clip", "frame", None, None, "tensor"),
        P(("clip", "frame"), "tensor", None, None),
        P("tensor", None, ("clip", "frame")),
        P("clip", "frame", None, "tensor"),
        P("clip", None),
        P("clip", None),
    )
    out_specs = (
        P("clip", "frame", None, "tensor"),
        P("clip", "frame", None, None, "tensor"),
        P(("clip", "frame"), "tensor", None, None),
        P("tensor", None, ("clip", "frame")),
    )
    return jax.shard_map(body, mesh=mesh, in_specs=in_specs, out_specs=out_specs, check_vma=False)
```

```python
import math

import jax
import jax.numpy as jnp
from jax import lax
from jax.experimental import pallas as pl
from jax.experimental.pallas import tpu as pltpu
from jax.sharding import PartitionSpec as P

HD = 128
SCALE = 1.0 / math.sqrt(HD)
BF = jnp.bfloat16
F32 = jnp.float32
NT = (((1,), (1,)), ((), ()))
TN = (((0,), (0,)), ((), ()))


def dot(a, b, dims=(((1,), (0,)), ((), ()))):
    return lax.dot_general(a, b, dims, preferred_element_type=F32)


def softmax(query, keys, mask):
    scores = jnp.where(mask, dot(query, keys, NT) * SCALE, -1e30)
    expo = jnp.exp(scores - jnp.max(scores, axis=-1, keepdims=True))
    return expo / jnp.sum(expo, axis=-1, keepdims=True)


def attention_grads(query, keys, values, probs, cotangent):
    d_values = dot(probs.astype(BF), cotangent, TN).astype(BF)
    d_probs = dot(cotangent, values, NT).astype(BF).astype(F32)
    inner = jnp.sum(probs * d_probs, axis=-1, keepdims=True)
    d_scores = (probs * (d_probs - inner) * SCALE).astype(BF)
    return dot(d_scores, keys).astype(BF), dot(d_scores, query, TN).astype(BF), d_values


def live_rows(row_ref, patch_ref, frame):
    return patch_ref[0, row_ref[0, frame]]


def spatial_forward(row_ref, patch_ref, qkv_ref, cot_ref, *refs):
    out_ref, whole_ref = refs
    frames, _, patches, width = qkv_ref.shape
    place = lax.axis_index("frame")
    owners = out_ref.shape[0]
    block = patches // owners
    for f in range(frames):
        count = live_rows(row_ref, patch_ref, place * frames + f)
        keys_live = lax.broadcasted_iota(jnp.int32, (patches, patches), 1) < count
        rows_live = lax.broadcasted_iota(jnp.int32, (patches, 1), 0) < count
        pieces = []
        for h in range(width // HD):
            cols = slice(h * HD, (h + 1) * HD)
            probs = softmax(qkv_ref[f, 0, :, cols], qkv_ref[f, 1, :, cols], keys_live)
            mixed = dot(probs.astype(BF), qkv_ref[f, 2, :, cols])
            pieces.append(jnp.where(rows_live, mixed, 0.0).astype(BF))
        whole_ref[0, f] = jnp.concatenate(pieces, axis=1)
        whole_ref[1, f] = jnp.where(rows_live, cot_ref[f].astype(F32), 0.0).astype(BF)
    for s in range(owners):
        out_ref[s] = whole_ref[:, :, s * block : (s + 1) * block, :]


def spatial_backward(row_ref, patch_ref, qkv_ref, cot_ref, *refs):
    blocks, (out_ref, grad_ref, whole_ref) = refs[:-3], refs[-3:]
    frames, _, patches, width = qkv_ref.shape
    place = lax.axis_index("frame")
    block = patches // len(blocks)
    for j, ref in enumerate(blocks):
        start = pl.multiple_of((place ^ j) * block, 16)
        for f in range(frames):
            whole_ref[:, f, pl.ds(start, block), :] = ref[:, f * block : (f + 1) * block, :]
    for f in range(frames):
        count = live_rows(row_ref, patch_ref, place * frames + f)
        keys_live = lax.broadcasted_iota(jnp.int32, (patches, patches), 1) < count
        rows_live = lax.broadcasted_iota(jnp.int32, (patches, 1), 0) < count
        d_spatial = cot_ref[f].astype(F32) + whole_ref[1, f].astype(F32)
        d_mixed = jnp.where(rows_live, d_spatial, 0.0).astype(BF)
        for h in range(width // HD):
            cols = slice(h * HD, (h + 1) * HD)
            query, keys, values = (qkv_ref[f, i, :, cols] for i in range(3))
            probs = softmax(query, keys, keys_live)
            mixed = dot(probs.astype(BF), values).astype(BF).astype(F32)
            total = mixed + whole_ref[0, f, :, cols].astype(F32)
            out_ref[f, :, cols] = jnp.where(rows_live, total, 0.0).astype(BF)
            grads = attention_grads(query, keys, values, probs, d_mixed[:, cols])
            for i in range(3):
                grad_ref[f, i, :, cols] = grads[i]


def pack_kernel(qkv_ref, out_ref, packed_ref):
    for ref, first in ((qkv_ref, 0), (out_ref, qkv_ref.shape[0])):
        for s in range(ref.shape[0]):
            packed_ref[:, (first + s) * HD : (first + s + 1) * HD] = ref[s]


def own_chip():
    place = lax.axis_index("frame")
    return lax.axis_index("clip"), place // 2, place % 2


def temporal_kernel(heads, row_key_ref, col_key_ref, whole_hbm, *refs):
    planes, refs = refs[:-11], refs[-11:]
    sums_hbm, both_ref, own_hbm, other_hbm, w_ref, token_ref, sums_ref, flip_ref = refs[:8]
    w_sem, in_sem, out_sem = refs[8:]
    at_clip, at_x, core = own_chip()
    place = lax.axis_index("frame")
    width = heads * HD
    ranks, owners, _, rows, _ = sums_ref.shape
    n, w_rows, _ = planes[0].shape
    tokens = [
        [
            pltpu.make_async_copy(
                whole_hbm.at[z, :, a],
                token_ref.at[a, :, :, z * width : (z + 1) * width],
                in_sem.at[a * ranks + z],
            )
            for z in range(ranks)
        ]
        for a in range(2)
    ]
    loads = [[], []]
    for half, owner in ((0, core), (1, 1 - core)):
        for second in range(n):
            for first in range(n):
                clip = lax.rem(at_clip + n - jnp.where(owner == 0, second, first), n)
                x = lax.rem(at_x + n - jnp.where(owner == 0, first, second), n)
                start = pl.multiple_of((clip * 2 * n + x * 2 + owner) * w_rows, 16)
                for g, cols in enumerate((pl.ds(0, 3 * width), pl.ds(3 * width, width))):
                    loads[g].append(
                        pltpu.make_async_copy(
                            planes[half * n + second].at[first, :, cols],
                            w_ref.at[pl.ds(start, w_rows), cols],
                            w_sem.at[g, len(loads[g])],
                        )
                    )
    for copy in tokens[0] + tokens[1] + loads[0]:
        copy.start()
    step = 4 * w_rows
    flips = []
    for a in range(2):
        for z in range(ranks):
            tokens[a][z].wait()
            part = token_ref[a, :, :, z * step : (z + 1) * step]
            flipped = part.reshape(owners * rows, step).T
            for i in range(2):
                even = flipped[2 * i * w_rows : (2 * i + 1) * w_rows]
                odd = flipped[(2 * i + 1) * w_rows : (2 * i + 2) * w_rows]
                to = slice((2 * z + i) * w_rows, (2 * z + i + 1) * w_rows)
                flip_ref[0, a, to] = jnp.where(core == 0, even, odd)
                flip_ref[1, a, to] = jnp.where(core == 0, odd, even)
    for i, ref in enumerate((own_hbm, other_hbm)):
        flips.append(pltpu.make_async_copy(flip_ref.at[i], ref, in_sem.at[2 * ranks + i]))
        flips[-1].start()
    mask = row_key_ref[...] == col_key_ref[...]
    for copy in loads[0]:
        copy.wait()
    for copy in loads[1]:
        copy.start()
    feats = token_ref[0].reshape(owners * rows, -1)
    query, keys, values = [], [], []
    for h in range(heads):
        qkv = dot(feats, w_ref[:, h * width : (h + 1) * width]).astype(BF)
        for i, parts in enumerate((query, keys, values)):
            parts.append(qkv[:, i * HD : (i + 1) * HD])
    each = range(heads)
    probs = [softmax(query[h], keys[h], mask) for h in each]
    mixed = [dot(probs[h].astype(BF), values[h]).astype(BF) for h in each]
    for copy in loads[1]:
        copy.wait()
    gated = token_ref[1].reshape(owners * rows, -1)
    cotangent = dot(gated, w_ref[:, 3 * width :]).astype(BF)
    for h in each:
        cols = slice(h * HD, (h + 1) * HD)
        grads = attention_grads(query[h], keys[h], values[h], probs[h], cotangent[:, cols])
        for i in range(3):
            both_ref[:, (3 * h + i) * HD : (3 * h + i + 1) * HD] = grads[i]
        both_ref[:, 3 * width + h * HD : 3 * width + (h + 1) * HD] = mixed[h]
    stores = []
    pair = 2
    for first in range(0, ranks, pair):
        part = slice(first * width, (first + pair) * width)
        projected = dot(both_ref[:, 3 * width :], w_ref[part, 3 * width :], NT).astype(BF)
        back = dot(both_ref[:, : 3 * width], w_ref[part, : 3 * width], NT).astype(BF)
        for i in range(pair):
            z, cols = first + i, slice(i * width, (i + 1) * width)
            for s in range(owners):
                sums_ref[z, s ^ place, 0] = projected[s * rows : (s + 1) * rows, cols]
                sums_ref[z, s ^ place, 1] = back[s * rows : (s + 1) * rows, cols]
            stores.append(pltpu.make_async_copy(sums_ref.at[z], sums_hbm.at[z], out_sem.at[z]))
            stores[-1].start()
    for copy in stores + flips:
        copy.wait()


def weight_grad_kernel(step, own_ref, pair_ref, both_ref, pair_both_ref, out_ref):
    at_clip, at_x, core = own_chip()
    n, slots, rows, _ = out_ref.shape
    wide = both_ref.shape[1] * 3 // 4
    starts = []
    for r in range(n):
        clip = lax.rem(at_clip + jnp.where(core == 0, r, step), n)
        x = lax.rem(at_x + jnp.where(core == 0, step, r), n)
        starts.append(pl.multiple_of((clip * n + x) * rows, 16))
    for a, cols in ((0, slice(0, wide)), (1, slice(wide, 4 * wide // 3))):
        left = jnp.concatenate(
            [
                jnp.concatenate([ref[a, pl.ds(start, rows), :] for start in starts], axis=0)
                for ref in (own_ref, pair_ref)
            ],
            axis=1,
        )
        right = jnp.concatenate([both_ref[:, cols], pair_both_ref[:, cols]], axis=0)
        total = dot(left, right).astype(BF)
        for r in range(n):
            for s in range(total.shape[1] // HD):
                part = total[r * rows : (r + 1) * rows, s * HD : (s + 1) * HD]
                out_ref[r, a * (slots * 3 // 4) + s] = part


def trade(value, j):
    return lax.ppermute(value, "frame", [(i, i ^ j) for i in range(8)])


def spread(value, step, second):
    pairs = []
    for clip in range(4):
        for x in range(4):
            for core in range(2):
                to_clip, to_x = clip, x
                if (core == 0) != second:
                    to_x = (x + step) % 4
                else:
                    to_clip = (clip + step) % 4
                pairs.append((clip * 8 + x * 2 + core, to_clip * 8 + to_x * 2 + core))
    return lax.ppermute(value, ("clip", "frame"), pairs)


def add(*values):
    return sum(v.astype(F32) for v in values)


def body(spatial_qkv, w_qkv, w_out, out_grad, frame_clip, clip_patches):
    ranks = lax.axis_size("frame")
    width_ranks = lax.axis_size("tensor")
    total_frames = frame_clip.shape[1]
    _, frames, patches, _, width = spatial_qkv.shape
    heads = width // HD
    block = patches // ranks
    rows_t = total_frames * block
    model = width * width_ranks
    slots = 4 * heads
    w_rows = w_qkv.shape[0]
    smem = pl.BlockSpec(memory_space=pltpu.SMEM)
    vmem = pl.BlockSpec(memory_space=pltpu.VMEM)
    hbm = pl.BlockSpec(memory_space=pltpu.HBM)

    qkv = spatial_qkv[0].transpose(0, 2, 1, 3)
    cot = out_grad[0]
    sent = pl.pallas_call(
        spatial_forward,
        out_shape=jax.ShapeDtypeStruct((ranks, 2, frames, block, width), BF),
        in_specs=[smem, smem, vmem, vmem],
        out_specs=vmem,
        scratch_shapes=[pltpu.VMEM((2, frames, patches, width), BF)],
        compiler_params=pltpu.CompilerParams(vmem_limit_bytes=58 * 2**20),
    )(frame_clip, clip_patches, qkv, cot)
    packed = pl.pallas_call(
        pack_kernel,
        out_shape=jax.ShapeDtypeStruct((w_rows, slots * HD), BF),
        in_specs=[vmem, vmem],
        out_specs=vmem,
    )(w_qkv.transpose(1, 2, 0, 3).reshape(3 * heads, w_rows, HD), w_out.transpose(0, 2, 1))
    near = [spread(packed, step, False) for step in (1, 2, 3)]
    cols = lax.all_to_all(sent, "frame", split_axis=0, concat_axis=0, tiled=True)
    cols = cols.reshape(ranks, 2, frames * block, width)
    cols, *near = lax.optimization_barrier([cols, *near])
    whole = lax.all_gather(cols, "tensor", axis=0, tiled=True)
    whole = whole.reshape((width_ranks,) + cols.shape)
    line = jnp.stack([packed] + near)
    plane = [line] + [spread(line, step, True) for step in (1, 2, 3)]
    plane += [trade(rows, 1) for rows in plane]

    clips = frame_clip[0][:, None] * block
    keys = (clips + jnp.arange(block, dtype=jnp.int32)[None, :]).reshape(rows_t)

    sums_shape = (width_ranks, ranks, 2, frames * block, width)
    halves = jax.ShapeDtypeStruct((2, model // 2, rows_t), BF)
    sums, both, own_flip, other_flip = pl.pallas_call(
        lambda *refs: temporal_kernel(heads, *refs),
        out_shape=[
            jax.ShapeDtypeStruct(sums_shape, BF),
            jax.ShapeDtypeStruct((rows_t, 4 * width), BF),
            halves,
            halves,
        ],
        in_specs=[vmem, vmem] + [hbm] * (1 + len(plane)),
        out_specs=[hbm, vmem, hbm, hbm],
        scratch_shapes=[
            pltpu.VMEM((model, 4 * width), BF),
            pltpu.VMEM((2, ranks, frames * block, model), BF),
            pltpu.VMEM(sums_shape, BF),
            pltpu.VMEM((2, 2, model // 2, rows_t), BF),
            pltpu.SemaphoreType.DMA((2, 4 * len(plane))),
            pltpu.SemaphoreType.DMA((2 * width_ranks + 2,)),
            pltpu.SemaphoreType.DMA((width_ranks,)),
        ],
        compiler_params=pltpu.CompilerParams(vmem_limit_bytes=58 * 2**20),
    )(keys[:, None], keys[None, :], whole, *plane)
    pair_flip = trade(other_flip, 1)
    own_sums = lax.psum_scatter(sums, "tensor", scatter_dimension=0, tiled=True)[0]
    pair_both = trade(both, 1)
    parts = {}
    for step in (2, 1, 3, 0):
        parts[step] = pl.pallas_call(
            lambda *refs, step=step: weight_grad_kernel(step, *refs),
            out_shape=jax.ShapeDtypeStruct((4, slots, w_rows, HD), BF),
            in_specs=[vmem] * 4,
            out_specs=vmem,
            compiler_params=pltpu.CompilerParams(vmem_limit_bytes=24 * 2**20),
        )(own_flip, pair_flip, both, pair_both)
    arrived = [parts[0]] + [spread(parts[step], step, False) for step in (2, 1, 3)]
    partial = [add(*(part[i] for part in arrived)).astype(BF) for i in range(4)]
    grads = add(partial[0], *(spread(partial[step], step, True) for step in (2, 1, 3)))

    traded = [own_sums[0]] + [trade(own_sums[j], j) for j in range(1, ranks)]
    block_out, qkv_grad = pl.pallas_call(
        spatial_backward,
        out_shape=[
            jax.ShapeDtypeStruct((frames, patches, width), BF),
            jax.ShapeDtypeStruct((frames, 3, patches, width), BF),
        ],
        in_specs=[smem, smem] + [vmem] * (2 + ranks),
        out_specs=[vmem, vmem],
        scratch_shapes=[pltpu.VMEM((2, frames, patches, width), BF)],
        compiler_params=pltpu.CompilerParams(vmem_limit_bytes=24 * 2**20),
    )(frame_clip, clip_patches, qkv, cot, *traded)

    w_qkv_grad = grads[: 3 * heads].reshape(heads, 3, w_rows, HD).transpose(2, 0, 1, 3)
    w_out_grad = grads[3 * heads :].transpose(0, 2, 1)
    return (block_out[None], qkv_grad.transpose(0, 2, 1, 3)[None], w_qkv_grad, w_out_grad)


def solution(mesh):
    in_specs = (
        P("clip", "frame", None, None, "tensor"),
        P(("clip", "frame"), "tensor", None, None),
        P("tensor", None, ("clip", "frame")),
        P("clip", "frame", None, "tensor"),
        P("clip", None),
        P("clip", None),
    )
    out_specs = (
        P("clip", "frame", None, "tensor"),
        P("clip", "frame", None, None, "tensor"),
        P(("clip", "frame"), "tensor", None, None),
        P("tensor", None, ("clip", "frame")),
    )
    return jax.shard_map(body, mesh=mesh, in_specs=in_specs, out_specs=out_specs, check_vma=False)
```

```python
import math

import jax
import jax.numpy as jnp
from jax import lax
from jax.experimental import pallas as pl
from jax.experimental.pallas import tpu as pltpu
from jax.sharding import PartitionSpec as P

HD = 128
SCALE = 1.0 / math.sqrt(HD)
BF = jnp.bfloat16
F32 = jnp.float32
NT = (((1,), (1,)), ((), ()))
TN = (((0,), (0,)), ((), ()))


def dot(a, b, dims=(((1,), (0,)), ((), ()))):
    return lax.dot_general(a, b, dims, preferred_element_type=F32)


def softmax(query, keys, mask):
    scores = jnp.where(mask, dot(query, keys, NT) * SCALE, -1e30)
    expo = jnp.exp(scores - jnp.max(scores, axis=-1, keepdims=True))
    return expo / jnp.sum(expo, axis=-1, keepdims=True)


def attention_grads(query, keys, values, probs, cotangent):
    d_values = dot(probs.astype(BF), cotangent, TN).astype(BF)
    d_probs = dot(cotangent, values, NT).astype(BF).astype(F32)
    inner = jnp.sum(probs * d_probs, axis=-1, keepdims=True)
    d_scores = (probs * (d_probs - inner) * SCALE).astype(BF)
    return dot(d_scores, keys).astype(BF), dot(d_scores, query, TN).astype(BF), d_values


def live_rows(row_ref, patch_ref, frame):
    return patch_ref[0, row_ref[0, frame]]


def spatial_forward(row_ref, patch_ref, qkv_ref, cot_ref, *refs):
    out_ref, whole_ref = refs
    frames, _, patches, width = qkv_ref.shape
    place = lax.axis_index("frame")
    owners = out_ref.shape[0]
    block = patches // owners
    for f in range(frames):
        count = live_rows(row_ref, patch_ref, place * frames + f)
        keys_live = lax.broadcasted_iota(jnp.int32, (patches, patches), 1) < count
        rows_live = lax.broadcasted_iota(jnp.int32, (patches, 1), 0) < count
        pieces = []
        for h in range(width // HD):
            cols = slice(h * HD, (h + 1) * HD)
            probs = softmax(qkv_ref[f, 0, :, cols], qkv_ref[f, 1, :, cols], keys_live)
            mixed = dot(probs.astype(BF), qkv_ref[f, 2, :, cols])
            pieces.append(jnp.where(rows_live, mixed, 0.0).astype(BF))
        whole_ref[0, f] = jnp.concatenate(pieces, axis=1)
        whole_ref[1, f] = jnp.where(rows_live, cot_ref[f].astype(F32), 0.0).astype(BF)
    for s in range(owners):
        out_ref[s] = whole_ref[:, :, s * block : (s + 1) * block, :]


def spatial_backward(row_ref, patch_ref, qkv_ref, cot_ref, *refs):
    sums_ref, out_ref, grad_ref, whole_ref = refs
    frames, _, patches, width = qkv_ref.shape
    place = lax.axis_index("frame")
    owners = sums_ref.shape[0]
    block = patches // owners
    for s in range(owners):
        for f in range(frames):
            part = sums_ref[s, :, f * block : (f + 1) * block, :]
            whole_ref[:, f, s * block : (s + 1) * block, :] = part
    for f in range(frames):
        count = live_rows(row_ref, patch_ref, place * frames + f)
        keys_live = lax.broadcasted_iota(jnp.int32, (patches, patches), 1) < count
        rows_live = lax.broadcasted_iota(jnp.int32, (patches, 1), 0) < count
        d_spatial = cot_ref[f].astype(F32) + whole_ref[1, f].astype(F32)
        d_mixed = jnp.where(rows_live, d_spatial, 0.0).astype(BF)
        for h in range(width // HD):
            cols = slice(h * HD, (h + 1) * HD)
            query, keys, values = (qkv_ref[f, i, :, cols] for i in range(3))
            probs = softmax(query, keys, keys_live)
            mixed = dot(probs.astype(BF), values).astype(BF).astype(F32)
            total = mixed + whole_ref[0, f, :, cols].astype(F32)
            out_ref[f, :, cols] = jnp.where(rows_live, total, 0.0).astype(BF)
            grads = attention_grads(query, keys, values, probs, d_mixed[:, cols])
            for i in range(3):
                grad_ref[f, i, :, cols] = grads[i]


def pack_kernel(qkv_ref, out_ref, packed_ref):
    for ref, first in ((qkv_ref, 0), (out_ref, qkv_ref.shape[0])):
        for s in range(ref.shape[0]):
            packed_ref[:, (first + s) * HD : (first + s + 1) * HD] = ref[s]


def own_chip():
    place = lax.axis_index("frame")
    return lax.axis_index("clip"), place // 2, place % 2


def line_kernel(own_ref, near_1, near_2, near_3, line_ref):
    at_clip, at_x, core = own_chip()
    at = jnp.where(core == 0, at_x, at_clip)
    for step, ref in enumerate((own_ref, near_1, near_2, near_3)):
        line_ref[lax.rem(at + 4 - step, 4)] = ref[...]


def flip_kernel(whole_ref, own_ref, other_ref):
    _, _, core = own_chip()
    pieces = 32
    owners, _, tokens, model = whole_ref.shape
    rows = model // pieces
    step = 4 * rows
    for a in range(2):
        for z in range(model // step):
            part = whole_ref[:, a, :, z * step : (z + 1) * step]
            flipped = part.reshape(owners * tokens, step).T
            for i in range(2):
                even = flipped[2 * i * rows : (2 * i + 1) * rows]
                odd = flipped[(2 * i + 1) * rows : (2 * i + 2) * rows]
                to = slice((2 * z + i) * rows, (2 * z + i + 1) * rows)
                own_ref[a, to] = jnp.where(core == 0, even, odd)
                other_ref[a, to] = jnp.where(core == 0, odd, even)


def temporal_kernel(heads, row_key_ref, col_key_ref, whole_hbm, *refs):
    planes, refs = refs[:-8], refs[-8:]
    sums_hbm, both_ref, w_ref, token_ref, sums_ref, w_sem, in_sem, out_sem = refs
    at_clip, at_x, core = own_chip()
    width = heads * HD
    groups = heads + 1
    ranks, owners, _, rows, _ = sums_ref.shape
    n = w_ref.shape[0]
    tokens = [
        pltpu.make_async_copy(whole_hbm.at[:, a], token_ref.at[a], in_sem.at[a]) for a in range(2)
    ]

    def load(g, act):
        cols = pl.ds(g * width, width)

        def for_core(known):
            for i, plane in enumerate(planes):
                step = i % n
                if (i < n) == (known == 0):
                    to = w_ref.at[lax.rem(at_clip + n - step, n), :, 0, :, cols]
                else:
                    to = w_ref.at[:, lax.rem(at_x + n - step, n), 1, :, cols]
                act(pltpu.make_async_copy(plane.at[:, :, cols], to, w_sem.at[g, i]))

        pl.when(core == 0)(lambda: for_core(0))
        pl.when(core == 1)(lambda: for_core(1))

    def start(copy):
        copy.start()

    def finish(copy):
        copy.wait()

    tokens[0].start()
    load(0, start)
    load(1, start)
    tokens[1].start()
    mask = row_key_ref[...] == col_key_ref[...]
    tokens[0].wait()
    feats = token_ref[0].reshape(owners * rows, -1)
    query, keys, values = [], [], []
    for h in range(heads):
        load(h, finish)
        if h + 2 < groups:
            load(h + 2, start)
        w_head = w_ref[:, :, :, :, h * width : (h + 1) * width].reshape(-1, width)
        qkv = dot(feats, w_head).astype(BF)
        for i, parts in enumerate((query, keys, values)):
            parts.append(qkv[:, i * HD : (i + 1) * HD])
    each = range(heads)
    probs = [softmax(query[h], keys[h], mask) for h in each]
    mixed = [dot(probs[h].astype(BF), values[h]).astype(BF) for h in each]
    tokens[1].wait()
    load(heads, finish)
    gated = token_ref[1].reshape(owners * rows, -1)
    w_last = w_ref[:, :, :, :, 3 * width :].reshape(-1, width)
    cotangent = dot(gated, w_last).astype(BF)
    for h in each:
        cols = slice(h * HD, (h + 1) * HD)
        grads = attention_grads(query[h], keys[h], values[h], probs[h], cotangent[:, cols])
        for i in range(3):
            both_ref[:, (3 * h + i) * HD : (3 * h + i + 1) * HD] = grads[i]
        both_ref[:, 3 * width + h * HD : 3 * width + (h + 1) * HD] = mixed[h]
    stores = []
    pair = 2
    for first in range(0, ranks, pair):
        w_part = w_ref[first // pair].reshape(pair * width, -1)
        projected = dot(both_ref[:, 3 * width :], w_part[:, 3 * width :], NT).astype(BF)
        back = dot(both_ref[:, : 3 * width], w_part[:, : 3 * width], NT).astype(BF)
        for i in range(pair):
            z, cols = first + i, slice(i * width, (i + 1) * width)
            for s in range(owners):
                sums_ref[z, s, 0] = projected[s * rows : (s + 1) * rows, cols]
                sums_ref[z, s, 1] = back[s * rows : (s + 1) * rows, cols]
            stores.append(pltpu.make_async_copy(sums_ref.at[z], sums_hbm.at[z], out_sem.at[z]))
            stores[-1].start()
    for copy in stores:
        copy.wait()


def weight_grad_kernel(step, own_ref, pair_ref, both_ref, pair_both_ref, out_ref):
    at_clip, at_x, core = own_chip()
    n, slots, rows, _ = out_ref.shape
    wide = both_ref.shape[1] * 3 // 4
    starts = []
    for r in range(n):
        clip = lax.rem(at_clip + jnp.where(core == 0, r, step), n)
        x = lax.rem(at_x + jnp.where(core == 0, step, r), n)
        starts.append(pl.multiple_of((clip * n + x) * rows, 16))
    for a, cols in ((0, slice(0, wide)), (1, slice(wide, 4 * wide // 3))):
        left = jnp.concatenate(
            [
                jnp.concatenate([ref[a, pl.ds(start, rows), :] for start in starts], axis=0)
                for ref in (own_ref, pair_ref)
            ],
            axis=1,
        )
        right = jnp.concatenate([both_ref[:, cols], pair_both_ref[:, cols]], axis=0)
        total = dot(left, right).astype(BF)
        for r in range(n):
            for s in range(total.shape[1] // HD):
                part = total[r * rows : (r + 1) * rows, s * HD : (s + 1) * HD]
                out_ref[r, a * (slots * 3 // 4) + s] = part


def trade(value, j):
    return lax.ppermute(value, "frame", [(i, i ^ j) for i in range(8)])


def spread(value, step, second):
    pairs = []
    for clip in range(4):
        for x in range(4):
            for core in range(2):
                to_clip, to_x = clip, x
                if (core == 0) != second:
                    to_x = (x + step) % 4
                else:
                    to_clip = (clip + step) % 4
                pairs.append((clip * 8 + x * 2 + core, to_clip * 8 + to_x * 2 + core))
    return lax.ppermute(value, ("clip", "frame"), pairs)


def add(*values):
    return sum(v.astype(F32) for v in values)


def body(spatial_qkv, w_qkv, w_out, out_grad, frame_clip, clip_patches):
    ranks = lax.axis_size("frame")
    width_ranks = lax.axis_size("tensor")
    total_frames = frame_clip.shape[1]
    _, frames, patches, _, width = spatial_qkv.shape
    heads = width // HD
    block = patches // ranks
    rows_t = total_frames * block
    model = width * width_ranks
    slots = 4 * heads
    w_rows = w_qkv.shape[0]
    smem = pl.BlockSpec(memory_space=pltpu.SMEM)
    vmem = pl.BlockSpec(memory_space=pltpu.VMEM)
    hbm = pl.BlockSpec(memory_space=pltpu.HBM)

    qkv = spatial_qkv[0].transpose(0, 2, 1, 3)
    cot = out_grad[0]
    sent = pl.pallas_call(
        spatial_forward,
        out_shape=jax.ShapeDtypeStruct((ranks, 2, frames, block, width), BF),
        in_specs=[smem, smem, vmem, vmem],
        out_specs=vmem,
        scratch_shapes=[pltpu.VMEM((2, frames, patches, width), BF)],
        compiler_params=pltpu.CompilerParams(vmem_limit_bytes=58 * 2**20),
    )(frame_clip, clip_patches, qkv, cot)
    packed = pl.pallas_call(
        pack_kernel,
        out_shape=jax.ShapeDtypeStruct((w_rows, slots * HD), BF),
        in_specs=[vmem, vmem],
        out_specs=vmem,
    )(w_qkv.transpose(1, 2, 0, 3).reshape(3 * heads, w_rows, HD), w_out.transpose(0, 2, 1))
    near = [spread(packed, step, False) for step in (1, 2, 3)]
    cols = lax.all_to_all(sent, "frame", split_axis=0, concat_axis=0, tiled=True)
    cols = cols.reshape(ranks, 2, frames * block, width)
    cols, near[0], near[2] = lax.optimization_barrier([cols, near[0], near[2]])
    whole = lax.all_gather(cols, "tensor", axis=3, tiled=True)
    line = pl.pallas_call(
        line_kernel,
        out_shape=jax.ShapeDtypeStruct((4,) + packed.shape, BF),
        in_specs=[vmem] * 4,
        out_specs=vmem,
    )(packed, *near)
    plane = [line] + [spread(line, step, True) for step in (1, 2, 3)]
    plane += [trade(rows, 1) for rows in plane]

    clips = frame_clip[0][:, None] * block
    keys = (clips + jnp.arange(block, dtype=jnp.int32)[None, :]).reshape(rows_t)

    sums_shape = (width_ranks, ranks, 2, frames * block, width)
    sums, both = pl.pallas_call(
        lambda *refs: temporal_kernel(heads, *refs),
        out_shape=[
            jax.ShapeDtypeStruct(sums_shape, BF),
            jax.ShapeDtypeStruct((rows_t, 4 * width), BF),
        ],
        in_specs=[vmem, vmem] + [hbm] * (1 + len(plane)),
        out_specs=[hbm, vmem],
        scratch_shapes=[
            pltpu.VMEM((4, 4, 2, w_rows, slots * HD), BF),
            pltpu.VMEM((2, ranks, frames * block, model), BF),
            pltpu.VMEM(sums_shape, BF),
            pltpu.SemaphoreType.DMA((heads + 1, len(plane))),
            pltpu.SemaphoreType.DMA((2,)),
            pltpu.SemaphoreType.DMA((width_ranks,)),
        ],
        compiler_params=pltpu.CompilerParams(vmem_limit_bytes=58 * 2**20),
    )(keys[:, None], keys[None, :], whole, *plane)

    halves = jax.ShapeDtypeStruct((2, model // 2, rows_t), BF)
    own_flip, other_flip = pl.pallas_call(
        flip_kernel,
        out_shape=[halves, halves],
        in_specs=[vmem],
        out_specs=[vmem] * 2,
        compiler_params=pltpu.CompilerParams(vmem_limit_bytes=16 * 2**20),
    )(whole)
    pair_flip = trade(other_flip, 1)
    own_sums = lax.psum_scatter(sums, "tensor", scatter_dimension=0, tiled=True)[0]
    pair_both = trade(both, 1)
    parts = {}
    for step in (2, 1, 3, 0):
        parts[step] = pl.pallas_call(
            lambda *refs, step=step: weight_grad_kernel(step, *refs),
            out_shape=jax.ShapeDtypeStruct((4, slots, w_rows, HD), BF),
            in_specs=[vmem] * 4,
            out_specs=vmem,
            compiler_params=pltpu.CompilerParams(vmem_limit_bytes=24 * 2**20),
        )(own_flip, pair_flip, both, pair_both)
    arrived = [parts[0]] + [spread(parts[step], step, False) for step in (2, 1, 3)]
    partial = [add(*(part[i] for part in arrived)).astype(BF) for i in range(4)]
    grads = add(partial[0], *(spread(partial[step], step, True) for step in (2, 1, 3)))

    row_sums = lax.all_to_all(own_sums, "frame", split_axis=0, concat_axis=0, tiled=True)
    block_out, qkv_grad = pl.pallas_call(
        spatial_backward,
        out_shape=[
            jax.ShapeDtypeStruct((frames, patches, width), BF),
            jax.ShapeDtypeStruct((frames, 3, patches, width), BF),
        ],
        in_specs=[smem, smem] + [vmem] * 3,
        out_specs=[vmem, vmem],
        scratch_shapes=[pltpu.VMEM((2, frames, patches, width), BF)],
        compiler_params=pltpu.CompilerParams(vmem_limit_bytes=24 * 2**20),
    )(frame_clip, clip_patches, qkv, cot, row_sums)

    w_qkv_grad = grads[: 3 * heads].reshape(heads, 3, w_rows, HD).transpose(2, 0, 1, 3)
    w_out_grad = grads[3 * heads :].transpose(0, 2, 1)
    return (block_out[None], qkv_grad.transpose(0, 2, 1, 3)[None], w_qkv_grad, w_out_grad)


def solution(mesh):
    in_specs = (
        P("clip", "frame", None, None, "tensor"),
        P(("clip", "frame"), "tensor", None, None),
        P("tensor", None, ("clip", "frame")),
        P("clip", "frame", None, "tensor"),
        P("clip", None),
        P("clip", None),
    )
    out_specs = (
        P("clip", "frame", None, "tensor"),
        P("clip", "frame", None, None, "tensor"),
        P(("clip", "frame"), "tensor", None, None),
        P("tensor", None, ("clip", "frame")),
    )
    return jax.shard_map(body, mesh=mesh, in_specs=in_specs, out_specs=out_specs, check_vma=False)
```

```python
import math

import jax
import jax.numpy as jnp
from jax import lax
from jax.experimental import pallas as pl
from jax.experimental.pallas import tpu as pltpu
from jax.sharding import PartitionSpec as P

HD = 128
SCALE = 1.0 / math.sqrt(HD)
BF = jnp.bfloat16
F32 = jnp.float32
NT = (((1,), (1,)), ((), ()))
TN = (((0,), (0,)), ((), ()))


def dot(a, b, dims=(((1,), (0,)), ((), ()))):
    return lax.dot_general(a, b, dims, preferred_element_type=F32)


def softmax(query, keys, mask):
    scores = jnp.where(mask, dot(query, keys, NT) * SCALE, -1e30)
    expo = jnp.exp(scores - jnp.max(scores, axis=-1, keepdims=True))
    return expo / jnp.sum(expo, axis=-1, keepdims=True)


def attention_grads(query, keys, values, probs, cotangent):
    d_values = dot(probs.astype(BF), cotangent, TN).astype(BF)
    d_probs = dot(cotangent, values, NT).astype(BF).astype(F32)
    inner = jnp.sum(probs * d_probs, axis=-1, keepdims=True)
    d_scores = (probs * (d_probs - inner) * SCALE).astype(BF)
    return dot(d_scores, keys).astype(BF), dot(d_scores, query, TN).astype(BF), d_values


def live_rows(row_ref, patch_ref, frame):
    return patch_ref[0, row_ref[0, frame]]


def spatial_forward(row_ref, patch_ref, qkv_ref, cot_ref, *refs):
    out_ref, whole_ref = refs
    frames, _, patches, width = qkv_ref.shape
    place = lax.axis_index("frame")
    owners = out_ref.shape[0]
    block = patches // owners
    for f in range(frames):
        count = live_rows(row_ref, patch_ref, place * frames + f)
        keys_live = lax.broadcasted_iota(jnp.int32, (patches, patches), 1) < count
        rows_live = lax.broadcasted_iota(jnp.int32, (patches, 1), 0) < count
        pieces = []
        for h in range(width // HD):
            cols = slice(h * HD, (h + 1) * HD)
            probs = softmax(qkv_ref[f, 0, :, cols], qkv_ref[f, 1, :, cols], keys_live)
            mixed = dot(probs.astype(BF), qkv_ref[f, 2, :, cols])
            pieces.append(jnp.where(rows_live, mixed, 0.0).astype(BF))
        whole_ref[0, f] = jnp.concatenate(pieces, axis=1)
        whole_ref[1, f] = jnp.where(rows_live, cot_ref[f].astype(F32), 0.0).astype(BF)
    for s in range(owners):
        out_ref[s] = whole_ref[:, :, s * block : (s + 1) * block, :]


def spatial_backward(row_ref, patch_ref, qkv_ref, cot_ref, *refs):
    sums_ref, out_ref, grad_ref, whole_ref = refs
    frames, _, patches, width = qkv_ref.shape
    place = lax.axis_index("frame")
    owners = sums_ref.shape[0]
    block = patches // owners
    for s in range(owners):
        for f in range(frames):
            part = sums_ref[s, :, f * block : (f + 1) * block, :]
            whole_ref[:, f, s * block : (s + 1) * block, :] = part
    for f in range(frames):
        count = live_rows(row_ref, patch_ref, place * frames + f)
        keys_live = lax.broadcasted_iota(jnp.int32, (patches, patches), 1) < count
        rows_live = lax.broadcasted_iota(jnp.int32, (patches, 1), 0) < count
        d_spatial = cot_ref[f].astype(F32) + whole_ref[1, f].astype(F32)
        d_mixed = jnp.where(rows_live, d_spatial, 0.0).astype(BF)
        for h in range(width // HD):
            cols = slice(h * HD, (h + 1) * HD)
            query, keys, values = (qkv_ref[f, i, :, cols] for i in range(3))
            probs = softmax(query, keys, keys_live)
            mixed = dot(probs.astype(BF), values).astype(BF).astype(F32)
            total = mixed + whole_ref[0, f, :, cols].astype(F32)
            out_ref[f, :, cols] = jnp.where(rows_live, total, 0.0).astype(BF)
            grads = attention_grads(query, keys, values, probs, d_mixed[:, cols])
            for i in range(3):
                grad_ref[f, i, :, cols] = grads[i]


def own_chip():
    place = lax.axis_index("frame")
    return lax.axis_index("clip"), place // 2, place % 2


def assemble_kernel(ranks, *refs):
    blocks, refs = refs[: 2 * ranks], refs[2 * ranks :]
    feat_ref, gated_ref, own_ref, other_ref, flip_ref, sem = refs
    me, core = lax.axis_index("tensor"), own_chip()[2]
    width = feat_ref.shape[1] // ranks
    copies = []
    for a, whole in enumerate((feat_ref, gated_ref)):
        for d in range(ranks):
            start = pl.multiple_of(lax.rem(me + d, ranks) * width, HD)
            i = a * ranks + d
            copies.append(
                pltpu.make_async_copy(blocks[i], whole.at[:, pl.ds(start, width)], sem.at[i])
            )
    for copy in copies:
        copy.start()
    for copy in copies:
        copy.wait()
    pieces = 32
    rows = feat_ref.shape[1] // pieces
    for a, whole in enumerate((feat_ref, gated_ref)):
        for z in range(ranks):
            part = slice(z * width, (z + 1) * width)
            flip_ref[part, :] = whole[:, part].T
        for i in range(pieces // 2):
            to = slice(i * rows, (i + 1) * rows)
            own_ref[a, to] = flip_ref[pl.ds(pl.multiple_of((2 * i + core) * rows, 16), rows), :]
            other_ref[a, to] = flip_ref[pl.ds(pl.multiple_of((2 * i + 1 - core) * rows, 16), rows), :]


def temporal_kernel(heads, row_key_ref, col_key_ref, feat_hbm, gated_hbm, _, w_hbm, *refs):
    sums_hbm, both_ref, feat_ref, gated_ref, w_ref, sums_ref, in_sem, w_sem, out_sem = refs
    width = heads * HD
    slots = 4 * heads
    ranks, owners, _, rows, _ = sums_ref.shape
    loads = [
        pltpu.make_async_copy(w_hbm.at[i], w_ref.at[:, i * HD : (i + 1) * HD], w_sem.at[i])
        for i in range(slots)
    ]
    feat_load = pltpu.make_async_copy(feat_hbm, feat_ref, in_sem.at[0])
    gated_load = pltpu.make_async_copy(gated_hbm, gated_ref, in_sem.at[1])
    feat_load.start()
    for copy in loads[:6]:
        copy.start()
    mask = row_key_ref[...] == col_key_ref[...]
    feat_load.wait()
    query, keys, values = [], [], []
    for h in range(heads):
        for copy in loads[3 * h : 3 * h + 3]:
            copy.wait()
        if h == 0:
            gated_load.start()
        for copy in loads[3 * h + 6 : 3 * h + 9]:
            copy.start()
        qkv = dot(feat_ref[...], w_ref[:, h * width : (h + 1) * width]).astype(BF)
        for i, parts in enumerate((query, keys, values)):
            parts.append(qkv[:, i * HD : (i + 1) * HD])
    each = range(heads)
    probs = [softmax(query[h], keys[h], mask) for h in each]
    mixed = [dot(probs[h].astype(BF), values[h]).astype(BF) for h in each]
    gated_load.wait()
    for copy in loads[9:]:
        copy.wait()
    cotangent = dot(gated_ref[...], w_ref[:, 3 * width :]).astype(BF)
    for h in each:
        cols = slice(h * HD, (h + 1) * HD)
        grads = attention_grads(query[h], keys[h], values[h], probs[h], cotangent[:, cols])
        for i in range(3):
            both_ref[:, (3 * h + i) * HD : (3 * h + i + 1) * HD] = grads[i]
        both_ref[:, 3 * width + h * HD : 3 * width + (h + 1) * HD] = mixed[h]
    stores = []
    pair = 4
    for first in range(0, ranks, pair):
        w_part = w_ref.at[first * width : (first + pair) * width]
        projected = dot(both_ref[:, 3 * width :], w_part[:, 3 * width :], NT).astype(BF)
        back = dot(both_ref[:, : 3 * width], w_part[:, : 3 * width], NT).astype(BF)
        for i in range(pair):
            z, cols = first + i, slice(i * width, (i + 1) * width)
            for s in range(owners):
                sums_ref[z, s, 0] = projected[s * rows : (s + 1) * rows, cols]
                sums_ref[z, s, 1] = back[s * rows : (s + 1) * rows, cols]
            stores.append(pltpu.make_async_copy(sums_ref.at[z], sums_hbm.at[z], out_sem.at[z]))
            stores[-1].start()
    for copy in stores:
        copy.wait()


def weight_grad_kernel(step, own_ref, pair_ref, both_ref, pair_both_ref, out_ref):
    at_clip, at_x, core = own_chip()
    n, slots, rows, _ = out_ref.shape
    wide = both_ref.shape[1] * 3 // 4
    starts = []
    for r in range(n):
        clip = lax.rem(at_clip + jnp.where(core == 0, r, step), n)
        x = lax.rem(at_x + jnp.where(core == 0, step, r), n)
        starts.append(pl.multiple_of((clip * n + x) * rows, 16))
    for a, cols in ((0, slice(0, wide)), (1, slice(wide, 4 * wide // 3))):
        left = jnp.concatenate(
            [
                jnp.concatenate([ref[a, pl.ds(start, rows), :] for start in starts], axis=0)
                for ref in (own_ref, pair_ref)
            ],
            axis=1,
        )
        right = jnp.concatenate([both_ref[:, cols], pair_both_ref[:, cols]], axis=0)
        total = dot(left, right).astype(BF)
        for r in range(n):
            for s in range(total.shape[1] // HD):
                part = total[r * rows : (r + 1) * rows, s * HD : (s + 1) * HD]
                out_ref[r, a * (slots * 3 // 4) + s] = part


def shift(value, axis, step, size):
    return lax.ppermute(value, axis, [(i, (i + step) % size) for i in range(size)])


def pair_swap(value):
    return lax.ppermute(value, "frame", [(i, i ^ 1) for i in range(8)])


def spread(value, step, second):
    pairs = []
    for clip in range(4):
        for x in range(4):
            for core in range(2):
                to_clip, to_x = clip, x
                if (core == 0) != second:
                    to_x = (x + step) % 4
                else:
                    to_clip = (clip + step) % 4
                pairs.append((clip * 8 + x * 2 + core, to_clip * 8 + to_x * 2 + core))
    return lax.ppermute(value, ("clip", "frame"), pairs)


def ring_gather(value, axis, size, last_forward):
    found = {0: value}
    up = down = value
    for step in range(1, size // 2):
        up = shift(up, axis, 1, size)
        down = shift(down, axis, -1, size)
        found[size - step], found[step] = up, down
    found[size // 2] = shift(up, axis, 1, size) if last_forward else shift(down, axis, -1, size)
    return [found[d] for d in range(size)]


def add(*values):
    return sum(v.astype(F32) for v in values)


def body(spatial_qkv, w_qkv, w_out, out_grad, frame_clip, clip_patches):
    ranks = lax.axis_size("frame")
    width_ranks = lax.axis_size("tensor")
    total_frames = frame_clip.shape[1]
    _, frames, patches, _, width = spatial_qkv.shape
    heads = width // HD
    block = patches // ranks
    rows_t = total_frames * block
    model = width * width_ranks
    slots = 4 * heads

    w_rows = w_qkv.shape[0]
    w_own = jnp.concatenate(
        [w_qkv.transpose(1, 2, 0, 3).reshape(3 * heads, w_rows, HD), w_out.transpose(0, 2, 1)],
        axis=0,
    )
    w_all = lax.all_gather(w_own, ("clip", "frame"), axis=1, tiled=True)

    clips = frame_clip[0][:, None] * block
    keys = (clips + jnp.arange(block, dtype=jnp.int32)[None, :]).reshape(rows_t)

    qkv = spatial_qkv[0].transpose(0, 2, 1, 3)
    cot = out_grad[0]
    smem = pl.BlockSpec(memory_space=pltpu.SMEM)
    vmem = pl.BlockSpec(memory_space=pltpu.VMEM)
    hbm = pl.BlockSpec(memory_space=pltpu.HBM)
    sent = pl.pallas_call(
        spatial_forward,
        out_shape=jax.ShapeDtypeStruct((ranks, 2, frames, block, width), BF),
        in_specs=[smem, smem, vmem, vmem],
        out_specs=vmem,
        scratch_shapes=[pltpu.VMEM((2, frames, patches, width), BF)],
        compiler_params=pltpu.CompilerParams(vmem_limit_bytes=58 * 2**20),
    )(frame_clip, clip_patches, qkv, cot)
    cols = lax.all_to_all(sent, "frame", split_axis=0, concat_axis=0, tiled=True)
    blocks = []
    for a in range(2):
        rows = cols[:, a].reshape(rows_t, width)
        blocks += ring_gather(rows, "tensor", width_ranks, a == 0)

    halves = jax.ShapeDtypeStruct((2, model // 2, rows_t), BF)
    wide = jax.ShapeDtypeStruct((rows_t, model), BF)
    feats, gated, own_flip, other_flip = pl.pallas_call(
        lambda *refs: assemble_kernel(width_ranks, *refs),
        out_shape=[wide, wide, halves, halves],
        in_specs=[hbm] * (2 * width_ranks),
        out_specs=[vmem] * 4,
        scratch_shapes=[
            pltpu.VMEM((model, rows_t), BF),
            pltpu.SemaphoreType.DMA((2 * width_ranks,)),
        ],
        compiler_params=pltpu.CompilerParams(vmem_limit_bytes=58 * 2**20),
    )(*blocks)
    pair_flip = pair_swap(other_flip)

    wide_scratch = pltpu.VMEM((rows_t, model), BF)
    sums_shape = (width_ranks, ranks, 2, frames * block, width)
    sums, both = pl.pallas_call(
        lambda *refs: temporal_kernel(heads, *refs),
        out_shape=[
            jax.ShapeDtypeStruct(sums_shape, BF),
            jax.ShapeDtypeStruct((rows_t, 4 * width), BF),
        ],
        in_specs=[vmem] * 2 + [hbm] * 4,
        out_specs=[hbm, vmem],
        scratch_shapes=[
            wide_scratch,
            wide_scratch,
            pltpu.VMEM((model, 4 * width), BF),
            pltpu.VMEM(sums_shape, BF),
            pltpu.SemaphoreType.DMA((2,)),
            pltpu.SemaphoreType.DMA((slots,)),
            pltpu.SemaphoreType.DMA((width_ranks,)),
        ],
        compiler_params=pltpu.CompilerParams(vmem_limit_bytes=56 * 2**20),
    )(keys[:, None], keys[None, :], feats, gated, pair_flip, w_all)

    own_sums = lax.psum_scatter(sums, "tensor", scatter_dimension=0, tiled=True)[0]
    pair_both = pair_swap(both)
    parts = {}
    for step in (2, 1, 3, 0):
        parts[step] = pl.pallas_call(
            lambda *refs, step=step: weight_grad_kernel(step, *refs),
            out_shape=jax.ShapeDtypeStruct((4, slots, w_rows, HD), BF),
            in_specs=[vmem] * 4,
            out_specs=vmem,
            compiler_params=pltpu.CompilerParams(vmem_limit_bytes=24 * 2**20),
        )(own_flip, pair_flip, both, pair_both)
    arrived = [parts[0]] + [spread(parts[step], step, False) for step in (2, 1, 3)]
    partial = [add(*(part[i] for part in arrived)).astype(BF) for i in range(4)]
    grads = add(partial[0], *(spread(partial[step], step, True) for step in (2, 1, 3)))

    row_sums = lax.all_to_all(own_sums, "frame", split_axis=0, concat_axis=0, tiled=True)
    block_out, qkv_grad = pl.pallas_call(
        spatial_backward,
        out_shape=[
            jax.ShapeDtypeStruct((frames, patches, width), BF),
            jax.ShapeDtypeStruct((frames, 3, patches, width), BF),
        ],
        in_specs=[smem, smem] + [vmem] * 3,
        out_specs=[vmem, vmem],
        scratch_shapes=[pltpu.VMEM((2, frames, patches, width), BF)],
        compiler_params=pltpu.CompilerParams(vmem_limit_bytes=24 * 2**20),
    )(frame_clip, clip_patches, qkv, cot, row_sums)

    w_qkv_grad = grads[: 3 * heads].reshape(heads, 3, w_rows, HD).transpose(2, 0, 1, 3)
    w_out_grad = grads[3 * heads :].transpose(0, 2, 1)
    return (block_out[None], qkv_grad.transpose(0, 2, 1, 3)[None], w_qkv_grad, w_out_grad)


def solution(mesh):
    in_specs = (
        P("clip", "frame", None, None, "tensor"),
        P(("clip", "frame"), "tensor", None, None),
        P("tensor", None, ("clip", "frame")),
        P("clip", "frame", None, "tensor"),
        P("clip", None),
        P("clip", None),
    )
    out_specs = (
        P("clip", "frame", None, "tensor"),
        P("clip", "frame", None, None, "tensor"),
        P(("clip", "frame"), "tensor", None, None),
        P("tensor", None, ("clip", "frame")),
    )
    return jax.shard_map(body, mesh=mesh, in_specs=in_specs, out_specs=out_specs, check_vma=False)
```

```python
import math

import jax
import jax.numpy as jnp
from jax import lax
from jax.experimental import pallas as pl
from jax.experimental.pallas import tpu as pltpu
from jax.sharding import PartitionSpec as P

HD = 128
SCALE = 1.0 / math.sqrt(HD)
BF = jnp.bfloat16
F32 = jnp.float32
NT = (((1,), (1,)), ((), ()))
TN = (((0,), (0,)), ((), ()))


def dot(a, b, dims=(((1,), (0,)), ((), ()))):
    return lax.dot_general(a, b, dims, preferred_element_type=F32)


def softmax(query, keys, mask):
    scores = jnp.where(mask, dot(query, keys, NT) * SCALE, -1e30)
    expo = jnp.exp(scores - jnp.max(scores, axis=-1, keepdims=True))
    return expo / jnp.sum(expo, axis=-1, keepdims=True)


def attention_grads(query, keys, values, probs, cotangent):
    d_values = dot(probs.astype(BF), cotangent, TN).astype(BF)
    d_probs = dot(cotangent, values, NT).astype(BF).astype(F32)
    inner = jnp.sum(probs * d_probs, axis=-1, keepdims=True)
    d_scores = (probs * (d_probs - inner) * SCALE).astype(BF)
    return dot(d_scores, keys).astype(BF), dot(d_scores, query, TN).astype(BF), d_values


def live_rows(row_ref, patch_ref, frame):
    return patch_ref[0, row_ref[0, frame]]


def spatial_forward(row_ref, patch_ref, qkv_ref, cot_ref, *refs):
    out_ref, whole_ref = refs
    frames, _, patches, width = qkv_ref.shape
    place = lax.axis_index("frame")
    owners = out_ref.shape[0]
    block = patches // owners
    for f in range(frames):
        count = live_rows(row_ref, patch_ref, place * frames + f)
        keys_live = lax.broadcasted_iota(jnp.int32, (patches, patches), 1) < count
        rows_live = lax.broadcasted_iota(jnp.int32, (patches, 1), 0) < count
        pieces = []
        for h in range(width // HD):
            cols = slice(h * HD, (h + 1) * HD)
            probs = softmax(qkv_ref[f, 0, :, cols], qkv_ref[f, 1, :, cols], keys_live)
            mixed = dot(probs.astype(BF), qkv_ref[f, 2, :, cols])
            pieces.append(jnp.where(rows_live, mixed, 0.0).astype(BF))
        whole_ref[0, f] = jnp.concatenate(pieces, axis=1)
        whole_ref[1, f] = jnp.where(rows_live, cot_ref[f].astype(F32), 0.0).astype(BF)
    for s in range(owners):
        out_ref[s] = whole_ref[:, :, s * block : (s + 1) * block, :]


def spatial_backward(row_ref, patch_ref, qkv_ref, cot_ref, *refs):
    sums_ref, out_ref, grad_ref, whole_ref = refs
    frames, _, patches, width = qkv_ref.shape
    place = lax.axis_index("frame")
    owners = sums_ref.shape[0]
    block = patches // owners
    for s in range(owners):
        for f in range(frames):
            part = sums_ref[s, :, f * block : (f + 1) * block, :]
            whole_ref[:, f, s * block : (s + 1) * block, :] = part
    for f in range(frames):
        count = live_rows(row_ref, patch_ref, place * frames + f)
        keys_live = lax.broadcasted_iota(jnp.int32, (patches, patches), 1) < count
        rows_live = lax.broadcasted_iota(jnp.int32, (patches, 1), 0) < count
        d_spatial = cot_ref[f].astype(F32) + whole_ref[1, f].astype(F32)
        d_mixed = jnp.where(rows_live, d_spatial, 0.0).astype(BF)
        for h in range(width // HD):
            cols = slice(h * HD, (h + 1) * HD)
            query, keys, values = (qkv_ref[f, i, :, cols] for i in range(3))
            probs = softmax(query, keys, keys_live)
            mixed = dot(probs.astype(BF), values).astype(BF).astype(F32)
            total = mixed + whole_ref[0, f, :, cols].astype(F32)
            out_ref[f, :, cols] = jnp.where(rows_live, total, 0.0).astype(BF)
            grads = attention_grads(query, keys, values, probs, d_mixed[:, cols])
            for i in range(3):
                grad_ref[f, i, :, cols] = grads[i]


def own_chip():
    place = lax.axis_index("frame")
    return lax.axis_index("clip"), place // 2, place % 2


def assemble_kernel(ranks, *refs):
    blocks, refs = refs[: 2 * ranks], refs[2 * ranks :]
    feat_ref, gated_ref, own_ref, other_ref, flip_ref, sem = refs
    me, core = lax.axis_index("tensor"), own_chip()[2]
    width = feat_ref.shape[1] // ranks
    copies = []
    for a, whole in enumerate((feat_ref, gated_ref)):
        for d in range(ranks):
            start = pl.multiple_of(lax.rem(me + d, ranks) * width, HD)
            i = a * ranks + d
            copies.append(
                pltpu.make_async_copy(blocks[i], whole.at[:, pl.ds(start, width)], sem.at[i])
            )
    for copy in copies:
        copy.start()
    for copy in copies:
        copy.wait()
    pieces = 32
    rows = feat_ref.shape[1] // pieces
    for a, whole in enumerate((feat_ref, gated_ref)):
        for z in range(ranks):
            part = slice(z * width, (z + 1) * width)
            flip_ref[part, :] = whole[:, part].T
        for i in range(pieces // 2):
            to = slice(i * rows, (i + 1) * rows)
            own_ref[a, to] = flip_ref[pl.ds(pl.multiple_of((2 * i + core) * rows, 16), rows), :]
            other_ref[a, to] = flip_ref[pl.ds(pl.multiple_of((2 * i + 1 - core) * rows, 16), rows), :]


def row_keys(clip_ref, rows, axis):
    frames = clip_ref.shape[1]
    block = rows // frames
    index = lax.broadcasted_iota(jnp.int32, (rows, 1) if axis == 0 else (1, rows), axis)
    keys = index
    for f in range(frames):
        inside = (index >= f * block) & (index < (f + 1) * block)
        keys = jnp.where(inside, index + (clip_ref[0, f] - f) * block, keys)
    return keys


def temporal_kernel(heads, clip_ref, feat_hbm, gated_hbm, _, w_hbm, *refs):
    sums_hbm, both_ref, feat_ref, gated_ref, w_ref, sums_ref, in_sem, w_sem, out_sem = refs
    width = heads * HD
    slots = 4 * heads
    ranks, owners, rows, _ = sums_ref.shape
    loads = [
        pltpu.make_async_copy(w_hbm.at[i], w_ref.at[:, i * HD : (i + 1) * HD], w_sem.at[i])
        for i in range(slots)
    ]
    feat_load = pltpu.make_async_copy(feat_hbm, feat_ref, in_sem.at[0])
    gated_load = pltpu.make_async_copy(gated_hbm, gated_ref, in_sem.at[1])
    feat_load.start()
    for copy in loads[:6]:
        copy.start()
    mask = row_keys(clip_ref, owners * rows, 0) == row_keys(clip_ref, owners * rows, 1)
    feat_load.wait()
    query, keys, values = [], [], []
    for h in range(heads):
        for copy in loads[3 * h : 3 * h + 3]:
            copy.wait()
        if h == 0:
            gated_load.start()
        for copy in loads[3 * h + 6 : 3 * h + 9]:
            copy.start()
        qkv = dot(feat_ref[...], w_ref[:, h * width : (h + 1) * width]).astype(BF)
        for i, parts in enumerate((query, keys, values)):
            parts.append(qkv[:, i * HD : (i + 1) * HD])
    each = range(heads)
    probs = [softmax(query[h], keys[h], mask) for h in each]
    mixed = [dot(probs[h].astype(BF), values[h]).astype(BF) for h in each]
    gated_load.wait()
    for copy in loads[9:]:
        copy.wait()
    cotangent = dot(gated_ref[...], w_ref[:, 3 * width :]).astype(BF)
    for h in each:
        cols = slice(h * HD, (h + 1) * HD)
        grads = attention_grads(query[h], keys[h], values[h], probs[h], cotangent[:, cols])
        for i in range(3):
            both_ref[:, (3 * h + i) * HD : (3 * h + i + 1) * HD] = grads[i]
        both_ref[:, 3 * width + h * HD : 3 * width + (h + 1) * HD] = mixed[h]
    stores = []
    pair = 4
    for first in range(0, ranks, pair):
        w_part = w_ref.at[first * width : (first + pair) * width]
        back = dot(both_ref[:, : 3 * width], w_part[:, : 3 * width], NT).astype(BF)
        for i in range(pair):
            z, cols = first + i, slice(i * width, (i + 1) * width)
            for s in range(owners):
                sums_ref[z, s] = back[s * rows : (s + 1) * rows, cols]
            stores.append(pltpu.make_async_copy(sums_ref.at[z], sums_hbm.at[z], out_sem.at[z]))
            stores[-1].start()
    for copy in stores:
        copy.wait()


def project_kernel(both_ref, w_hbm, *refs):
    outs, (w_ref, sem) = refs[:-2], refs[-2:]
    heads = w_ref.shape[1] // HD
    width = heads * HD
    loads = [
        pltpu.make_async_copy(
            w_hbm.at[3 * heads + h], w_ref.at[:, h * HD : (h + 1) * HD], sem.at[h]
        )
        for h in range(heads)
    ]
    for copy in loads:
        copy.start()
    for copy in loads:
        copy.wait()
    mixed = both_ref[:, 3 * width :]
    for d, out_ref in enumerate(outs):
        z = lax.rem(lax.axis_index("tensor") + d, len(outs))
        w_part = w_ref[pl.ds(pl.multiple_of(z * width, 16), width), :]
        out_ref[...] = dot(mixed, w_part, NT).astype(BF).reshape(out_ref.shape)


def weight_grad_kernel(step, own_ref, pair_ref, both_ref, pair_both_ref, out_ref):
    at_clip, at_x, core = own_chip()
    n, slots, rows, _ = out_ref.shape
    wide = both_ref.shape[1] * 3 // 4
    starts = []
    for r in range(n):
        clip = lax.rem(at_clip + jnp.where(core == 0, r, step), n)
        x = lax.rem(at_x + jnp.where(core == 0, step, r), n)
        starts.append(pl.multiple_of((clip * n + x) * rows, 16))
    for a, cols in ((0, slice(0, wide)), (1, slice(wide, 4 * wide // 3))):
        left = jnp.concatenate(
            [
                jnp.concatenate([ref[a, pl.ds(start, rows), :] for start in starts], axis=0)
                for ref in (own_ref, pair_ref)
            ],
            axis=1,
        )
        right = jnp.concatenate([both_ref[:, cols], pair_both_ref[:, cols]], axis=0)
        total = dot(left, right).astype(BF)
        for r in range(n):
            for s in range(total.shape[1] // HD):
                part = total[r * rows : (r + 1) * rows, s * HD : (s + 1) * HD]
                out_ref[r, a * (slots * 3 // 4) + s] = part


def shift(value, axis, step, size):
    return lax.ppermute(value, axis, [(i, (i + step) % size) for i in range(size)])


def pair_swap(value):
    return lax.ppermute(value, "frame", [(i, i ^ 1) for i in range(8)])


def spread(value, step, second):
    pairs = []
    for clip in range(4):
        for x in range(4):
            for core in range(2):
                to_clip, to_x = clip, x
                if (core == 0) != second:
                    to_x = (x + step) % 4
                else:
                    to_clip = (clip + step) % 4
                pairs.append((clip * 8 + x * 2 + core, to_clip * 8 + to_x * 2 + core))
    return lax.ppermute(value, ("clip", "frame"), pairs)


def ring_gather(value, axis, size, last_forward):
    found = {0: value}
    up = down = value
    for step in range(1, size // 2):
        up = shift(up, axis, 1, size)
        down = shift(down, axis, -1, size)
        found[size - step], found[step] = up, down
    found[size // 2] = shift(up, axis, 1, size) if last_forward else shift(down, axis, -1, size)
    return [found[d] for d in range(size)]


def ring_sum(parts, axis):
    size = len(parts)
    up, down = parts[size // 2], parts[size // 2 + 1]
    for d in range(size // 2 - 1, 0, -1):
        up = add(shift(up, axis, 1, size), parts[d]).astype(BF)
    for d in range(size // 2 + 2, size):
        down = add(shift(down, axis, -1, size), parts[d]).astype(BF)
    return add(parts[0], shift(up, axis, 1, size), shift(down, axis, -1, size)).astype(BF)


def add(*values):
    return sum(v.astype(F32) for v in values)


def body(spatial_qkv, w_qkv, w_out, out_grad, frame_clip, clip_patches):
    ranks = lax.axis_size("frame")
    width_ranks = lax.axis_size("tensor")
    total_frames = frame_clip.shape[1]
    _, frames, patches, _, width = spatial_qkv.shape
    heads = width // HD
    block = patches // ranks
    rows_t = total_frames * block
    model = width * width_ranks
    slots = 4 * heads

    w_rows = w_qkv.shape[0]
    w_own = jnp.concatenate(
        [w_qkv.transpose(1, 2, 0, 3).reshape(3 * heads, w_rows, HD), w_out.transpose(0, 2, 1)],
        axis=0,
    )
    w_all = lax.all_gather(w_own, ("clip", "frame"), axis=1, tiled=True)

    qkv = spatial_qkv[0].transpose(0, 2, 1, 3)
    cot = out_grad[0]
    smem = pl.BlockSpec(memory_space=pltpu.SMEM)
    vmem = pl.BlockSpec(memory_space=pltpu.VMEM)
    hbm = pl.BlockSpec(memory_space=pltpu.HBM)
    sent = pl.pallas_call(
        spatial_forward,
        out_shape=jax.ShapeDtypeStruct((ranks, 2, frames, block, width), BF),
        in_specs=[smem, smem, vmem, vmem],
        out_specs=vmem,
        scratch_shapes=[pltpu.VMEM((2, frames, patches, width), BF)],
        compiler_params=pltpu.CompilerParams(vmem_limit_bytes=58 * 2**20),
    )(frame_clip, clip_patches, qkv, cot)
    cols = lax.all_to_all(sent, "frame", split_axis=0, concat_axis=0, tiled=True)
    blocks = []
    for a in range(2):
        rows = cols[:, a].reshape(rows_t, width)
        blocks += ring_gather(rows, "tensor", width_ranks, a == 0)

    halves = jax.ShapeDtypeStruct((2, model // 2, rows_t), BF)
    wide = jax.ShapeDtypeStruct((rows_t, model), BF)
    feats, gated, own_flip, other_flip = pl.pallas_call(
        lambda *refs: assemble_kernel(width_ranks, *refs),
        out_shape=[wide, wide, halves, halves],
        in_specs=[hbm] * (2 * width_ranks),
        out_specs=[vmem] * 4,
        scratch_shapes=[
            pltpu.VMEM((model, rows_t), BF),
            pltpu.SemaphoreType.DMA((2 * width_ranks,)),
        ],
        compiler_params=pltpu.CompilerParams(vmem_limit_bytes=58 * 2**20),
    )(*blocks)
    pair_flip = pair_swap(other_flip)

    wide_scratch = pltpu.VMEM((rows_t, model), BF)
    sums_shape = (width_ranks, ranks, frames * block, width)
    sums, both = pl.pallas_call(
        lambda *refs: temporal_kernel(heads, *refs),
        out_shape=[
            jax.ShapeDtypeStruct(sums_shape, BF),
            jax.ShapeDtypeStruct((rows_t, 4 * width), BF),
        ],
        in_specs=[smem] + [hbm] * 4,
        out_specs=[hbm, vmem],
        scratch_shapes=[
            wide_scratch,
            wide_scratch,
            pltpu.VMEM((model, 4 * width), BF),
            pltpu.VMEM(sums_shape, BF),
            pltpu.SemaphoreType.DMA((2,)),
            pltpu.SemaphoreType.DMA((slots,)),
            pltpu.SemaphoreType.DMA((width_ranks,)),
        ],
        compiler_params=pltpu.CompilerParams(vmem_limit_bytes=56 * 2**20),
    )(frame_clip, feats, gated, pair_flip, w_all)

    own_back = lax.psum_scatter(sums, "tensor", scatter_dimension=0, tiled=True)[0]
    projected = pl.pallas_call(
        project_kernel,
        out_shape=[jax.ShapeDtypeStruct(sums_shape[1:], BF)] * width_ranks,
        in_specs=[vmem, hbm],
        out_specs=[vmem] * width_ranks,
        scratch_shapes=[pltpu.VMEM((model, width), BF), pltpu.SemaphoreType.DMA((heads,))],
        compiler_params=pltpu.CompilerParams(vmem_limit_bytes=52 * 2**20),
    )(both, w_all)
    own_sums = jnp.stack([ring_sum(projected, "tensor"), own_back], axis=1)
    pair_both = pair_swap(both)
    parts = {}
    for step in (2, 1, 3, 0):
        parts[step] = pl.pallas_call(
            lambda *refs, step=step: weight_grad_kernel(step, *refs),
            out_shape=jax.ShapeDtypeStruct((4, slots, w_rows, HD), BF),
            in_specs=[vmem] * 4,
            out_specs=vmem,
            compiler_params=pltpu.CompilerParams(vmem_limit_bytes=24 * 2**20),
        )(own_flip, pair_flip, both, pair_both)
    arrived = [parts[0]] + [spread(parts[step], step, False) for step in (2, 1, 3)]
    partial = [add(*(part[i] for part in arrived)).astype(BF) for i in range(4)]
    grads = add(partial[0], *(spread(partial[step], step, True) for step in (2, 1, 3)))

    row_sums = lax.all_to_all(own_sums, "frame", split_axis=0, concat_axis=0, tiled=True)
    block_out, qkv_grad = pl.pallas_call(
        spatial_backward,
        out_shape=[
            jax.ShapeDtypeStruct((frames, patches, width), BF),
            jax.ShapeDtypeStruct((frames, 3, patches, width), BF),
        ],
        in_specs=[smem, smem] + [vmem] * 3,
        out_specs=[vmem, vmem],
        scratch_shapes=[pltpu.VMEM((2, frames, patches, width), BF)],
        compiler_params=pltpu.CompilerParams(vmem_limit_bytes=24 * 2**20),
    )(frame_clip, clip_patches, qkv, cot, row_sums)

    w_qkv_grad = grads[: 3 * heads].reshape(heads, 3, w_rows, HD).transpose(2, 0, 1, 3)
    w_out_grad = grads[3 * heads :].transpose(0, 2, 1)
    return (block_out[None], qkv_grad.transpose(0, 2, 1, 3)[None], w_qkv_grad, w_out_grad)


def solution(mesh):
    in_specs = (
        P("clip", "frame", None, None, "tensor"),
        P(("clip", "frame"), "tensor", None, None),
        P("tensor", None, ("clip", "frame")),
        P("clip", "frame", None, "tensor"),
        P("clip", None),
        P("clip", None),
    )
    out_specs = (
        P("clip", "frame", None, "tensor"),
        P("clip", "frame", None, None, "tensor"),
        P(("clip", "frame"), "tensor", None, None),
        P("tensor", None, ("clip", "frame")),
    )
    return jax.shard_map(body, mesh=mesh, in_specs=in_specs, out_specs=out_specs, check_vma=False)
```

```python
import math

import jax
import jax.numpy as jnp
from jax import lax
from jax.experimental import pallas as pl
from jax.experimental.pallas import tpu as pltpu
from jax.sharding import PartitionSpec as P

HD = 128
SCALE = 1.0 / math.sqrt(HD)
BF = jnp.bfloat16
F32 = jnp.float32
NT = (((1,), (1,)), ((), ()))
TN = (((0,), (0,)), ((), ()))


def dot(a, b, dims=(((1,), (0,)), ((), ()))):
    return lax.dot_general(a, b, dims, preferred_element_type=F32)


def softmax(query, keys, mask):
    scores = jnp.where(mask, dot(query, keys, NT) * SCALE, -1e30)
    expo = jnp.exp(scores - jnp.max(scores, axis=-1, keepdims=True))
    return expo / jnp.sum(expo, axis=-1, keepdims=True)


def attention_grads(query, keys, values, probs, cotangent):
    d_values = dot(probs.astype(BF), cotangent, TN).astype(BF)
    d_probs = dot(cotangent, values, NT).astype(BF).astype(F32)
    inner = jnp.sum(probs * d_probs, axis=-1, keepdims=True)
    d_scores = (probs * (d_probs - inner) * SCALE).astype(BF)
    return dot(d_scores, keys).astype(BF), dot(d_scores, query, TN).astype(BF), d_values


def live_rows(row_ref, patch_ref, frame):
    return patch_ref[0, row_ref[0, frame]]


def spatial_forward(row_ref, patch_ref, qkv_ref, cot_ref, *refs):
    out_ref, whole_ref = refs
    frames, _, patches, width = qkv_ref.shape
    place = lax.axis_index("frame")
    owners = out_ref.shape[0]
    block = patches // owners
    for f in range(frames):
        count = live_rows(row_ref, patch_ref, place * frames + f)
        keys_live = lax.broadcasted_iota(jnp.int32, (patches, patches), 1) < count
        rows_live = lax.broadcasted_iota(jnp.int32, (patches, 1), 0) < count
        pieces = []
        for h in range(width // HD):
            cols = slice(h * HD, (h + 1) * HD)
            probs = softmax(qkv_ref[f, 0, :, cols], qkv_ref[f, 1, :, cols], keys_live)
            mixed = dot(probs.astype(BF), qkv_ref[f, 2, :, cols])
            pieces.append(jnp.where(rows_live, mixed, 0.0).astype(BF))
        whole_ref[0, f] = jnp.concatenate(pieces, axis=1)
        whole_ref[1, f] = jnp.where(rows_live, cot_ref[f].astype(F32), 0.0).astype(BF)
    for s in range(owners):
        out_ref[s] = whole_ref[:, :, s * block : (s + 1) * block, :]


def spatial_backward(row_ref, patch_ref, qkv_ref, cot_ref, *refs):
    sums_ref, out_ref, grad_ref, whole_ref = refs
    frames, _, patches, width = qkv_ref.shape
    place = lax.axis_index("frame")
    owners = sums_ref.shape[0]
    block = patches // owners
    for s in range(owners):
        for f in range(frames):
            part = sums_ref[s, :, f * block : (f + 1) * block, :]
            whole_ref[:, f, s * block : (s + 1) * block, :] = part
    for f in range(frames):
        count = live_rows(row_ref, patch_ref, place * frames + f)
        keys_live = lax.broadcasted_iota(jnp.int32, (patches, patches), 1) < count
        rows_live = lax.broadcasted_iota(jnp.int32, (patches, 1), 0) < count
        d_spatial = cot_ref[f].astype(F32) + whole_ref[1, f].astype(F32)
        d_mixed = jnp.where(rows_live, d_spatial, 0.0).astype(BF)
        for h in range(width // HD):
            cols = slice(h * HD, (h + 1) * HD)
            query, keys, values = (qkv_ref[f, i, :, cols] for i in range(3))
            probs = softmax(query, keys, keys_live)
            mixed = dot(probs.astype(BF), values).astype(BF).astype(F32)
            total = mixed + whole_ref[0, f, :, cols].astype(F32)
            out_ref[f, :, cols] = jnp.where(rows_live, total, 0.0).astype(BF)
            grads = attention_grads(query, keys, values, probs, d_mixed[:, cols])
            for i in range(3):
                grad_ref[f, i, :, cols] = grads[i]


def pack_kernel(qkv_ref, out_ref, packed_ref):
    for ref, first in ((qkv_ref, 0), (out_ref, qkv_ref.shape[0])):
        for s in range(ref.shape[0]):
            packed_ref[:, (first + s) * HD : (first + s + 1) * HD] = ref[s]


def own_chip():
    place = lax.axis_index("frame")
    return lax.axis_index("clip"), place // 2, place % 2


def line_kernel(own_ref, near_1, near_2, near_3, line_ref):
    at_clip, at_x, core = own_chip()
    at = jnp.where(core == 0, at_x, at_clip)
    for step, ref in enumerate((own_ref, near_1, near_2, near_3)):
        line_ref[lax.rem(at + 4 - step, 4)] = ref[...]


def flip_kernel(*refs):
    blocks, (own_ref, other_ref) = refs[:-2], refs[-2:]
    _, _, core = own_chip()
    ranks = len(blocks)
    owners, _, tokens, step = blocks[0].shape
    rows = step // 4
    for d, block in enumerate(blocks):
        z = lax.rem(lax.axis_index("tensor") + d, ranks)
        for a in range(2):
            flipped = block[:, a].reshape(owners * tokens, step).T
            for i in range(2):
                even = flipped[2 * i * rows : (2 * i + 1) * rows]
                odd = flipped[(2 * i + 1) * rows : (2 * i + 2) * rows]
                to = pl.ds(pl.multiple_of((2 * z + i) * rows, 16), rows)
                own_ref[a, to] = jnp.where(core == 0, even, odd)
                other_ref[a, to] = jnp.where(core == 0, odd, even)


def row_keys(clip_ref, rows, axis):
    frames = clip_ref.shape[1]
    block = rows // frames
    index = lax.broadcasted_iota(jnp.int32, (rows, 1) if axis == 0 else (1, rows), axis)
    keys = index
    for f in range(frames):
        inside = (index >= f * block) & (index < (f + 1) * block)
        keys = jnp.where(inside, index + (clip_ref[0, f] - f) * block, keys)
    return keys


def temporal_kernel(heads, clip_ref, *refs):
    blocks, planes, sums, refs = refs[:8], refs[8:16], refs[16:24], refs[24:]
    both_ref, w_ref, token_ref, w_sem, in_sem = refs
    at_clip, at_x, core = own_chip()
    width = heads * HD
    groups = heads + 1
    ranks = len(blocks)
    owners, _, rows, _ = blocks[0].shape
    n = w_ref.shape[0]
    me = lax.axis_index("tensor")
    tokens = [[], []]
    for a in range(2):
        for d, block in enumerate(blocks):
            cols = pl.ds(pl.multiple_of(lax.rem(me + d, ranks) * width, HD), width)
            to = token_ref.at[a, :, :, cols]
            tokens[a].append(pltpu.make_async_copy(block.at[:, a], to, in_sem.at[a, d]))

    def load(g, act):
        cols = pl.ds(g * width, width)

        def for_core(known):
            for i, plane in enumerate(planes):
                step = i % n
                if (i < n) == (known == 0):
                    to = w_ref.at[lax.rem(at_clip + n - step, n), :, 0, :, cols]
                else:
                    to = w_ref.at[:, lax.rem(at_x + n - step, n), 1, :, cols]
                act(pltpu.make_async_copy(plane.at[:, :, cols], to, w_sem.at[g, i]))

        pl.when(core == 0)(lambda: for_core(0))
        pl.when(core == 1)(lambda: for_core(1))

    def start(copy):
        copy.start()

    def finish(copy):
        copy.wait()

    for copy in tokens[0]:
        copy.start()
    load(0, start)
    load(1, start)
    for copy in tokens[1]:
        copy.start()
    mask = row_keys(clip_ref, owners * rows, 0) == row_keys(clip_ref, owners * rows, 1)
    for copy in tokens[0]:
        copy.wait()
    feats = token_ref[0].reshape(owners * rows, -1)
    query, keys, values = [], [], []
    for h in range(heads):
        load(h, finish)
        if h + 2 < groups:
            load(h + 2, start)
        w_head = w_ref[:, :, :, :, h * width : (h + 1) * width].reshape(-1, width)
        qkv = dot(feats, w_head).astype(BF)
        for i, parts in enumerate((query, keys, values)):
            parts.append(qkv[:, i * HD : (i + 1) * HD])
    each = range(heads)
    probs = [softmax(query[h], keys[h], mask) for h in each]
    mixed = [dot(probs[h].astype(BF), values[h]).astype(BF) for h in each]
    for copy in tokens[1]:
        copy.wait()
    load(heads, finish)
    gated = token_ref[1].reshape(owners * rows, -1)
    w_last = w_ref[:, :, :, :, 3 * width :].reshape(-1, width)
    cotangent = dot(gated, w_last).astype(BF)
    for h in each:
        cols = slice(h * HD, (h + 1) * HD)
        grads = attention_grads(query[h], keys[h], values[h], probs[h], cotangent[:, cols])
        for i in range(3):
            both_ref[:, (3 * h + i) * HD : (3 * h + i + 1) * HD] = grads[i]
        both_ref[:, 3 * width + h * HD : 3 * width + (h + 1) * HD] = mixed[h]
    for d, out_ref in enumerate(sums):
        z = lax.rem(me + d, ranks)
        w_part = w_ref[z // 2, pl.ds(lax.rem(z, 2) * 2, 2)].reshape(width, -1)
        projected = dot(both_ref[:, 3 * width :], w_part[:, 3 * width :], NT).astype(BF)
        back = dot(both_ref[:, : 3 * width], w_part[:, : 3 * width], NT).astype(BF)
        for s in range(owners):
            out_ref[s, 0] = projected[s * rows : (s + 1) * rows]
            out_ref[s, 1] = back[s * rows : (s + 1) * rows]


def weight_grad_kernel(step, own_ref, pair_ref, both_ref, pair_both_ref, out_ref):
    at_clip, at_x, core = own_chip()
    n, slots, rows, _ = out_ref.shape
    wide = both_ref.shape[1] * 3 // 4
    starts = []
    for r in range(n):
        clip = lax.rem(at_clip + jnp.where(core == 0, r, step), n)
        x = lax.rem(at_x + jnp.where(core == 0, step, r), n)
        starts.append(pl.multiple_of((clip * n + x) * rows, 16))
    for a, cols in ((0, slice(0, wide)), (1, slice(wide, 4 * wide // 3))):
        left = jnp.concatenate(
            [
                jnp.concatenate([ref[a, pl.ds(start, rows), :] for start in starts], axis=0)
                for ref in (own_ref, pair_ref)
            ],
            axis=1,
        )
        right = jnp.concatenate([both_ref[:, cols], pair_both_ref[:, cols]], axis=0)
        total = dot(left, right).astype(BF)
        for r in range(n):
            for s in range(total.shape[1] // HD):
                part = total[r * rows : (r + 1) * rows, s * HD : (s + 1) * HD]
                out_ref[r, a * (slots * 3 // 4) + s] = part


def trade(value, j):
    return lax.ppermute(value, "frame", [(i, i ^ j) for i in range(8)])


def spread(value, step, second):
    pairs = []
    for clip in range(4):
        for x in range(4):
            for core in range(2):
                to_clip, to_x = clip, x
                if (core == 0) != second:
                    to_x = (x + step) % 4
                else:
                    to_clip = (clip + step) % 4
                pairs.append((clip * 8 + x * 2 + core, to_clip * 8 + to_x * 2 + core))
    return lax.ppermute(value, ("clip", "frame"), pairs)


def shift(value, axis, step, size):
    return lax.ppermute(value, axis, [(i, (i + step) % size) for i in range(size)])


def ring_gather(value, axis, size):
    found = {0: value}
    up = down = value
    for step in range(1, size // 2):
        up = shift(up, axis, 1, size)
        down = shift(down, axis, -1, size)
        found[size - step], found[step] = up, down
    found[size // 2] = shift(up, axis, 1, size)
    return [found[d] for d in range(size)]


def ring_sum(parts, axis):
    size = len(parts)
    up, down = parts[size // 2], parts[size // 2 + 1]
    for d in range(size // 2 - 1, 0, -1):
        up = add(shift(up, axis, 1, size), parts[d]).astype(BF)
    for d in range(size // 2 + 2, size):
        down = add(shift(down, axis, -1, size), parts[d]).astype(BF)
    return add(parts[0], shift(up, axis, 1, size), shift(down, axis, -1, size)).astype(BF)


def add(*values):
    return sum(v.astype(F32) for v in values)


def body(spatial_qkv, w_qkv, w_out, out_grad, frame_clip, clip_patches):
    ranks = lax.axis_size("frame")
    width_ranks = lax.axis_size("tensor")
    total_frames = frame_clip.shape[1]
    _, frames, patches, _, width = spatial_qkv.shape
    heads = width // HD
    block = patches // ranks
    rows_t = total_frames * block
    model = width * width_ranks
    slots = 4 * heads
    w_rows = w_qkv.shape[0]
    smem = pl.BlockSpec(memory_space=pltpu.SMEM)
    vmem = pl.BlockSpec(memory_space=pltpu.VMEM)
    hbm = pl.BlockSpec(memory_space=pltpu.HBM)

    qkv = spatial_qkv[0].transpose(0, 2, 1, 3)
    cot = out_grad[0]
    sent = pl.pallas_call(
        spatial_forward,
        out_shape=jax.ShapeDtypeStruct((ranks, 2, frames, block, width), BF),
        in_specs=[smem, smem, vmem, vmem],
        out_specs=vmem,
        scratch_shapes=[pltpu.VMEM((2, frames, patches, width), BF)],
        compiler_params=pltpu.CompilerParams(vmem_limit_bytes=58 * 2**20),
    )(frame_clip, clip_patches, qkv, cot)
    packed = pl.pallas_call(
        pack_kernel,
        out_shape=jax.ShapeDtypeStruct((w_rows, slots * HD), BF),
        in_specs=[vmem, vmem],
        out_specs=vmem,
    )(w_qkv.transpose(1, 2, 0, 3).reshape(3 * heads, w_rows, HD), w_out.transpose(0, 2, 1))
    near = [spread(packed, step, False) for step in (1, 2, 3)]
    cols = lax.all_to_all(sent, "frame", split_axis=0, concat_axis=0, tiled=True)
    cols = cols.reshape(ranks, 2, frames * block, width)
    blocks = ring_gather(cols, "tensor", width_ranks)
    line = pl.pallas_call(
        line_kernel,
        out_shape=jax.ShapeDtypeStruct((4,) + packed.shape, BF),
        in_specs=[vmem] * 4,
        out_specs=vmem,
    )(packed, *near)
    plane = [line] + [spread(line, step, True) for step in (1, 2, 3)]
    plane += [trade(rows, 1) for rows in plane]

    sums_shape = (ranks, 2, frames * block, width)
    *sums, both = pl.pallas_call(
        lambda *refs: temporal_kernel(heads, *refs),
        out_shape=[jax.ShapeDtypeStruct(sums_shape, BF)] * width_ranks
        + [jax.ShapeDtypeStruct((rows_t, 4 * width), BF)],
        in_specs=[smem] + [hbm] * (width_ranks + len(plane)),
        out_specs=[vmem] * (width_ranks + 1),
        scratch_shapes=[
            pltpu.VMEM((4, 4, 2, w_rows, slots * HD), BF),
            pltpu.VMEM((2, ranks, frames * block, model), BF),
            pltpu.SemaphoreType.DMA((heads + 1, len(plane))),
            pltpu.SemaphoreType.DMA((2, width_ranks)),
        ],
        compiler_params=pltpu.CompilerParams(vmem_limit_bytes=32 * 2**20),
    )(frame_clip, *blocks, *plane)

    halves = jax.ShapeDtypeStruct((2, model // 2, rows_t), BF)
    own_flip, other_flip = pl.pallas_call(
        flip_kernel,
        out_shape=[halves, halves],
        in_specs=[vmem] * width_ranks,
        out_specs=[vmem] * 2,
        compiler_params=pltpu.CompilerParams(vmem_limit_bytes=16 * 2**20),
    )(*blocks)
    pair_flip = trade(other_flip, 1)
    own_sums = ring_sum(sums, "tensor")
    pair_both = trade(both, 1)
    parts = {}
    for step in (2, 1, 3, 0):
        parts[step] = pl.pallas_call(
            lambda *refs, step=step: weight_grad_kernel(step, *refs),
            out_shape=jax.ShapeDtypeStruct((4, slots, w_rows, HD), BF),
            in_specs=[vmem] * 4,
            out_specs=vmem,
            compiler_params=pltpu.CompilerParams(vmem_limit_bytes=24 * 2**20),
        )(own_flip, pair_flip, both, pair_both)
    arrived = [parts[0]] + [spread(parts[step], step, False) for step in (2, 1, 3)]
    partial = [add(*(part[i] for part in arrived)).astype(BF) for i in range(4)]
    grads = add(partial[0], *(spread(partial[step], step, True) for step in (2, 1, 3)))

    row_sums = lax.all_to_all(own_sums, "frame", split_axis=0, concat_axis=0, tiled=True)
    block_out, qkv_grad = pl.pallas_call(
        spatial_backward,
        out_shape=[
            jax.ShapeDtypeStruct((frames, patches, width), BF),
            jax.ShapeDtypeStruct((frames, 3, patches, width), BF),
        ],
        in_specs=[smem, smem] + [vmem] * 3,
        out_specs=[vmem, vmem],
        scratch_shapes=[pltpu.VMEM((2, frames, patches, width), BF)],
        compiler_params=pltpu.CompilerParams(vmem_limit_bytes=24 * 2**20),
    )(frame_clip, clip_patches, qkv, cot, row_sums)

    w_qkv_grad = grads[: 3 * heads].reshape(heads, 3, w_rows, HD).transpose(2, 0, 1, 3)
    w_out_grad = grads[3 * heads :].transpose(0, 2, 1)
    return (block_out[None], qkv_grad.transpose(0, 2, 1, 3)[None], w_qkv_grad, w_out_grad)


def solution(mesh):
    in_specs = (
        P("clip", "frame", None, None, "tensor"),
        P(("clip", "frame"), "tensor", None, None),
        P("tensor", None, ("clip", "frame")),
        P("clip", "frame", None, "tensor"),
        P("clip", None),
        P("clip", None),
    )
    out_specs = (
        P("clip", "frame", None, "tensor"),
        P("clip", "frame", None, None, "tensor"),
        P(("clip", "frame"), "tensor", None, None),
        P("tensor", None, ("clip", "frame")),
    )
    return jax.shard_map(body, mesh=mesh, in_specs=in_specs, out_specs=out_specs, check_vma=False)
```

```python
import math

import jax
import jax.numpy as jnp
from jax import lax
from jax.experimental import pallas as pl
from jax.experimental.pallas import tpu as pltpu
from jax.sharding import PartitionSpec as P

HD = 128
SCALE = 1.0 / math.sqrt(HD)
BF = jnp.bfloat16
F32 = jnp.float32
NT = (((1,), (1,)), ((), ()))
TN = (((0,), (0,)), ((), ()))


def dot(a, b, dims=(((1,), (0,)), ((), ()))):
    return lax.dot_general(a, b, dims, preferred_element_type=F32)


def softmax(query, keys, mask):
    scores = jnp.where(mask, dot(query, keys, NT) * SCALE, -1e30)
    expo = jnp.exp(scores - jnp.max(scores, axis=-1, keepdims=True))
    return expo / jnp.sum(expo, axis=-1, keepdims=True)


def attention_grads(query, keys, values, probs, cotangent):
    d_values = dot(probs.astype(BF), cotangent, TN).astype(BF)
    d_probs = dot(cotangent, values, NT).astype(BF).astype(F32)
    inner = jnp.sum(probs * d_probs, axis=-1, keepdims=True)
    d_scores = (probs * (d_probs - inner) * SCALE).astype(BF)
    return dot(d_scores, keys).astype(BF), dot(d_scores, query, TN).astype(BF), d_values


def live_rows(row_ref, patch_ref, frame):
    return patch_ref[0, row_ref[0, frame]]


def spatial_forward(row_ref, patch_ref, qkv_ref, cot_ref, *refs):
    out_ref, whole_ref = refs
    frames, _, patches, width = qkv_ref.shape
    place = lax.axis_index("frame")
    owners = out_ref.shape[0]
    block = patches // owners

    def one(f, carry):
        count = live_rows(row_ref, patch_ref, place * frames + f)
        keys_live = lax.broadcasted_iota(jnp.int32, (patches, patches), 1) < count
        rows_live = lax.broadcasted_iota(jnp.int32, (patches, 1), 0) < count
        pieces = []
        for h in range(width // HD):
            cols = slice(h * HD, (h + 1) * HD)
            probs = softmax(qkv_ref[f, 0, :, cols], qkv_ref[f, 1, :, cols], keys_live)
            mixed = dot(probs.astype(BF), qkv_ref[f, 2, :, cols])
            pieces.append(jnp.where(rows_live, mixed, 0.0).astype(BF))
        whole_ref[0, f] = jnp.concatenate(pieces, axis=1)
        whole_ref[1, f] = jnp.where(rows_live, cot_ref[f].astype(F32), 0.0).astype(BF)
        return carry

    lax.fori_loop(0, frames, one, 0)
    for s in range(owners):
        out_ref[s] = whole_ref[:, :, s * block : (s + 1) * block, :]


def spatial_backward(row_ref, patch_ref, qkv_ref, cot_ref, *refs):
    sums_ref, out_ref, grad_ref, whole_ref = refs
    frames, _, patches, width = qkv_ref.shape
    place = lax.axis_index("frame")
    owners = sums_ref.shape[0]
    block = patches // owners
    for s in range(owners):
        for f in range(frames):
            part = sums_ref[s, :, f * block : (f + 1) * block, :]
            whole_ref[:, f, s * block : (s + 1) * block, :] = part

    def one(f, carry):
        count = live_rows(row_ref, patch_ref, place * frames + f)
        keys_live = lax.broadcasted_iota(jnp.int32, (patches, patches), 1) < count
        rows_live = lax.broadcasted_iota(jnp.int32, (patches, 1), 0) < count
        d_spatial = cot_ref[f].astype(F32) + whole_ref[1, f].astype(F32)
        d_mixed = jnp.where(rows_live, d_spatial, 0.0).astype(BF)
        for h in range(width // HD):
            cols = slice(h * HD, (h + 1) * HD)
            query, keys, values = (qkv_ref[f, i, :, cols] for i in range(3))
            probs = softmax(query, keys, keys_live)
            mixed = dot(probs.astype(BF), values).astype(BF).astype(F32)
            total = mixed + whole_ref[0, f, :, cols].astype(F32)
            out_ref[f, :, cols] = jnp.where(rows_live, total, 0.0).astype(BF)
            grads = attention_grads(query, keys, values, probs, d_mixed[:, cols])
            for i in range(3):
                grad_ref[f, i, :, cols] = grads[i]
        return carry

    lax.fori_loop(0, frames, one, 0)


def pack_kernel(qkv_ref, out_ref, packed_ref):
    for ref, first in ((qkv_ref, 0), (out_ref, qkv_ref.shape[0])):
        for s in range(ref.shape[0]):
            packed_ref[:, (first + s) * HD : (first + s + 1) * HD] = ref[s]


def own_chip():
    place = lax.axis_index("frame")
    return lax.axis_index("clip"), place // 2, place % 2


def line_kernel(own_ref, near_1, near_2, near_3, line_ref):
    at_clip, at_x, core = own_chip()
    at = jnp.where(core == 0, at_x, at_clip)
    for step, ref in enumerate((own_ref, near_1, near_2, near_3)):
        line_ref[lax.rem(at + 4 - step, 4)] = ref[...]


def flip_kernel(*refs):
    blocks, (own_ref, other_ref) = refs[:-2], refs[-2:]
    _, _, core = own_chip()
    ranks = len(blocks) // 2
    owners, tokens, step = blocks[0].shape
    rows = step // 4
    for i, block in enumerate(blocks):
        a, d = divmod(i, ranks)
        z = lax.rem(lax.axis_index("tensor") + d, ranks)
        flipped = block[...].reshape(owners * tokens, step).T
        for k in range(2):
            even = flipped[2 * k * rows : (2 * k + 1) * rows]
            odd = flipped[(2 * k + 1) * rows : (2 * k + 2) * rows]
            to = pl.ds(pl.multiple_of((2 * z + k) * rows, 16), rows)
            own_ref[a, to] = jnp.where(core == 0, even, odd)
            other_ref[a, to] = jnp.where(core == 0, odd, even)


def row_keys(clip_ref, rows, axis):
    frames = clip_ref.shape[1]
    block = rows // frames
    index = lax.broadcasted_iota(jnp.int32, (rows, 1) if axis == 0 else (1, rows), axis)
    keys = index
    for f in range(frames):
        inside = (index >= f * block) & (index < (f + 1) * block)
        keys = jnp.where(inside, index + (clip_ref[0, f] - f) * block, keys)
    return keys


def temporal_kernel(heads, clip_ref, *refs):
    blocks, planes, refs = refs[:16], refs[16:24], refs[24:]
    sums_ref, both_ref, w_ref, token_ref, qkv_ref, w_sem, in_sem = refs
    at_clip, at_x, core = own_chip()
    me = lax.axis_index("tensor")
    width = heads * HD
    ranks, owners, _, rows, _ = sums_ref.shape
    n = w_ref.shape[0]
    tokens = []
    for i, block in enumerate(blocks):
        cols = pl.ds(pl.multiple_of(lax.rem(me + i % ranks, ranks) * width, HD), width)
        to = token_ref.at[i // ranks, :, :, cols]
        tokens.append(pltpu.make_async_copy(block, to, in_sem.at[i]))

    def load(known, act):
        for i, plane in enumerate(planes):
            step = i % n
            if (i < n) == (known == 0):
                to = w_ref.at[lax.rem(at_clip + n - step, n), :, 0]
            else:
                to = w_ref.at[:, lax.rem(at_x + n - step, n), 1]
            act(pltpu.make_async_copy(plane, to, w_sem.at[i]))

    def start(copy):
        copy.start()

    def finish(copy):
        copy.wait()

    for act in (start, finish):
        for copy in tokens:
            act(copy)
        pl.when(core == 0)(lambda act=act: load(0, act))
        pl.when(core == 1)(lambda act=act: load(1, act))
    mask = row_keys(clip_ref, owners * rows, 0) == row_keys(clip_ref, owners * rows, 1)

    def project(h, carry):
        cols = pl.ds(pl.multiple_of(h * width, HD), width)
        tokens_in = token_ref[h // heads].reshape(owners * rows, -1)
        w_part = w_ref[:, :, :, :, cols].reshape(-1, width)
        qkv_ref[:, cols] = dot(tokens_in, w_part).astype(BF)
        return carry

    lax.fori_loop(0, heads + 1, project, 0)
    query, keys, values = (
        [qkv_ref[:, (3 * h + i) * HD : (3 * h + i + 1) * HD] for h in range(heads)]
        for i in range(3)
    )
    each = range(heads)
    probs = [softmax(query[h], keys[h], mask) for h in each]
    for h in each:
        cols = slice(3 * width + h * HD, 3 * width + (h + 1) * HD)
        grads = attention_grads(query[h], keys[h], values[h], probs[h], qkv_ref[:, cols])
        for i in range(3):
            both_ref[:, (3 * h + i) * HD : (3 * h + i + 1) * HD] = grads[i]
        both_ref[:, cols] = dot(probs[h].astype(BF), values[h]).astype(BF)

    def back_project(d, carry):
        z = lax.rem(me + d, ranks)
        w_part = w_ref[z // 2, pl.ds(lax.rem(z, 2) * 2, 2)].reshape(width, -1)
        projected = dot(both_ref[:, 3 * width :], w_part[:, 3 * width :], NT).astype(BF)
        back = dot(both_ref[:, : 3 * width], w_part[:, : 3 * width], NT).astype(BF)
        sums_ref[d, :, 0] = projected.reshape(owners, rows, width)
        sums_ref[d, :, 1] = back.reshape(owners, rows, width)
        return carry

    lax.fori_loop(0, ranks, back_project, 0)


def weight_grad_kernel(step, own_ref, pair_ref, both_ref, pair_both_ref, out_ref):
    at_clip, at_x, core = own_chip()
    n, slots, rows, _ = out_ref.shape
    wide = both_ref.shape[1] * 3 // 4

    def one(r, carry):
        clip = lax.rem(at_clip + jnp.where(core == 0, r, step), n)
        x = lax.rem(at_x + jnp.where(core == 0, step, r), n)
        here = pl.ds(pl.multiple_of((clip * n + x) * rows, 16), rows)
        for a, cols in ((0, slice(0, wide)), (1, slice(wide, 4 * wide // 3))):
            total = dot(own_ref[a, here, :], both_ref[:, cols])
            total = (total + dot(pair_ref[a, here, :], pair_both_ref[:, cols])).astype(BF)
            for s in range(total.shape[1] // HD):
                out_ref[r, a * (slots * 3 // 4) + s] = total[:, s * HD : (s + 1) * HD]
        return carry

    lax.fori_loop(0, n, one, 0)


def trade(value, j):
    return lax.ppermute(value, "frame", [(i, i ^ j) for i in range(8)])


def spread(value, step, second):
    pairs = []
    for clip in range(4):
        for x in range(4):
            for core in range(2):
                to_clip, to_x = clip, x
                if (core == 0) != second:
                    to_x = (x + step) % 4
                else:
                    to_clip = (clip + step) % 4
                pairs.append((clip * 8 + x * 2 + core, to_clip * 8 + to_x * 2 + core))
    return lax.ppermute(value, ("clip", "frame"), pairs)


def shift(value, axis, step, size):
    return lax.ppermute(value, axis, [(i, (i + step) % size) for i in range(size)])


def ring_gather(value, axis, size, last_up):
    found = {0: value}
    up = down = value
    for step in range(1, size // 2):
        up = shift(up, axis, 1, size)
        down = shift(down, axis, -1, size)
        found[size - step], found[step] = up, down
    found[size // 2] = shift(up, axis, 1, size) if last_up else shift(down, axis, -1, size)
    return [found[d] for d in range(size)]


def ring_sum(parts, axis):
    size = len(parts)
    up, down = parts[size // 2], parts[size // 2 + 1]
    for d in range(size // 2 - 1, 0, -1):
        up = add(shift(up, axis, 1, size), parts[d]).astype(BF)
    for d in range(size // 2 + 2, size):
        down = add(shift(down, axis, -1, size), parts[d]).astype(BF)
    return add(parts[0], shift(up, axis, 1, size), shift(down, axis, -1, size)).astype(BF)


def add(*values):
    return sum(v.astype(F32) for v in values)


def body(spatial_qkv, w_qkv, w_out, out_grad, frame_clip, clip_patches):
    ranks = lax.axis_size("frame")
    width_ranks = lax.axis_size("tensor")
    total_frames = frame_clip.shape[1]
    _, frames, patches, _, width = spatial_qkv.shape
    heads = width // HD
    block = patches // ranks
    rows_t = total_frames * block
    model = width * width_ranks
    slots = 4 * heads
    w_rows = w_qkv.shape[0]
    smem = pl.BlockSpec(memory_space=pltpu.SMEM)
    vmem = pl.BlockSpec(memory_space=pltpu.VMEM)
    hbm = pl.BlockSpec(memory_space=pltpu.HBM)

    qkv = spatial_qkv[0].transpose(0, 2, 1, 3)
    cot = out_grad[0]
    sent = pl.pallas_call(
        spatial_forward,
        out_shape=jax.ShapeDtypeStruct((ranks, 2, frames, block, width), BF),
        in_specs=[smem, smem, vmem, vmem],
        out_specs=vmem,
        scratch_shapes=[pltpu.VMEM((2, frames, patches, width), BF)],
        compiler_params=pltpu.CompilerParams(vmem_limit_bytes=58 * 2**20),
    )(frame_clip, clip_patches, qkv, cot)
    packed = pl.pallas_call(
        pack_kernel,
        out_shape=jax.ShapeDtypeStruct((w_rows, slots * HD), BF),
        in_specs=[vmem, vmem],
        out_specs=vmem,
    )(w_qkv.transpose(1, 2, 0, 3).reshape(3 * heads, w_rows, HD), w_out.transpose(0, 2, 1))
    near = [spread(packed, step, False) for step in (1, 2, 3)]
    cols = lax.all_to_all(sent, "frame", split_axis=0, concat_axis=0, tiled=True)
    cols = cols.reshape(ranks, 2, frames * block, width)
    blocks = []
    for a in range(2):
        blocks += ring_gather(cols[:, a], "tensor", width_ranks, a == 0)
    line = pl.pallas_call(
        line_kernel,
        out_shape=jax.ShapeDtypeStruct((4,) + packed.shape, BF),
        in_specs=[vmem] * 4,
        out_specs=vmem,
    )(packed, *near)
    plane = [line] + [spread(line, step, True) for step in (1, 2, 3)]
    plane += [trade(rows, 1) for rows in plane]

    sums, both = pl.pallas_call(
        lambda *refs: temporal_kernel(heads, *refs),
        out_shape=[
            jax.ShapeDtypeStruct((width_ranks, ranks, 2, frames * block, width), BF),
            jax.ShapeDtypeStruct((rows_t, 4 * width), BF),
        ],
        in_specs=[smem] + [hbm] * (len(blocks) + len(plane)),
        out_specs=[vmem] * 2,
        scratch_shapes=[
            pltpu.VMEM((4, 4, 2, w_rows, slots * HD), BF),
            pltpu.VMEM((2, ranks, frames * block, model), BF),
            pltpu.VMEM((rows_t, 4 * width), BF),
            pltpu.SemaphoreType.DMA((len(plane),)),
            pltpu.SemaphoreType.DMA((len(blocks),)),
        ],
        compiler_params=pltpu.CompilerParams(vmem_limit_bytes=32 * 2**20),
    )(frame_clip, *blocks, *plane)

    halves = jax.ShapeDtypeStruct((2, model // 2, rows_t), BF)
    own_flip, other_flip = pl.pallas_call(
        flip_kernel,
        out_shape=[halves, halves],
        in_specs=[vmem] * len(blocks),
        out_specs=[vmem] * 2,
        compiler_params=pltpu.CompilerParams(vmem_limit_bytes=16 * 2**20),
    )(*blocks)
    pair_flip = trade(other_flip, 1)
    pair_both = trade(both, 1)
    parts = {}
    for step in (2, 1, 3, 0):
        parts[step] = pl.pallas_call(
            lambda *refs, step=step: weight_grad_kernel(step, *refs),
            out_shape=jax.ShapeDtypeStruct((4, slots, w_rows, HD), BF),
            in_specs=[vmem] * 4,
            out_specs=vmem,
            compiler_params=pltpu.CompilerParams(vmem_limit_bytes=24 * 2**20),
        )(own_flip, pair_flip, both, pair_both)
    later, parts[1], parts[2], parts[3] = lax.optimization_barrier(
        [sums, parts[1], parts[2], parts[3]]
    )
    own_sums = ring_sum([(sums if d in (4, 5) else later)[d] for d in range(width_ranks)], "tensor")
    arrived = [parts[0]] + [spread(parts[step], step, False) for step in (2, 1, 3)]
    partial = [add(*(part[i] for part in arrived)).astype(BF) for i in range(4)]
    grads = add(partial[0], *(spread(partial[step], step, True) for step in (2, 1, 3)))

    row_sums = lax.all_to_all(own_sums, "frame", split_axis=0, concat_axis=0, tiled=True)
    block_out, qkv_grad = pl.pallas_call(
        spatial_backward,
        out_shape=[
            jax.ShapeDtypeStruct((frames, patches, width), BF),
            jax.ShapeDtypeStruct((frames, 3, patches, width), BF),
        ],
        in_specs=[smem, smem] + [vmem] * 3,
        out_specs=[vmem, vmem],
        scratch_shapes=[pltpu.VMEM((2, frames, patches, width), BF)],
        compiler_params=pltpu.CompilerParams(vmem_limit_bytes=24 * 2**20),
    )(frame_clip, clip_patches, qkv, cot, row_sums)

    w_qkv_grad = grads[: 3 * heads].reshape(heads, 3, w_rows, HD).transpose(2, 0, 1, 3)
    w_out_grad = grads[3 * heads :].transpose(0, 2, 1)
    return (block_out[None], qkv_grad.transpose(0, 2, 1, 3)[None], w_qkv_grad, w_out_grad)


def solution(mesh):
    in_specs = (
        P("clip", "frame", None, None, "tensor"),
        P(("clip", "frame"), "tensor", None, None),
        P("tensor", None, ("clip", "frame")),
        P("clip", "frame", None, "tensor"),
        P("clip", None),
        P("clip", None),
    )
    out_specs = (
        P("clip", "frame", None, "tensor"),
        P("clip", "frame", None, None, "tensor"),
        P(("clip", "frame"), "tensor", None, None),
        P("tensor", None, ("clip", "frame")),
    )
    return jax.shard_map(body, mesh=mesh, in_specs=in_specs, out_specs=out_specs, check_vma=False)
```

```python
import math

import jax
import jax.numpy as jnp
from jax import lax
from jax.experimental import pallas as pl
from jax.experimental.pallas import tpu as pltpu
from jax.sharding import PartitionSpec as P

HD = 128
SCALE = 1.0 / math.sqrt(HD)
BF = jnp.bfloat16
F32 = jnp.float32
NT = (((1,), (1,)), ((), ()))
TN = (((0,), (0,)), ((), ()))


def dot(a, b, dims=(((1,), (0,)), ((), ()))):
    return lax.dot_general(a, b, dims, preferred_element_type=F32)


def softmax(query, keys, mask):
    scores = jnp.where(mask, dot(query, keys, NT) * SCALE, -1e30)
    expo = jnp.exp(scores - jnp.max(scores, axis=-1, keepdims=True))
    return expo / jnp.sum(expo, axis=-1, keepdims=True)


def attention_grads(queries, keys, values, probs, cotangents):
    each = range(len(probs))
    d_values = [dot(probs[i].astype(BF), cotangents[i], TN).astype(BF) for i in each]
    d_probs = [dot(cotangents[i], values[i], NT).astype(BF).astype(F32) for i in each]
    inner = [jnp.sum(probs[i] * d_probs[i], axis=-1, keepdims=True) for i in each]
    d_scores = [(probs[i] * (d_probs[i] - inner[i]) * SCALE).astype(BF) for i in each]
    d_queries = [dot(d_scores[i], keys[i]).astype(BF) for i in each]
    d_keys = [dot(d_scores[i], queries[i], TN).astype(BF) for i in each]
    return list(zip(d_queries, d_keys, d_values))


def live_rows(row_ref, patch_ref, frame):
    return patch_ref[0, row_ref[0, frame]]


def spatial_forward(row_ref, patch_ref, qkv_ref, cot_ref, *refs):
    out_ref, whole_ref = refs
    frames, _, patches, width = qkv_ref.shape
    place = lax.axis_index("frame")
    owners = out_ref.shape[0]
    block = patches // owners
    for f in range(frames):
        count = live_rows(row_ref, patch_ref, place * frames + f)
        keys_live = lax.broadcasted_iota(jnp.int32, (patches, patches), 1) < count
        rows_live = lax.broadcasted_iota(jnp.int32, (patches, 1), 0) < count
        pieces = []
        for h in range(width // HD):
            cols = slice(h * HD, (h + 1) * HD)
            probs = softmax(qkv_ref[f, 0, :, cols], qkv_ref[f, 1, :, cols], keys_live)
            mixed = dot(probs.astype(BF), qkv_ref[f, 2, :, cols])
            pieces.append(jnp.where(rows_live, mixed, 0.0).astype(BF))
        whole_ref[0, f] = jnp.concatenate(pieces, axis=1)
        whole_ref[1, f] = jnp.where(rows_live, cot_ref[f].astype(F32), 0.0).astype(BF)
    for s in range(owners):
        out_ref[s] = whole_ref[:, :, s * block : (s + 1) * block, :]


def spatial_backward(row_ref, patch_ref, qkv_ref, cot_ref, *refs):
    sums_ref, out_ref, grad_ref, whole_ref = refs
    frames, _, patches, width = qkv_ref.shape
    place = lax.axis_index("frame")
    owners = sums_ref.shape[0]
    block = patches // owners
    for s in range(owners):
        for f in range(frames):
            part = sums_ref[s, :, f * block : (f + 1) * block, :]
            whole_ref[:, f, s * block : (s + 1) * block, :] = part
    live, d_mixed = [], []
    for f in range(frames):
        count = live_rows(row_ref, patch_ref, place * frames + f)
        keys_live = lax.broadcasted_iota(jnp.int32, (patches, patches), 1) < count
        live.append((keys_live, lax.broadcasted_iota(jnp.int32, (patches, 1), 0) < count))
        d_spatial = cot_ref[f].astype(F32) + whole_ref[1, f].astype(F32)
        d_mixed.append(jnp.where(live[f][1], d_spatial, 0.0).astype(BF))
    each = [(f, slice(h * HD, (h + 1) * HD)) for f in range(frames) for h in range(width // HD)]
    queries, keys, values = ([qkv_ref[f, i, :, cols] for f, cols in each] for i in range(3))
    cotangents = [d_mixed[f][:, cols] for f, cols in each]
    probs = [softmax(queries[i], keys[i], live[f][0]) for i, (f, _) in enumerate(each)]
    grads = attention_grads(queries, keys, values, probs, cotangents)
    for i, (f, cols) in enumerate(each):
        mixed = dot(probs[i].astype(BF), values[i]).astype(BF).astype(F32)
        total = mixed + whole_ref[0, f, :, cols].astype(F32)
        out_ref[f, :, cols] = jnp.where(live[f][1], total, 0.0).astype(BF)
        for k in range(3):
            grad_ref[f, k, :, cols] = grads[i][k]


def own_chip():
    place = lax.axis_index("frame")
    return lax.axis_index("clip"), place // 2, place % 2


def assemble_kernel(ranks, *refs):
    blocks, refs = refs[: 2 * ranks], refs[2 * ranks :]
    feat_ref, gated_ref, own_ref, other_ref, flip_ref, sem = refs
    me, core = lax.axis_index("tensor"), own_chip()[2]
    width = feat_ref.shape[1] // ranks
    copies = []
    for a, whole in enumerate((feat_ref, gated_ref)):
        for d in range(ranks):
            start = pl.multiple_of(lax.rem(me + d, ranks) * width, HD)
            i = a * ranks + d
            copies.append(
                pltpu.make_async_copy(blocks[i], whole.at[:, pl.ds(start, width)], sem.at[i])
            )
    for copy in copies:
        copy.start()
    for copy in copies:
        copy.wait()
    pieces = 32
    rows = feat_ref.shape[1] // pieces
    for a, whole in enumerate((feat_ref, gated_ref)):
        for z in range(ranks):
            part = slice(z * width, (z + 1) * width)
            flip_ref[part, :] = whole[:, part].T
        for i in range(pieces // 2):
            to = slice(i * rows, (i + 1) * rows)
            own_ref[a, to] = flip_ref[pl.ds(pl.multiple_of((2 * i + core) * rows, 16), rows), :]
            other_ref[a, to] = flip_ref[pl.ds(pl.multiple_of((2 * i + 1 - core) * rows, 16), rows), :]


def row_keys(clip_ref, rows, axis):
    frames = clip_ref.shape[1]
    block = rows // frames
    index = lax.broadcasted_iota(jnp.int32, (rows, 1) if axis == 0 else (1, rows), axis)
    keys = index
    for f in range(frames):
        inside = (index >= f * block) & (index < (f + 1) * block)
        keys = jnp.where(inside, index + (clip_ref[0, f] - f) * block, keys)
    return keys


def temporal_kernel(heads, clip_ref, feat_hbm, gated_hbm, w_hbm, *refs):
    sums_hbm, both_ref, feat_ref, gated_ref, w_ref, sums_ref, in_sem, w_sem, out_sem = refs
    width = heads * HD
    slots = 4 * heads
    ranks, owners, _, rows, _ = sums_ref.shape
    loads = [
        pltpu.make_async_copy(w_hbm.at[i], w_ref.at[:, i * HD : (i + 1) * HD], w_sem.at[i])
        for i in range(slots)
    ]
    feat_load = pltpu.make_async_copy(feat_hbm, feat_ref, in_sem.at[0])
    gated_load = pltpu.make_async_copy(gated_hbm, gated_ref, in_sem.at[1])
    feat_load.start()
    for copy in loads[:6]:
        copy.start()
    mask = row_keys(clip_ref, owners * rows, 0) == row_keys(clip_ref, owners * rows, 1)
    feat_load.wait()
    query, keys, values = [], [], []
    for h in range(heads):
        for copy in loads[3 * h : 3 * h + 3]:
            copy.wait()
        if h == 0:
            gated_load.start()
        for copy in loads[3 * h + 6 : 3 * h + 9]:
            copy.start()
        qkv = dot(feat_ref[...], w_ref[:, h * width : (h + 1) * width]).astype(BF)
        for i, parts in enumerate((query, keys, values)):
            parts.append(qkv[:, i * HD : (i + 1) * HD])
    each = range(heads)
    probs = [softmax(query[h], keys[h], mask) for h in each]
    mixed = [dot(probs[h].astype(BF), values[h]).astype(BF) for h in each]
    gated_load.wait()
    for copy in loads[9:]:
        copy.wait()
    cotangent = dot(gated_ref[...], w_ref[:, 3 * width :]).astype(BF)
    cotangents = [cotangent[:, h * HD : (h + 1) * HD] for h in each]
    grads = attention_grads(query, keys, values, probs, cotangents)
    for h in each:
        for i in range(3):
            both_ref[:, (3 * h + i) * HD : (3 * h + i + 1) * HD] = grads[h][i]
        both_ref[:, 3 * width + h * HD : 3 * width + (h + 1) * HD] = mixed[h]
    stores = []
    pair = 4
    for first in range(0, ranks, pair):
        w_part = w_ref.at[first * width : (first + pair) * width]
        projected = dot(both_ref[:, 3 * width :], w_part[:, 3 * width :], NT).astype(BF)
        back = dot(both_ref[:, : 3 * width], w_part[:, : 3 * width], NT).astype(BF)
        for i in range(pair):
            z, cols = first + i, slice(i * width, (i + 1) * width)
            for s in range(owners):
                sums_ref[z, s, 0] = projected[s * rows : (s + 1) * rows, cols]
                sums_ref[z, s, 1] = back[s * rows : (s + 1) * rows, cols]
            stores.append(pltpu.make_async_copy(sums_ref.at[z], sums_hbm.at[z], out_sem.at[z]))
            stores[-1].start()
    for copy in stores:
        copy.wait()


def weight_grad_kernel(step, own_ref, pair_ref, both_ref, pair_both_ref, out_ref):
    at_clip, at_x, core = own_chip()
    n, slots, rows, _ = out_ref.shape
    wide = both_ref.shape[1] * 3 // 4
    starts = []
    for r in range(n):
        clip = lax.rem(at_clip + jnp.where(core == 0, r, step), n)
        x = lax.rem(at_x + jnp.where(core == 0, step, r), n)
        starts.append(pl.multiple_of((clip * n + x) * rows, 16))
    for a, cols in ((0, slice(0, wide)), (1, slice(wide, 4 * wide // 3))):
        left = jnp.concatenate(
            [
                jnp.concatenate([ref[a, pl.ds(start, rows), :] for start in starts], axis=0)
                for ref in (own_ref, pair_ref)
            ],
            axis=1,
        )
        right = jnp.concatenate([both_ref[:, cols], pair_both_ref[:, cols]], axis=0)
        total = dot(left, right).astype(BF)
        for r in range(n):
            for s in range(total.shape[1] // HD):
                part = total[r * rows : (r + 1) * rows, s * HD : (s + 1) * HD]
                out_ref[r, a * (slots * 3 // 4) + s] = part


def shift(value, axis, step, size):
    return lax.ppermute(value, axis, [(i, (i + step) % size) for i in range(size)])


def pair_swap(value):
    return lax.ppermute(value, "frame", [(i, i ^ 1) for i in range(8)])


def spread(value, step, second):
    pairs = []
    for clip in range(4):
        for x in range(4):
            for core in range(2):
                to_clip, to_x = clip, x
                if (core == 0) != second:
                    to_x = (x + step) % 4
                else:
                    to_clip = (clip + step) % 4
                pairs.append((clip * 8 + x * 2 + core, to_clip * 8 + to_x * 2 + core))
    return lax.ppermute(value, ("clip", "frame"), pairs)


def ring_gather(value, axis, size, last_forward):
    found = {0: value}
    up = down = value
    for step in range(1, size // 2):
        up = shift(up, axis, 1, size)
        down = shift(down, axis, -1, size)
        found[size - step], found[step] = up, down
    found[size // 2] = shift(up, axis, 1, size) if last_forward else shift(down, axis, -1, size)
    return [found[d] for d in range(size)]


def add(*values):
    return sum(v.astype(F32) for v in values)


def body(spatial_qkv, w_qkv, w_out, out_grad, frame_clip, clip_patches):
    ranks = lax.axis_size("frame")
    width_ranks = lax.axis_size("tensor")
    total_frames = frame_clip.shape[1]
    _, frames, patches, _, width = spatial_qkv.shape
    heads = width // HD
    block = patches // ranks
    rows_t = total_frames * block
    model = width * width_ranks
    slots = 4 * heads

    w_rows = w_qkv.shape[0]
    w_own = jnp.concatenate(
        [w_qkv.transpose(1, 2, 0, 3).reshape(3 * heads, w_rows, HD), w_out.transpose(0, 2, 1)],
        axis=0,
    )
    w_all = lax.all_gather(w_own, ("clip", "frame"), axis=1, tiled=True)

    qkv = spatial_qkv[0].transpose(0, 2, 1, 3)
    cot = out_grad[0]
    smem = pl.BlockSpec(memory_space=pltpu.SMEM)
    vmem = pl.BlockSpec(memory_space=pltpu.VMEM)
    hbm = pl.BlockSpec(memory_space=pltpu.HBM)
    sent = pl.pallas_call(
        spatial_forward,
        out_shape=jax.ShapeDtypeStruct((ranks, 2, frames, block, width), BF),
        in_specs=[smem, smem, vmem, vmem],
        out_specs=vmem,
        scratch_shapes=[pltpu.VMEM((2, frames, patches, width), BF)],
        compiler_params=pltpu.CompilerParams(vmem_limit_bytes=58 * 2**20),
    )(frame_clip, clip_patches, qkv, cot)
    cols = lax.all_to_all(sent, "frame", split_axis=0, concat_axis=0, tiled=True)
    blocks = []
    for a in range(2):
        rows = cols[:, a].reshape(rows_t, width)
        blocks += ring_gather(rows, "tensor", width_ranks, a == 0)

    halves = jax.ShapeDtypeStruct((2, model // 2, rows_t), BF)
    wide = jax.ShapeDtypeStruct((rows_t, model), BF)
    feats, gated, own_flip, other_flip = pl.pallas_call(
        lambda *refs: assemble_kernel(width_ranks, *refs),
        out_shape=[wide, wide, halves, halves],
        in_specs=[hbm] * (2 * width_ranks),
        out_specs=[vmem] * 4,
        scratch_shapes=[
            pltpu.VMEM((model, rows_t), BF),
            pltpu.SemaphoreType.DMA((2 * width_ranks,)),
        ],
        compiler_params=pltpu.CompilerParams(vmem_limit_bytes=58 * 2**20),
    )(*blocks)
    pair_flip = pair_swap(other_flip)
    feats, pair_flip = lax.optimization_barrier([feats, pair_flip])

    wide_scratch = pltpu.VMEM((rows_t, model), BF)
    sums_shape = (width_ranks, ranks, 2, frames * block, width)
    sums, both = pl.pallas_call(
        lambda *refs: temporal_kernel(heads, *refs),
        out_shape=[
            jax.ShapeDtypeStruct(sums_shape, BF),
            jax.ShapeDtypeStruct((rows_t, 4 * width), BF),
        ],
        in_specs=[smem] + [hbm] * 3,
        out_specs=[hbm, vmem],
        scratch_shapes=[
            wide_scratch,
            wide_scratch,
            pltpu.VMEM((model, 4 * width), BF),
            pltpu.VMEM(sums_shape, BF),
            pltpu.SemaphoreType.DMA((2,)),
            pltpu.SemaphoreType.DMA((slots,)),
            pltpu.SemaphoreType.DMA((width_ranks,)),
        ],
        compiler_params=pltpu.CompilerParams(vmem_limit_bytes=56 * 2**20),
    )(frame_clip, feats, gated, w_all)

    own_sums = lax.psum_scatter(sums, "tensor", scatter_dimension=0, tiled=True)[0]
    pair_both = pair_swap(both)
    parts = {}
    for step in (2, 1, 3, 0):
        parts[step] = pl.pallas_call(
            lambda *refs, step=step: weight_grad_kernel(step, *refs),
            out_shape=jax.ShapeDtypeStruct((4, slots, w_rows, HD), BF),
            in_specs=[vmem] * 4,
            out_specs=vmem,
            compiler_params=pltpu.CompilerParams(vmem_limit_bytes=24 * 2**20),
        )(own_flip, pair_flip, both, pair_both)
    arrived = [parts[0]] + [spread(parts[step], step, False) for step in (2, 1, 3)]
    partial = [add(*(part[i] for part in arrived)).astype(BF) for i in range(4)]
    grads = add(partial[0], *(spread(partial[step], step, True) for step in (2, 1, 3)))

    row_sums = lax.all_to_all(own_sums, "frame", split_axis=0, concat_axis=0, tiled=True)
    block_out, qkv_grad = pl.pallas_call(
        spatial_backward,
        out_shape=[
            jax.ShapeDtypeStruct((frames, patches, width), BF),
            jax.ShapeDtypeStruct((frames, 3, patches, width), BF),
        ],
        in_specs=[smem, smem] + [vmem] * 3,
        out_specs=[vmem, vmem],
        scratch_shapes=[pltpu.VMEM((2, frames, patches, width), BF)],
        compiler_params=pltpu.CompilerParams(vmem_limit_bytes=24 * 2**20),
    )(frame_clip, clip_patches, qkv, cot, row_sums)

    w_qkv_grad = grads[: 3 * heads].reshape(heads, 3, w_rows, HD).transpose(2, 0, 1, 3)
    w_out_grad = grads[3 * heads :].transpose(0, 2, 1)
    return (block_out[None], qkv_grad.transpose(0, 2, 1, 3)[None], w_qkv_grad, w_out_grad)


def solution(mesh):
    in_specs = (
        P("clip", "frame", None, None, "tensor"),
        P(("clip", "frame"), "tensor", None, None),
        P("tensor", None, ("clip", "frame")),
        P("clip", "frame", None, "tensor"),
        P("clip", None),
        P("clip", None),
    )
    out_specs = (
        P("clip", "frame", None, "tensor"),
        P("clip", "frame", None, None, "tensor"),
        P(("clip", "frame"), "tensor", None, None),
        P("tensor", None, ("clip", "frame")),
    )
    return jax.shard_map(body, mesh=mesh, in_specs=in_specs, out_specs=out_specs, check_vma=False)
```

```python
import math

import jax
import jax.numpy as jnp
from jax import lax
from jax.experimental import pallas as pl
from jax.experimental.pallas import tpu as pltpu
from jax.sharding import PartitionSpec as P

HD = 128
SCALE = 1.0 / math.sqrt(HD)
BF = jnp.bfloat16
F32 = jnp.float32
NT = (((1,), (1,)), ((), ()))
TN = (((0,), (0,)), ((), ()))


def dot(a, b, dims=(((1,), (0,)), ((), ()))):
    return lax.dot_general(a, b, dims, preferred_element_type=F32)


def softmax(query, keys, mask):
    scores = jnp.where(mask, dot(query, keys, NT) * SCALE, -1e30)
    expo = jnp.exp(scores - jnp.max(scores, axis=-1, keepdims=True))
    return expo / jnp.sum(expo, axis=-1, keepdims=True)


def attention_grads(queries, keys, values, probs, cotangents):
    each = range(len(probs))
    d_values = [dot(probs[i].astype(BF), cotangents[i], TN).astype(BF) for i in each]
    d_probs = [dot(cotangents[i], values[i], NT).astype(BF).astype(F32) for i in each]
    inner = [jnp.sum(probs[i] * d_probs[i], axis=-1, keepdims=True) for i in each]
    d_scores = [(probs[i] * (d_probs[i] - inner[i]) * SCALE).astype(BF) for i in each]
    d_queries = [dot(d_scores[i], keys[i]).astype(BF) for i in each]
    d_keys = [dot(d_scores[i], queries[i], TN).astype(BF) for i in each]
    return list(zip(d_queries, d_keys, d_values))


def live_rows(row_ref, patch_ref, frame):
    return patch_ref[0, row_ref[0, frame]]


def spatial_forward(row_ref, patch_ref, qkv_ref, cot_ref, *refs):
    out_ref, whole_ref = refs
    frames, _, patches, width = qkv_ref.shape
    place = lax.axis_index("frame")
    owners = out_ref.shape[0]
    block = patches // owners
    for f in range(frames):
        count = live_rows(row_ref, patch_ref, place * frames + f)
        keys_live = lax.broadcasted_iota(jnp.int32, (patches, patches), 1) < count
        rows_live = lax.broadcasted_iota(jnp.int32, (patches, 1), 0) < count
        pieces = []
        for h in range(width // HD):
            cols = slice(h * HD, (h + 1) * HD)
            probs = softmax(qkv_ref[f, 0, :, cols], qkv_ref[f, 1, :, cols], keys_live)
            mixed = dot(probs.astype(BF), qkv_ref[f, 2, :, cols])
            pieces.append(jnp.where(rows_live, mixed, 0.0).astype(BF))
        whole_ref[0, f] = jnp.concatenate(pieces, axis=1)
        whole_ref[1, f] = jnp.where(rows_live, cot_ref[f].astype(F32), 0.0).astype(BF)
    for s in range(owners):
        out_ref[s] = whole_ref[:, :, s * block : (s + 1) * block, :]


def spatial_backward(row_ref, patch_ref, qkv_ref, cot_ref, *refs):
    blocks, (out_ref, grad_ref, whole_ref) = refs[:-3], refs[-3:]
    frames, _, patches, width = qkv_ref.shape
    place = lax.axis_index("frame")
    block = blocks[0].shape[2] // frames
    for m, ref in enumerate(blocks):
        for i in range(2):
            start = pl.multiple_of((place ^ (2 * m + i)) * block, 16)
            for f in range(frames):
                part = ref[i, :, f * block : (f + 1) * block, :]
                whole_ref[:, f, pl.ds(start, block), :] = part
    live, d_mixed = [], []
    for f in range(frames):
        count = live_rows(row_ref, patch_ref, place * frames + f)
        keys_live = lax.broadcasted_iota(jnp.int32, (patches, patches), 1) < count
        live.append((keys_live, lax.broadcasted_iota(jnp.int32, (patches, 1), 0) < count))
        d_spatial = cot_ref[f].astype(F32) + whole_ref[1, f].astype(F32)
        d_mixed.append(jnp.where(live[f][1], d_spatial, 0.0).astype(BF))
    each = [(f, slice(h * HD, (h + 1) * HD)) for f in range(frames) for h in range(width // HD)]
    queries, keys, values = ([qkv_ref[f, i, :, cols] for f, cols in each] for i in range(3))
    cotangents = [d_mixed[f][:, cols] for f, cols in each]
    probs = [softmax(queries[i], keys[i], live[f][0]) for i, (f, _) in enumerate(each)]
    grads = attention_grads(queries, keys, values, probs, cotangents)
    for i, (f, cols) in enumerate(each):
        mixed = dot(probs[i].astype(BF), values[i]).astype(BF).astype(F32)
        total = mixed + whole_ref[0, f, :, cols].astype(F32)
        out_ref[f, :, cols] = jnp.where(live[f][1], total, 0.0).astype(BF)
        for k in range(3):
            grad_ref[f, k, :, cols] = grads[i][k]


def own_chip():
    place = lax.axis_index("frame")
    return lax.axis_index("clip"), place // 2, place % 2


def assemble_kernel(ranks, *refs):
    blocks, refs = refs[: 2 * ranks], refs[2 * ranks :]
    feat_ref, gated_ref, own_ref, other_ref, flip_ref, sem = refs
    me, core = lax.axis_index("tensor"), own_chip()[2]
    width = feat_ref.shape[1] // ranks
    copies = []
    for a, whole in enumerate((feat_ref, gated_ref)):
        for d in range(ranks):
            start = pl.multiple_of(lax.rem(me + d, ranks) * width, HD)
            i = a * ranks + d
            copies.append(
                pltpu.make_async_copy(blocks[i], whole.at[:, pl.ds(start, width)], sem.at[i])
            )
    for copy in copies:
        copy.start()
    for copy in copies:
        copy.wait()
    pieces = 32
    rows = feat_ref.shape[1] // pieces
    for a, whole in enumerate((feat_ref, gated_ref)):
        for z in range(ranks):
            part = slice(z * width, (z + 1) * width)
            flip_ref[part, :] = whole[:, part].T
        for i in range(pieces // 2):
            to = slice(i * rows, (i + 1) * rows)
            own_ref[a, to] = flip_ref[pl.ds(pl.multiple_of((2 * i + core) * rows, 16), rows), :]
            other_ref[a, to] = flip_ref[pl.ds(pl.multiple_of((2 * i + 1 - core) * rows, 16), rows), :]


def row_keys(clip_ref, rows, axis):
    frames = clip_ref.shape[1]
    block = rows // frames
    index = lax.broadcasted_iota(jnp.int32, (rows, 1) if axis == 0 else (1, rows), axis)
    keys = index
    for f in range(frames):
        inside = (index >= f * block) & (index < (f + 1) * block)
        keys = jnp.where(inside, index + (clip_ref[0, f] - f) * block, keys)
    return keys


def temporal_kernel(heads, clip_ref, feat_hbm, gated_hbm, w_hbm, *refs):
    sums_hbm, both_ref, feat_ref, gated_ref, w_ref, sums_ref, in_sem, w_sem, out_sem = refs
    width = heads * HD
    slots = 4 * heads
    ranks, owners, _, rows, _ = sums_ref.shape
    loads = [
        pltpu.make_async_copy(w_hbm.at[i], w_ref.at[:, i * HD : (i + 1) * HD], w_sem.at[i])
        for i in range(slots)
    ]
    feat_load = pltpu.make_async_copy(feat_hbm, feat_ref, in_sem.at[0])
    gated_load = pltpu.make_async_copy(gated_hbm, gated_ref, in_sem.at[1])
    feat_load.start()
    for copy in loads[:6]:
        copy.start()
    mask = row_keys(clip_ref, owners * rows, 0) == row_keys(clip_ref, owners * rows, 1)
    feat_load.wait()
    query, keys, values = [], [], []
    for h in range(heads):
        for copy in loads[3 * h : 3 * h + 3]:
            copy.wait()
        if h == 0:
            gated_load.start()
        for copy in loads[3 * h + 6 : 3 * h + 9]:
            copy.start()
        qkv = dot(feat_ref[...], w_ref[:, h * width : (h + 1) * width]).astype(BF)
        for i, parts in enumerate((query, keys, values)):
            parts.append(qkv[:, i * HD : (i + 1) * HD])
    each = range(heads)
    probs = [softmax(query[h], keys[h], mask) for h in each]
    mixed = [dot(probs[h].astype(BF), values[h]).astype(BF) for h in each]
    gated_load.wait()
    for copy in loads[9:]:
        copy.wait()
    cotangent = dot(gated_ref[...], w_ref[:, 3 * width :]).astype(BF)
    cotangents = [cotangent[:, h * HD : (h + 1) * HD] for h in each]
    grads = attention_grads(query, keys, values, probs, cotangents)
    for h in each:
        for i in range(3):
            both_ref[:, (3 * h + i) * HD : (3 * h + i + 1) * HD] = grads[h][i]
        both_ref[:, 3 * width + h * HD : 3 * width + (h + 1) * HD] = mixed[h]
    stores = []
    pair = 4
    for first in range(0, ranks, pair):
        w_part = w_ref.at[first * width : (first + pair) * width]
        projected = dot(both_ref[:, 3 * width :], w_part[:, 3 * width :], NT).astype(BF)
        back = dot(both_ref[:, : 3 * width], w_part[:, : 3 * width], NT).astype(BF)
        for i in range(pair):
            z, cols = first + i, slice(i * width, (i + 1) * width)
            for s in range(owners):
                apart = lax.axis_index("frame") ^ s
                slot = lax.rem(apart, 2) * 4 + apart // 2
                sums_ref[z, slot, 0] = projected[s * rows : (s + 1) * rows, cols]
                sums_ref[z, slot, 1] = back[s * rows : (s + 1) * rows, cols]
            stores.append(pltpu.make_async_copy(sums_ref.at[z], sums_hbm.at[z], out_sem.at[z]))
            stores[-1].start()
    for copy in stores:
        copy.wait()


def weight_grad_kernel(step, own_ref, pair_ref, both_ref, pair_both_ref, out_ref):
    at_clip, at_x, core = own_chip()
    n, slots, rows, _ = out_ref.shape
    wide = both_ref.shape[1] * 3 // 4
    starts = []
    for r in range(n):
        clip = lax.rem(at_clip + jnp.where(core == 0, r, step), n)
        x = lax.rem(at_x + jnp.where(core == 0, step, r), n)
        starts.append(pl.multiple_of((clip * n + x) * rows, 16))
    for a, cols in ((0, slice(0, wide)), (1, slice(wide, 4 * wide // 3))):
        left = jnp.concatenate(
            [
                jnp.concatenate([ref[a, pl.ds(start, rows), :] for start in starts], axis=0)
                for ref in (own_ref, pair_ref)
            ],
            axis=1,
        )
        right = jnp.concatenate([both_ref[:, cols], pair_both_ref[:, cols]], axis=0)
        total = dot(left, right).astype(BF)
        for r in range(n):
            for s in range(total.shape[1] // HD):
                part = total[r * rows : (r + 1) * rows, s * HD : (s + 1) * HD]
                out_ref[r, a * (slots * 3 // 4) + s] = part


def shift(value, axis, step, size):
    return lax.ppermute(value, axis, [(i, (i + step) % size) for i in range(size)])


def pair_swap(value):
    return lax.ppermute(value, "frame", [(i, i ^ 1) for i in range(8)])


def spread(value, step, second):
    pairs = []
    for clip in range(4):
        for x in range(4):
            for core in range(2):
                to_clip, to_x = clip, x
                if (core == 0) != second:
                    to_x = (x + step) % 4
                else:
                    to_clip = (clip + step) % 4
                pairs.append((clip * 8 + x * 2 + core, to_clip * 8 + to_x * 2 + core))
    return lax.ppermute(value, ("clip", "frame"), pairs)


def ring_gather(value, axis, size, last_forward):
    found = {0: value}
    up = down = value
    for step in range(1, size // 2):
        up = shift(up, axis, 1, size)
        down = shift(down, axis, -1, size)
        found[size - step], found[step] = up, down
    found[size // 2] = shift(up, axis, 1, size) if last_forward else shift(down, axis, -1, size)
    return [found[d] for d in range(size)]


def add(*values):
    return sum(v.astype(F32) for v in values)


def body(spatial_qkv, w_qkv, w_out, out_grad, frame_clip, clip_patches):
    ranks = lax.axis_size("frame")
    width_ranks = lax.axis_size("tensor")
    total_frames = frame_clip.shape[1]
    _, frames, patches, _, width = spatial_qkv.shape
    heads = width // HD
    block = patches // ranks
    rows_t = total_frames * block
    model = width * width_ranks
    slots = 4 * heads

    w_rows = w_qkv.shape[0]
    w_own = jnp.concatenate(
        [w_qkv.transpose(1, 2, 0, 3).reshape(3 * heads, w_rows, HD), w_out.transpose(0, 2, 1)],
        axis=0,
    )
    w_all = lax.all_gather(w_own, ("clip", "frame"), axis=1, tiled=True)

    qkv = spatial_qkv[0].transpose(0, 2, 1, 3)
    cot = out_grad[0]
    smem = pl.BlockSpec(memory_space=pltpu.SMEM)
    vmem = pl.BlockSpec(memory_space=pltpu.VMEM)
    hbm = pl.BlockSpec(memory_space=pltpu.HBM)
    sent = pl.pallas_call(
        spatial_forward,
        out_shape=jax.ShapeDtypeStruct((ranks, 2, frames, block, width), BF),
        in_specs=[smem, smem, vmem, vmem],
        out_specs=vmem,
        scratch_shapes=[pltpu.VMEM((2, frames, patches, width), BF)],
        compiler_params=pltpu.CompilerParams(vmem_limit_bytes=58 * 2**20),
    )(frame_clip, clip_patches, qkv, cot)
    cols = lax.all_to_all(sent, "frame", split_axis=0, concat_axis=0, tiled=True)
    blocks = []
    for a in range(2):
        rows = cols[:, a].reshape(rows_t, width)
        blocks += ring_gather(rows, "tensor", width_ranks, a == 0)

    halves = jax.ShapeDtypeStruct((2, model // 2, rows_t), BF)
    wide = jax.ShapeDtypeStruct((rows_t, model), BF)
    feats, gated, own_flip, other_flip = pl.pallas_call(
        lambda *refs: assemble_kernel(width_ranks, *refs),
        out_shape=[wide, wide, halves, halves],
        in_specs=[hbm] * (2 * width_ranks),
        out_specs=[vmem] * 4,
        scratch_shapes=[
            pltpu.VMEM((model, rows_t), BF),
            pltpu.SemaphoreType.DMA((2 * width_ranks,)),
        ],
        compiler_params=pltpu.CompilerParams(vmem_limit_bytes=58 * 2**20),
    )(*blocks)
    pair_flip = pair_swap(other_flip)
    feats, pair_flip = lax.optimization_barrier([feats, pair_flip])

    wide_scratch = pltpu.VMEM((rows_t, model), BF)
    sums_shape = (width_ranks, ranks, 2, frames * block, width)
    sums, both = pl.pallas_call(
        lambda *refs: temporal_kernel(heads, *refs),
        out_shape=[
            jax.ShapeDtypeStruct(sums_shape, BF),
            jax.ShapeDtypeStruct((rows_t, 4 * width), BF),
        ],
        in_specs=[smem] + [hbm] * 3,
        out_specs=[hbm, vmem],
        scratch_shapes=[
            wide_scratch,
            wide_scratch,
            pltpu.VMEM((model, 4 * width), BF),
            pltpu.VMEM(sums_shape, BF),
            pltpu.SemaphoreType.DMA((2,)),
            pltpu.SemaphoreType.DMA((slots,)),
            pltpu.SemaphoreType.DMA((width_ranks,)),
        ],
        compiler_params=pltpu.CompilerParams(vmem_limit_bytes=56 * 2**20),
    )(frame_clip, feats, gated, w_all)

    own_sums = lax.psum_scatter(sums, "tensor", scatter_dimension=0, tiled=True)[0]
    pair_both = pair_swap(both)
    parts = {}
    for step in (2, 1, 3, 0):
        parts[step] = pl.pallas_call(
            lambda *refs, step=step: weight_grad_kernel(step, *refs),
            out_shape=jax.ShapeDtypeStruct((4, slots, w_rows, HD), BF),
            in_specs=[vmem] * 4,
            out_specs=vmem,
            compiler_params=pltpu.CompilerParams(vmem_limit_bytes=24 * 2**20),
        )(own_flip, pair_flip, both, pair_both)
    arrived = [parts[0]] + [spread(parts[step], step, False) for step in (2, 1, 3)]
    partial = [add(*(part[i] for part in arrived)).astype(BF) for i in range(4)]
    grads = add(partial[0], *(spread(partial[step], step, True) for step in (2, 1, 3)))

    own_part, got = own_sums[:4], pair_swap(own_sums[4:])
    joined = [jnp.concatenate([own_part[m : m + 1], got[m : m + 1]], axis=0) for m in range(4)]
    row_sums = joined[:1]
    for m in range(1, 4):
        pairs = [(i, i ^ (2 * m)) for i in range(8)]
        row_sums.append(lax.ppermute(joined[m], "frame", pairs))
    block_out, qkv_grad = pl.pallas_call(
        spatial_backward,
        out_shape=[
            jax.ShapeDtypeStruct((frames, patches, width), BF),
            jax.ShapeDtypeStruct((frames, 3, patches, width), BF),
        ],
        in_specs=[smem, smem] + [vmem] * 6,
        out_specs=[vmem, vmem],
        scratch_shapes=[pltpu.VMEM((2, frames, patches, width), BF)],
        compiler_params=pltpu.CompilerParams(vmem_limit_bytes=24 * 2**20),
    )(frame_clip, clip_patches, qkv, cot, *row_sums)

    w_qkv_grad = grads[: 3 * heads].reshape(heads, 3, w_rows, HD).transpose(2, 0, 1, 3)
    w_out_grad = grads[3 * heads :].transpose(0, 2, 1)
    return (block_out[None], qkv_grad.transpose(0, 2, 1, 3)[None], w_qkv_grad, w_out_grad)


def solution(mesh):
    in_specs = (
        P("clip", "frame", None, None, "tensor"),
        P(("clip", "frame"), "tensor", None, None),
        P("tensor", None, ("clip", "frame")),
        P("clip", "frame", None, "tensor"),
        P("clip", None),
        P("clip", None),
    )
    out_specs = (
        P("clip", "frame", None, "tensor"),
        P("clip", "frame", None, None, "tensor"),
        P(("clip", "frame"), "tensor", None, None),
        P("tensor", None, ("clip", "frame")),
    )
    return jax.shard_map(body, mesh=mesh, in_specs=in_specs, out_specs=out_specs, check_vma=False)
```

```python
import math

import jax
import jax.numpy as jnp
from jax import lax
from jax.experimental import pallas as pl
from jax.experimental.pallas import tpu as pltpu
from jax.sharding import PartitionSpec as P

HD = 128
SCALE = 1.0 / math.sqrt(HD)
BF = jnp.bfloat16
F32 = jnp.float32
NT = (((1,), (1,)), ((), ()))
TN = (((0,), (0,)), ((), ()))


def dot(a, b, dims=(((1,), (0,)), ((), ()))):
    return lax.dot_general(a, b, dims, preferred_element_type=F32)


def softmax(query, keys, mask):
    scores = jnp.where(mask, dot(query, keys, NT) * SCALE, -1e30)
    expo = jnp.exp(scores - jnp.max(scores, axis=-1, keepdims=True))
    return expo / jnp.sum(expo, axis=-1, keepdims=True)


def attention_grads(queries, keys, values, probs, cotangents):
    each = range(len(probs))
    d_values = [dot(probs[i].astype(BF), cotangents[i], TN).astype(BF) for i in each]
    d_probs = [dot(cotangents[i], values[i], NT).astype(BF).astype(F32) for i in each]
    inner = [jnp.sum(probs[i] * d_probs[i], axis=-1, keepdims=True) for i in each]
    d_scores = [(probs[i] * (d_probs[i] - inner[i]) * SCALE).astype(BF) for i in each]
    d_queries = [dot(d_scores[i], keys[i]).astype(BF) for i in each]
    d_keys = [dot(d_scores[i], queries[i], TN).astype(BF) for i in each]
    return list(zip(d_queries, d_keys, d_values))


def live_rows(row_ref, patch_ref, frame):
    return patch_ref[0, row_ref[0, frame]]


def spatial_forward(row_ref, patch_ref, qkv_ref, cot_ref, *refs):
    out_ref, whole_ref = refs
    frames, _, patches, width = qkv_ref.shape
    place = lax.axis_index("frame")
    owners = out_ref.shape[0]
    block = patches // owners
    for f in range(frames):
        count = live_rows(row_ref, patch_ref, place * frames + f)
        keys_live = lax.broadcasted_iota(jnp.int32, (patches, patches), 1) < count
        rows_live = lax.broadcasted_iota(jnp.int32, (patches, 1), 0) < count
        pieces = []
        for h in range(width // HD):
            cols = slice(h * HD, (h + 1) * HD)
            probs = softmax(qkv_ref[f, 0, :, cols], qkv_ref[f, 1, :, cols], keys_live)
            mixed = dot(probs.astype(BF), qkv_ref[f, 2, :, cols])
            pieces.append(jnp.where(rows_live, mixed, 0.0).astype(BF))
        whole_ref[0, f] = jnp.concatenate(pieces, axis=1)
        whole_ref[1, f] = jnp.where(rows_live, cot_ref[f].astype(F32), 0.0).astype(BF)
    for s in range(owners):
        out_ref[s] = whole_ref[:, :, s * block : (s + 1) * block, :]


def spatial_backward(row_ref, patch_ref, qkv_ref, cot_ref, *refs):
    sums_ref, out_ref, grad_ref, whole_ref = refs
    frames, _, patches, width = qkv_ref.shape
    place = lax.axis_index("frame")
    owners = sums_ref.shape[0]
    block = patches // owners
    for s in range(owners):
        for f in range(frames):
            part = sums_ref[s, :, f * block : (f + 1) * block, :]
            whole_ref[:, f, s * block : (s + 1) * block, :] = part
    live, d_mixed = [], []
    for f in range(frames):
        count = live_rows(row_ref, patch_ref, place * frames + f)
        keys_live = lax.broadcasted_iota(jnp.int32, (patches, patches), 1) < count
        live.append((keys_live, lax.broadcasted_iota(jnp.int32, (patches, 1), 0) < count))
        d_spatial = cot_ref[f].astype(F32) + whole_ref[1, f].astype(F32)
        d_mixed.append(jnp.where(live[f][1], d_spatial, 0.0).astype(BF))
    each = [(f, slice(h * HD, (h + 1) * HD)) for f in range(frames) for h in range(width // HD)]
    queries, keys, values = ([qkv_ref[f, i, :, cols] for f, cols in each] for i in range(3))
    cotangents = [d_mixed[f][:, cols] for f, cols in each]
    probs = [softmax(queries[i], keys[i], live[f][0]) for i, (f, _) in enumerate(each)]
    grads = attention_grads(queries, keys, values, probs, cotangents)
    for i, (f, cols) in enumerate(each):
        mixed = dot(probs[i].astype(BF), values[i]).astype(BF).astype(F32)
        total = mixed + whole_ref[0, f, :, cols].astype(F32)
        out_ref[f, :, cols] = jnp.where(live[f][1], total, 0.0).astype(BF)
        for k in range(3):
            grad_ref[f, k, :, cols] = grads[i][k]


def own_chip():
    place = lax.axis_index("frame")
    return lax.axis_index("clip"), place // 2, place % 2


def assemble_kernel(ranks, *refs):
    blocks, refs = refs[: 2 * ranks], refs[2 * ranks :]
    feat_ref, gated_ref, own_ref, other_ref, flip_ref, sem = refs
    me, core = lax.axis_index("tensor"), own_chip()[2]
    width = feat_ref.shape[1] // ranks
    copies = []
    for a, whole in enumerate((feat_ref, gated_ref)):
        for d in range(ranks):
            start = pl.multiple_of(lax.rem(me + d, ranks) * width, HD)
            i = a * ranks + d
            copies.append(
                pltpu.make_async_copy(blocks[i], whole.at[:, pl.ds(start, width)], sem.at[i])
            )
    for copy in copies:
        copy.start()
    for copy in copies:
        copy.wait()
    pieces = 32
    rows = feat_ref.shape[1] // pieces
    for a, whole in enumerate((feat_ref, gated_ref)):
        for z in range(ranks):
            part = slice(z * width, (z + 1) * width)
            flip_ref[part, :] = whole[:, part].T
        for i in range(pieces // 2):
            to = slice(i * rows, (i + 1) * rows)
            own_ref[a, to] = flip_ref[pl.ds(pl.multiple_of((2 * i + core) * rows, 16), rows), :]
            other_ref[a, to] = flip_ref[pl.ds(pl.multiple_of((2 * i + 1 - core) * rows, 16), rows), :]


def row_keys(clip_ref, rows, axis):
    frames = clip_ref.shape[1]
    block = rows // frames
    index = lax.broadcasted_iota(jnp.int32, (rows, 1) if axis == 0 else (1, rows), axis)
    keys = index
    for f in range(frames):
        inside = (index >= f * block) & (index < (f + 1) * block)
        keys = jnp.where(inside, index + (clip_ref[0, f] - f) * block, keys)
    return keys


def temporal_kernel(heads, clip_ref, feat_hbm, gated_hbm, w_hbm, *refs):
    sums_hbm, both_ref, feat_ref, gated_ref, w_ref, sums_ref, in_sem, w_sem, out_sem = refs
    width = heads * HD
    slots = 4 * heads
    ranks, owners, _, rows, _ = sums_ref.shape
    loads = [
        pltpu.make_async_copy(w_hbm.at[i], w_ref.at[:, i * HD : (i + 1) * HD], w_sem.at[i])
        for i in range(slots)
    ]
    feat_load = pltpu.make_async_copy(feat_hbm, feat_ref, in_sem.at[0])
    gated_load = pltpu.make_async_copy(gated_hbm, gated_ref, in_sem.at[1])
    feat_load.start()
    for copy in loads[:6]:
        copy.start()
    mask = row_keys(clip_ref, owners * rows, 0) == row_keys(clip_ref, owners * rows, 1)
    feat_load.wait()
    query, keys, values = [], [], []
    for h in range(heads):
        for copy in loads[3 * h : 3 * h + 3]:
            copy.wait()
        if h == 0:
            gated_load.start()
        for copy in loads[3 * h + 6 : 3 * h + 9]:
            copy.start()
        qkv = dot(feat_ref[...], w_ref[:, h * width : (h + 1) * width]).astype(BF)
        for i, parts in enumerate((query, keys, values)):
            parts.append(qkv[:, i * HD : (i + 1) * HD])
    each = range(heads)
    probs = [softmax(query[h], keys[h], mask) for h in each]
    mixed = [dot(probs[h].astype(BF), values[h]).astype(BF) for h in each]
    gated_load.wait()
    for copy in loads[9:]:
        copy.wait()
    cotangent = dot(gated_ref[...], w_ref[:, 3 * width :]).astype(BF)
    cotangents = [cotangent[:, h * HD : (h + 1) * HD] for h in each]
    grads = attention_grads(query, keys, values, probs, cotangents)
    for h in each:
        for i in range(3):
            both_ref[:, (3 * h + i) * HD : (3 * h + i + 1) * HD] = grads[h][i]
        both_ref[:, 3 * width + h * HD : 3 * width + (h + 1) * HD] = mixed[h]
    stores = []
    pair = 8
    for first in range(0, ranks, pair):
        w_part = w_ref.at[first * width : (first + pair) * width]
        projected = dot(both_ref[:, 3 * width :], w_part[:, 3 * width :], NT).astype(BF)
        back = dot(both_ref[:, : 3 * width], w_part[:, : 3 * width], NT).astype(BF)
        for i in range(pair):
            z, cols = first + i, slice(i * width, (i + 1) * width)
            for s in range(owners):
                sums_ref[z, s, 0] = projected[s * rows : (s + 1) * rows, cols]
                sums_ref[z, s, 1] = back[s * rows : (s + 1) * rows, cols]
            stores.append(pltpu.make_async_copy(sums_ref.at[z], sums_hbm.at[z], out_sem.at[z]))
            stores[-1].start()
    for copy in stores:
        copy.wait()


def weight_grad_kernel(step, own_ref, pair_ref, both_ref, pair_both_ref, out_ref):
    at_clip, at_x, core = own_chip()
    n, slots, rows, _ = out_ref.shape
    wide = both_ref.shape[1] * 3 // 4
    starts = []
    for r in range(n):
        clip = lax.rem(at_clip + jnp.where(core == 0, r, step), n)
        x = lax.rem(at_x + jnp.where(core == 0, step, r), n)
        starts.append(pl.multiple_of((clip * n + x) * rows, 16))
    for a, cols in ((0, slice(0, wide)), (1, slice(wide, 4 * wide // 3))):
        left = jnp.concatenate(
            [
                jnp.concatenate([ref[a, pl.ds(start, rows), :] for start in starts], axis=0)
                for ref in (own_ref, pair_ref)
            ],
            axis=1,
        )
        right = jnp.concatenate([both_ref[:, cols], pair_both_ref[:, cols]], axis=0)
        total = dot(left, right).astype(BF)
        for r in range(n):
            for s in range(total.shape[1] // HD):
                part = total[r * rows : (r + 1) * rows, s * HD : (s + 1) * HD]
                out_ref[r, a * (slots * 3 // 4) + s] = part


def shift(value, axis, step, size):
    return lax.ppermute(value, axis, [(i, (i + step) % size) for i in range(size)])


def pair_swap(value):
    return lax.ppermute(value, "frame", [(i, i ^ 1) for i in range(8)])


def spread(value, step, second):
    pairs = []
    for clip in range(4):
        for x in range(4):
            for core in range(2):
                to_clip, to_x = clip, x
                if (core == 0) != second:
                    to_x = (x + step) % 4
                else:
                    to_clip = (clip + step) % 4
                pairs.append((clip * 8 + x * 2 + core, to_clip * 8 + to_x * 2 + core))
    return lax.ppermute(value, ("clip", "frame"), pairs)


def ring_gather(value, axis, size, last_forward):
    found = {0: value}
    up = down = value
    for step in range(1, size // 2):
        up = shift(up, axis, 1, size)
        down = shift(down, axis, -1, size)
        found[size - step], found[step] = up, down
    found[size // 2] = shift(up, axis, 1, size) if last_forward else shift(down, axis, -1, size)
    return [found[d] for d in range(size)]


def add(*values):
    return sum(v.astype(F32) for v in values)


def body(spatial_qkv, w_qkv, w_out, out_grad, frame_clip, clip_patches):
    ranks = lax.axis_size("frame")
    width_ranks = lax.axis_size("tensor")
    total_frames = frame_clip.shape[1]
    _, frames, patches, _, width = spatial_qkv.shape
    heads = width // HD
    block = patches // ranks
    rows_t = total_frames * block
    model = width * width_ranks
    slots = 4 * heads

    w_rows = w_qkv.shape[0]
    w_own = jnp.concatenate(
        [w_qkv.transpose(1, 2, 0, 3).reshape(3 * heads, w_rows, HD), w_out.transpose(0, 2, 1)],
        axis=0,
    )
    w_all = lax.all_gather(w_own, ("clip", "frame"), axis=1, tiled=True)

    qkv = spatial_qkv[0].transpose(0, 2, 1, 3)
    cot = out_grad[0]
    smem = pl.BlockSpec(memory_space=pltpu.SMEM)
    vmem = pl.BlockSpec(memory_space=pltpu.VMEM)
    hbm = pl.BlockSpec(memory_space=pltpu.HBM)
    sent = pl.pallas_call(
        spatial_forward,
        out_shape=jax.ShapeDtypeStruct((ranks, 2, frames, block, width), BF),
        in_specs=[smem, smem, vmem, vmem],
        out_specs=vmem,
        scratch_shapes=[pltpu.VMEM((2, frames, patches, width), BF)],
        compiler_params=pltpu.CompilerParams(vmem_limit_bytes=58 * 2**20),
    )(frame_clip, clip_patches, qkv, cot)
    cols = lax.all_to_all(sent, "frame", split_axis=0, concat_axis=0, tiled=True)
    blocks = []
    for a in range(2):
        rows = cols[:, a].reshape(rows_t, width)
        blocks += ring_gather(rows, "tensor", width_ranks, a == 0)

    halves = jax.ShapeDtypeStruct((2, model // 2, rows_t), BF)
    wide = jax.ShapeDtypeStruct((rows_t, model), BF)
    feats, gated, own_flip, other_flip = pl.pallas_call(
        lambda *refs: assemble_kernel(width_ranks, *refs),
        out_shape=[wide, wide, halves, halves],
        in_specs=[hbm] * (2 * width_ranks),
        out_specs=[vmem] * 4,
        scratch_shapes=[
            pltpu.VMEM((model, rows_t), BF),
            pltpu.SemaphoreType.DMA((2 * width_ranks,)),
        ],
        compiler_params=pltpu.CompilerParams(vmem_limit_bytes=58 * 2**20),
    )(*blocks)
    pair_flip = pair_swap(other_flip)
    feats, pair_flip = lax.optimization_barrier([feats, pair_flip])

    wide_scratch = pltpu.VMEM((rows_t, model), BF)
    sums_shape = (width_ranks, ranks, 2, frames * block, width)
    sums, both = pl.pallas_call(
        lambda *refs: temporal_kernel(heads, *refs),
        out_shape=[
            jax.ShapeDtypeStruct(sums_shape, BF),
            jax.ShapeDtypeStruct((rows_t, 4 * width), BF),
        ],
        in_specs=[smem] + [hbm] * 3,
        out_specs=[hbm, vmem],
        scratch_shapes=[
            wide_scratch,
            wide_scratch,
            pltpu.VMEM((model, 4 * width), BF),
            pltpu.VMEM(sums_shape, BF),
            pltpu.SemaphoreType.DMA((2,)),
            pltpu.SemaphoreType.DMA((slots,)),
            pltpu.SemaphoreType.DMA((width_ranks,)),
        ],
        compiler_params=pltpu.CompilerParams(vmem_limit_bytes=56 * 2**20),
    )(frame_clip, feats, gated, w_all)

    own_sums = lax.psum_scatter(sums, "tensor", scatter_dimension=0, tiled=True)[0]
    pair_both = pair_swap(both)
    parts = {}
    for step in (2, 1, 3, 0):
        parts[step] = pl.pallas_call(
            lambda *refs, step=step: weight_grad_kernel(step, *refs),
            out_shape=jax.ShapeDtypeStruct((4, slots, w_rows, HD), BF),
            in_specs=[vmem] * 4,
            out_specs=vmem,
            compiler_params=pltpu.CompilerParams(vmem_limit_bytes=24 * 2**20),
        )(own_flip, pair_flip, both, pair_both)
    arrived = [parts[0]] + [spread(parts[step], step, False) for step in (2, 1, 3)]
    partial = [add(*(part[i] for part in arrived)).astype(BF) for i in range(4)]
    grads = add(partial[0], *(spread(partial[step], step, True) for step in (2, 1, 3)))

    row_sums = lax.all_to_all(own_sums, "frame", split_axis=0, concat_axis=0, tiled=True)
    block_out, qkv_grad = pl.pallas_call(
        spatial_backward,
        out_shape=[
            jax.ShapeDtypeStruct((frames, patches, width), BF),
            jax.ShapeDtypeStruct((frames, 3, patches, width), BF),
        ],
        in_specs=[smem, smem] + [vmem] * 3,
        out_specs=[vmem, vmem],
        scratch_shapes=[pltpu.VMEM((2, frames, patches, width), BF)],
        compiler_params=pltpu.CompilerParams(vmem_limit_bytes=24 * 2**20),
    )(frame_clip, clip_patches, qkv, cot, row_sums)

    w_qkv_grad = grads[: 3 * heads].reshape(heads, 3, w_rows, HD).transpose(2, 0, 1, 3)
    w_out_grad = grads[3 * heads :].transpose(0, 2, 1)
    return (block_out[None], qkv_grad.transpose(0, 2, 1, 3)[None], w_qkv_grad, w_out_grad)


def solution(mesh):
    in_specs = (
        P("clip", "frame", None, None, "tensor"),
        P(("clip", "frame"), "tensor", None, None),
        P("tensor", None, ("clip", "frame")),
        P("clip", "frame", None, "tensor"),
        P("clip", None),
        P("clip", None),
    )
    out_specs = (
        P("clip", "frame", None, "tensor"),
        P("clip", "frame", None, None, "tensor"),
        P(("clip", "frame"), "tensor", None, None),
        P("tensor", None, ("clip", "frame")),
    )
    return jax.shard_map(body, mesh=mesh, in_specs=in_specs, out_specs=out_specs, check_vma=False)
```
